256 devices in a mesh: dp: 64 (over y, z_hi, x, core), head: 4 (over z_lo).
Axes of the slice: x: 4, y: 4, z: 8 (z_hi: 2, z_lo: 4; z = z_hi * 4 + z_lo), core: 2. Of those that a mesh axis runs over, the one named last changes fastest.
Arguments:
- decode_query: bfloat16 [1024, 4096], P('dp', 'head'), may hold values from -320 to 320
- new_kv: bfloat16 [1024, 2, 512], P('dp', None, 'head'), may hold values from -6 to 6
- sample_order: int32 [1024], P('dp'), may hold values from 0 to 1023, each once
- suffix_len: int32 [1024], P('dp'), may hold values from 1 to 128, 65536 in all
- suffix_kv: bfloat16 [1024, 2, 128, 512], P('dp', None, None, 'head'), may hold values from -6 to 6
- prefix_kv: bfloat16 [64, 2, 384, 512], P('dp', None, None, 'head'), may hold values from -6 to 6
- prefix_len: int32 [64], P('dp'), may hold values from 1 to 384, 12288 in all
- prefill_query: bfloat16 [16384, 4096], P('dp', 'head'), may hold values from -320 to 320
- prefill_kv: bfloat16 [16384, 2, 512], P('dp', None, 'head'), may hold values from -6 to 6
- prefill_segment: int32 [64, 256], P('dp'), may hold values from 0 to 2, never falling along the last dimension, each value on 1 to 128 neighbouring positions
- out_weight: bfloat16 [4096, 5120], P('head'), may hold values from -0.09375 to 0.09375
Outputs:
- decode_out: bfloat16 [1024, 5120], P('dp', 'head')
- prefill_out: bfloat16 [16384, 5120], P('dp', 'head')
The draws below stay inside these ranges and needn't reach their ends.
Inputs may be any that keep to these rules, and one draw needn't show every extreme that they name: `sample_order`: each prompt is continued by exactly 16 rows; every number appears once. `suffix_len`: some row reaches 128. `prefix_len`: some prompt reaches 384. `prefill_segment`: never falls along a block.
All inputs are finite; a program needn't handle non-finite values. No bound on the sum of `suffix_len` or of `prefix_len` on one device may be relied on, other than what follows from the above.
Results may differ from the reference program's by a relative error of at most 0.017.
Values may be sent and summed in bfloat16 or wider, within the bound.
A program may use at most 128 MiB of HBM per device.

```python
import math
import jax
import jax.numpy as jnp
import numpy as np
from jax import lax

D = 5120
HEAD_DIM = 128
SAMPLES = 16
PREFIX = 384
SUFFIX = 128
STRETCH = 256
GROUP = 8
QW = 4096
KVW = 512
PROMPTS = 64
ROWS = 1024
BLOCKS = 64
STRETCH_TOKENS = 16384


def draw_decode_query(key, part):
    key = jax.random.fold_in(key, 11)
    values = jnp.clip(jax.random.normal(key, (ROWS, QW), jnp.float32), -4.0, 4.0)
    return values.astype(jnp.bfloat16)


def draw_prefill_query(key, part):
    key = jax.random.fold_in(key, 23)
    values = jnp.clip(jax.random.normal(key, (STRETCH_TOKENS, QW), jnp.float32), -4.0, 4.0)
    return values.astype(jnp.bfloat16)


def levels(rng, extent, split, smallest, top_value):
    def one(dim, blocks):
        heights = jax.random.uniform(jax.random.fold_in(jax.random.fold_in(rng, 6), dim), (blocks,), jnp.float32, smallest / len(split), top_value / len(split))
        return jnp.repeat(jnp.exp(heights), extent[dim] // blocks).reshape((-1,) + (1,) * (len(extent) - dim - 1))

    loudness = one(*split[0])
    for cut in split[1:]:
        loudness = loudness * one(*cut)
    return loudness


def split_up(amount, total, most, skew):
    weights = [(1 << 20) // math.isqrt(standing ** skew) + 1 for standing in range(2, amount + 1)]
    rest, counts = total - most - (amount - 1), [1] * (amount - 1)
    while rest > 0:
        free = [i for i in range(amount - 1) if counts[i] < most]
        pool, left = sum([weights[i] for i in free]), rest
        for i in free:
            extra = min(most - counts[i], max(1, left * weights[i] // pool), rest)
            counts[i] = counts[i] + extra
            rest = rest - extra
    return np.array([most] + counts)


def uneven_parts(stream_key, count, total, bound, slope):
    if count == 2:
        one = jax.random.randint(stream_key, (), max(1, total - bound), min(bound, total - 1) + 1)
        return jnp.stack([one, total - one])
    lengths = jnp.asarray(split_up(count, total, bound, slope), jnp.int32)
    twos = (count - 1) // 2
    giver, receiver = lengths[1:1 + 2 * twos:2], lengths[2:2 + 2 * twos:2]
    margin = jnp.minimum(giver - 1, bound - receiver)
    passed = jax.random.randint(jax.random.fold_in(stream_key, 1), (twos,), 0, 1 << 20) % (margin + 1)
    lengths = lengths.at[1:1 + 2 * twos:2].set(giver - passed).at[2:2 + 2 * twos:2].set(receiver + passed)
    return lengths[jax.random.permutation(jax.random.fold_in(stream_key, 2), count)]


def bell_draw(own_key, shape, scale, bound, split=(), held_as=jnp.bfloat16):
    entries = scale * jax.random.normal(own_key, shape, jnp.float32)
    if split:
        entries = entries * levels(own_key, shape, split, -0.22, 0.18)
    return jnp.clip(entries, -bound, bound).astype(held_as)


def setup_inputs(seed: int = 0) -> dict:
    key_of = jax.random.split(jax.random.key(seed), 12)
    return {
        "decode_query": draw_decode_query(jax.random.fold_in(key_of[11], 71), 0),
        "new_kv": bell_draw(key_of[1], (ROWS, 2, KVW), 1.0, 6.0, ((0, 64), (2, 4))),
        "sample_order": jax.random.permutation(key_of[2], ROWS).astype(jnp.int32),
        "suffix_len": uneven_parts(key_of[3], ROWS, ROWS * SUFFIX // 2, SUFFIX, 2).astype(jnp.int32),
        "suffix_kv": bell_draw(key_of[4], (ROWS, 2, SUFFIX, KVW), 1.0, 6.0, ((0, 64), (3, 4))),
        "prefix_kv": bell_draw(key_of[5], (PROMPTS, 2, PREFIX, KVW), 1.0, 6.0, ((0, 64), (3, 4))),
        "prefix_len": uneven_parts(key_of[6], PROMPTS, PROMPTS * PREFIX // 2, PREFIX, 2).astype(jnp.int32),
        "prefill_query": draw_prefill_query(jax.random.fold_in(key_of[11], 71), 0),
        "prefill_kv": bell_draw(key_of[8], (STRETCH_TOKENS, 2, KVW), 1.0, 6.0, ((0, 64), (2, 4))),
        "prefill_segment": jax.vmap(lambda own: jnp.searchsorted(jnp.cumsum(uneven_parts(own, 3, STRETCH, STRETCH // 2, 0)), jnp.arange(STRETCH), side="right"))(jax.random.split(key_of[9], BLOCKS)).reshape((BLOCKS, STRETCH)).astype(jnp.int32),
        "out_weight": bell_draw(key_of[10], (QW, D), QW ** -0.5, 0.09375, ((0, 4),)),
    }


FLOOR_SCORE = -1e+30

def decode_rows(query_rows, fresh_pairs, group_rows, suffix_lengths, suffix_pairs, prefix_kv, prefix_len):
    row_count = query_rows.shape[0]
    kv_heads = fresh_pairs.shape[2] // HEAD_DIM
    page_rows = prefix_kv[group_rows]
    page_lengths = prefix_len[group_rows]
    key_rows = jnp.concatenate([page_rows[:, 0], suffix_pairs[:, 0], fresh_pairs[:, 0][:, None, :]], axis=1)
    value_rows = jnp.concatenate([page_rows[:, 1], suffix_pairs[:, 1], fresh_pairs[:, 1][:, None, :]], axis=1)
    span = key_rows.shape[1]
    key_rows = key_rows.reshape(row_count, span, kv_heads, HEAD_DIM).astype(jnp.float32)
    value_rows = value_rows.reshape(row_count, span, kv_heads, HEAD_DIM).astype(jnp.float32)
    query_heads = query_rows.reshape(row_count, kv_heads, GROUP, HEAD_DIM).astype(jnp.float32)
    live_mask = jnp.concatenate([jnp.arange(PREFIX)[None, :] < page_lengths[:, None], jnp.arange(SUFFIX)[None, :] < suffix_lengths[:, None], jnp.ones((row_count, 1), bool)], axis=1)[:, None, None, :]
    scores = jnp.einsum('rkgd,rskd->rkgs', query_heads, key_rows) * (1.0 / math.sqrt(HEAD_DIM))
    best_score = lax.optimization_barrier(jnp.max(jnp.where(live_mask, scores, FLOOR_SCORE), axis=-1))
    weights = jnp.where(live_mask, jnp.exp(scores - best_score[..., None]), 0.0)
    weight_sum = lax.optimization_barrier(jnp.sum(weights, axis=-1))
    rounded = lax.optimization_barrier(weights.astype(jnp.bfloat16)).astype(jnp.float32)
    mixed_sum = jnp.einsum('rkgs,rskd->rkgd', rounded, value_rows)
    return (mixed_sum / weight_sum[..., None]).reshape(row_count, -1).astype(jnp.bfloat16)

def prefill_rows(query_rows, pair_rows, segment_row):
    token_count = query_rows.shape[0]
    kv_heads = pair_rows.shape[2] // HEAD_DIM
    query_heads = query_rows.reshape(token_count, kv_heads, GROUP, HEAD_DIM).astype(jnp.float32)
    key_rows = pair_rows[:, 0].reshape(token_count, kv_heads, HEAD_DIM).astype(jnp.float32)
    value_rows = pair_rows[:, 1].reshape(token_count, kv_heads, HEAD_DIM).astype(jnp.float32)
    positions = jnp.arange(token_count)
    live_mask = (positions[None, :] <= positions[:, None]) & (segment_row[None, :] == segment_row[:, None])
    scores = jnp.einsum('qkgd,tkd->kgqt', query_heads, key_rows) * (1.0 / math.sqrt(HEAD_DIM))
    best_score = lax.optimization_barrier(jnp.max(jnp.where(live_mask, scores, FLOOR_SCORE), axis=-1))
    weights = jnp.where(live_mask, jnp.exp(scores - best_score[..., None]), 0.0)
    weight_sum = lax.optimization_barrier(jnp.sum(weights, axis=-1))
    rounded = lax.optimization_barrier(weights.astype(jnp.bfloat16)).astype(jnp.float32)
    mixed_sum = jnp.einsum('kgqt,tkd->qkgd', rounded, value_rows)
    normal = mixed_sum / jnp.transpose(weight_sum, (2, 0, 1))[..., None]
    return normal.reshape(token_count, -1).astype(jnp.bfloat16)

def reference(decode_query, new_kv, sample_order, suffix_len, suffix_kv, prefix_kv, prefix_len, prefill_query, prefill_kv, prefill_segment, out_weight):
    group_ids = (sample_order // SAMPLES).astype(jnp.int32)
    block_count = ROWS // SAMPLES

    def one_block(inputs):
        query_rows, fresh_pairs, group_rows, suffix_lengths, suffix_pairs = inputs
        return decode_rows(query_rows, fresh_pairs, group_rows, suffix_lengths, suffix_pairs, prefix_kv, prefix_len)
    decode_attn = lax.map(one_block, (decode_query.reshape(block_count, SAMPLES, QW), new_kv.reshape(block_count, SAMPLES, 2, KVW), group_ids.reshape(block_count, SAMPLES), suffix_len.reshape(block_count, SAMPLES), suffix_kv.reshape(block_count, SAMPLES, 2, SUFFIX, KVW))).reshape(ROWS, QW)

    def one_stretch(inputs):
        query_rows, pair_rows, segment_row = inputs
        return prefill_rows(query_rows, pair_rows, segment_row)
    prefill_attn = lax.map(one_stretch, (prefill_query.reshape(BLOCKS, STRETCH, QW), prefill_kv.reshape(BLOCKS, STRETCH, 2, KVW), prefill_segment)).reshape(STRETCH_TOKENS, QW)
    decode_out = jnp.dot(decode_attn, out_weight, preferred_element_type=jnp.float32).astype(jnp.bfloat16)
    prefill_out = jnp.dot(prefill_attn, out_weight, preferred_element_type=jnp.float32).astype(jnp.bfloat16)
    return (decode_out, prefill_out)
```

```python
import math

import jax
import jax.numpy as jnp
from jax import lax
from jax.experimental import pallas as pl
from jax.experimental.pallas import tpu as pltpu
from jax.sharding import PartitionSpec as P

MESH = pl.DeviceIdType.MESH
HD = 128
SAMPLES = 16
GROUP = 8
FLOOR = -1e30
SCALE = 1.0 / math.sqrt(HD)
PX = 384
MSG = 1024 + 128
KVROWS = 2 * PX + 16
CH = 256
NCH = 5
SHARD = CH * NCH
F32 = jnp.float32
BF16 = jnp.bfloat16


def dot(a, b):
    return jnp.dot(a, b, preferred_element_type=F32)


def dot_t(a, b):
    return lax.dot_general(a, b, (((1,), (1,)), ((), ())), preferred_element_type=F32)


def stack_heads(rows):
    return jnp.concatenate([rows[:, HD * h : HD * (h + 1)] for h in range(GROUP)], axis=0)


def unstack_heads(rows):
    return jnp.concatenate([rows[SAMPLES * h : SAMPLES * (h + 1)] for h in range(GROUP)], axis=1)


def kernel(
    so_ref, sl_ref, pfl_ref, dq_ref, nkv_ref, pkv_ref, seg_ref, pq_hbm, skv_hbm, pre_hbm, w_hbm,
    dout_ref, pout_ref,
    wv, pq, skv, pall, qall, rsend, rrecv, zsend, zrecv,
    attn, dattn, tmp, dtmp, bias, qsel, osel, suf_o, suf_m, suf_l,
    sR, sL, rL, rR, dsR, dsL, drL, drR,
    lsem, xs, xr, ys, yr, y2s, y2r, ms, mr,
    sRs, sLs, rLs, rRs, dsRs, dsLs, drLs, drRs,
):
    d = lax.axis_index("dp")
    k = lax.axis_index("head")
    c = lax.rem(d, 2)
    x = lax.rem(d // 2, 4)
    zh = lax.rem(d // 8, 2)
    y = d // 16
    a = d // 8

    def dev(y_, zh_, x_, c_):
        return (((y_ * 2 + zh_) * 4 + x_) * 2 + c_, k)

    sibling = dev(y, zh, x, 1 - c)
    partner = dev(y, 1 - zh, x, c)
    xpeer = [dev(y, zh, lax.rem(x + i, 4), c) for i in (1, 2, 3)]
    ypeer = [dev(lax.rem(y + i, 4), zh, x, c) for i in (1, 2, 3)]
    right = (d, jnp.minimum(k + 1, 3))
    left = (d, jnp.maximum(k - 1, 0))

    bar = pltpu.get_barrier_semaphore()
    for peer in [sibling, partner] + xpeer + ypeer:
        pl.semaphore_signal(bar, inc=1, device_id=peer, device_id_type=MESH)

    @pl.when(k < 3)
    def _():
        pl.semaphore_signal(bar, inc=1, device_id=right, device_id_type=MESH)

    @pl.when(k > 0)
    def _():
        pl.semaphore_signal(bar, inc=1, device_id=left, device_id_type=MESH)

    loads = [
        pltpu.make_async_copy(pq_hbm, pq, lsem.at[0]),
        pltpu.make_async_copy(pre_hbm.at[0, 0], pall.at[c, x, pl.ds(0, PX)], lsem.at[1]),
        pltpu.make_async_copy(pre_hbm.at[0, 1], pall.at[c, x, pl.ds(PX, PX)], lsem.at[2]),
        pltpu.make_async_copy(w_hbm, wv, lsem.at[3]),
        pltpu.make_async_copy(skv_hbm, skv, lsem.at[4]),
    ]
    for load in loads:
        load.start()

    lane = lax.broadcasted_iota(jnp.int32, (SAMPLES, 128), 1)
    row = lax.broadcasted_iota(jnp.int32, (SAMPLES, 128), 0)
    extra = jnp.zeros((SAMPLES, 128), jnp.int32)
    for r in range(SAMPLES):
        number = so_ref[r]
        part = jnp.where(lane == 0, number >> 4, jnp.where(lane == 1, number & 15, 0))
        extra = jnp.where(row == r, part, extra)
    qall[y, zh, :, 0:1024] = dq_ref[...]
    qall[y, zh, :, 1024:MSG] = extra.astype(F32).astype(BF16)
    length = pfl_ref[0]
    pall[c, x, 2 * PX : KVROWS, :] = (
        jnp.where(row == 0, length >> 4, jnp.where(row == 1, length & 15, 0)).astype(F32).astype(BF16)
    )

    pl.semaphore_wait(bar, 8 + jnp.where(k < 3, 1, 0) + jnp.where(k > 0, 1, 0))

    def remote(src, dst, ss, rs, target):
        return pltpu.make_async_remote_copy(
            src_ref=src, dst_ref=dst, send_sem=ss, recv_sem=rs, device_id=target, device_id_type=MESH
        )

    z1 = remote(qall.at[y, zh], qall.at[y, zh], ms.at[0], mr.at[0], partner)
    z1.start()
    loads[1].wait()
    loads[2].wait()
    px = [
        remote(pall.at[c, x], pall.at[c, x], xs.at[i], xr.at[i], xpeer[i]) for i in range(3)
    ]
    for copy in px:
        copy.start()

    qpos = lax.broadcasted_iota(jnp.int32, (256, 256), 0)
    kpos = lax.broadcasted_iota(jnp.int32, (256, 256), 1)
    seg_row = jnp.broadcast_to(seg_ref[...].astype(F32), (256, 256))
    seg_col = jnp.sum(jnp.where(qpos == kpos, seg_row, 0.0), axis=1, keepdims=True)
    bias[...] = jnp.where((kpos <= qpos) & (seg_row == seg_col), 0.0, FLOOR)
    keys = pkv_ref[:, 0, :]
    values = pkv_ref[:, 1, :]
    loads[0].wait()

    def one_head(h, _):
        cols = pl.ds(pl.multiple_of(h * HD, HD), HD)
        s = dot_t(pq[:, cols], keys) * SCALE + bias[...]
        top = jnp.max(s, axis=1, keepdims=True)
        w = jnp.exp(s - top)
        total = jnp.sum(w, axis=1, keepdims=True)
        attn[:, cols] = (dot(w.astype(BF16), values) / total).astype(BF16)
        return 0

    lax.fori_loop(0, GROUP, one_head, 0)
    loads[3].wait()

    def right_copy(p, j):
        return remote(sR.at[p, j], rL.at[p, j], sRs.at[p, j], rLs.at[p, j], right)

    def left_copy(p, j):
        return remote(sL.at[p, j], rR.at[p, j], sLs.at[p, j], rRs.at[p, j], left)

    def cols_of(dest, j):
        return pl.ds(pl.multiple_of(dest * SHARD + j * CH, CH), CH)

    def right_item(p, j):
        @pl.when(p < 3 - k)
        def _():
            tmp[...] = dot(attn[...], wv[:, cols_of(3 - p, j)])

            @pl.when(k > 0)
            def _():
                right_copy(p, j).wait_recv()
                tmp[...] += rL[p, j].astype(F32)

            sR[p, j] = tmp[...].astype(BF16)
            right_copy(p, j).start()

    def left_item(p, j):
        @pl.when(p < k)
        def _():
            tmp[...] = dot(attn[...], wv[:, cols_of(p, j)])

            @pl.when(k < 3)
            def _():
                left_copy(p, j).wait_recv()
                tmp[...] += rR[p, j].astype(F32)

            sL[p, j] = tmp[...].astype(BF16)
            left_copy(p, j).start()

    def send_wait(p, j):
        @pl.when(p < 3 - k)
        def _():
            right_copy(p, j).wait_send()

        @pl.when(p < k)
        def _():
            left_copy(p, j).wait_send()

    def final_item(j):
        tmp[...] = dot(attn[...], wv[:, cols_of(k, j)])

        @pl.when(k > 0)
        def _():
            right_copy(3 - k, j).wait_recv()
            tmp[...] += rL[3 - k, j].astype(F32)

        @pl.when(k < 3)
        def _():
            left_copy(k, j).wait_recv()
            tmp[...] += rR[k, j].astype(F32)

        pout_ref[:, pl.ds(pl.multiple_of(j * CH, CH), CH)] = tmp[...].astype(BF16)

    def items(lo, hi):
        def body(n, _):
            p, j = n // NCH, lax.rem(n, NCH)

            @pl.when(n >= 2)
            def _():
                send_wait((n - 2) // NCH, lax.rem(n - 2, NCH))

            right_item(p, j)
            left_item(p, j)
            return 0

        lax.fori_loop(lo, hi, body, 0)

    def dright_copy(p):
        return remote(dsR.at[p], drL.at[p], dsRs.at[p], drLs.at[p], right)

    def dleft_copy(p):
        return remote(dsL.at[p], drR.at[p], dsLs.at[p], drRs.at[p], left)

    def ddot(dest):
        def tile(j, _):
            out = pl.ds(pl.multiple_of(j * CH, CH), CH)
            dtmp[:, out] = dot(dattn[...], wv[:, cols_of(dest, j)])
            return 0

        lax.fori_loop(0, NCH, tile, 0)

    def decode_items(p):
        @pl.when(p < 3 - k)
        def _():
            ddot(3 - p)

            @pl.when(k > 0)
            def _():
                dright_copy(p).wait_recv()
                dtmp[...] += drL[p].astype(F32)

            dsR[p] = dtmp[...].astype(BF16)
            dright_copy(p).start()

        @pl.when(p < k)
        def _():
            ddot(p)

            @pl.when(k < 3)
            def _():
                dleft_copy(p).wait_recv()
                dtmp[...] += drR[p].astype(F32)

            dsL[p] = dtmp[...].astype(BF16)
            dleft_copy(p).start()

    def decode_final():
        ddot(k)

        @pl.when(k > 0)
        def _():
            dright_copy(3 - k).wait_recv()
            dtmp[...] += drL[3 - k].astype(F32)

        @pl.when(k < 3)
        def _():
            dleft_copy(k).wait_recv()
            dtmp[...] += drR[k].astype(F32)

        dout_ref[...] = dtmp[...].astype(BF16)

    rmod = lax.rem(lax.broadcasted_iota(jnp.int32, (128, 128), 0), SAMPLES)
    lane128 = lax.broadcasted_iota(jnp.int32, (128, 128), 1)

    def suffix():
        loads[4].wait()
        qs = stack_heads(dq_ref[...])
        scores = jnp.zeros((128, 128), F32)
        lens = jnp.zeros((128, 128), jnp.int32)
        for r in range(SAMPLES):
            scores = jnp.where(rmod == r, dot_t(qs, skv[r, 0]), scores)
            lens = jnp.where(rmod == r, sl_ref[r], lens)
        live = lane128 < lens
        scores = jnp.where(live, scores * SCALE, FLOOR)
        new_k = jnp.concatenate([nkv_ref[:, 0, :].astype(F32)] * GROUP, axis=0)
        new_v = jnp.concatenate([nkv_ref[:, 1, :].astype(F32)] * GROUP, axis=0)
        new_score = jnp.sum(qs.astype(F32) * new_k, axis=1, keepdims=True) * SCALE
        top = jnp.maximum(jnp.max(scores, axis=1, keepdims=True), new_score)
        w = jnp.where(live, jnp.exp(scores - top), 0.0)
        new_w = jnp.exp(new_score - top)
        acc = new_w.astype(BF16).astype(F32) * new_v
        for r in range(SAMPLES):
            acc = acc + dot(jnp.where(rmod == r, w, 0.0).astype(BF16), skv[r, 1])
        suf_o[...] = acc
        suf_m[...] = jnp.broadcast_to(top, (128, 128))
        suf_l[...] = jnp.broadcast_to(jnp.sum(w, axis=1, keepdims=True) + new_w, (128, 128))

    y1 = [remote(qall.at[y], qall.at[y], ys.at[i], yr.at[i], ypeer[i]) for i in range(3)]
    core = remote(pall.at[c], pall.at[c], ms.at[1], mr.at[1], sibling)
    y2 = [
        remote(rsend.at[lax.rem(y + i + 1, 4)], rrecv.at[i], y2s.at[i], y2r.at[i], ypeer[i])
        for i in range(3)
    ]
    z2 = remote(zsend, zrecv, ms.at[2], mr.at[2], partner)

    def prefix():
        rows = qall[...].reshape(128, MSG)
        tags = rows[:, 1024:MSG].astype(F32)
        number = tags[:, 0:1] * 16.0 + tags[:, 1:2] - (a * 128).astype(F32)
        to_slot = jnp.where(number == lane128.astype(F32), 1.0, 0.0)
        qsel[...] = dot(to_slot.T.astype(BF16), rows[:, 0:1024]).astype(BF16)
        lane16 = lax.broadcasted_iota(jnp.int32, (SAMPLES, 128), 1)

        def one_prompt(j, _):
            slot = pl.ds(pl.multiple_of(j * SAMPLES, SAMPLES), SAMPLES)
            jc, jx = lax.rem(j, 2), j // 2
            q = stack_heads(qsel[slot, :])
            k_ = pall[jc, jx, 0:PX, :]
            v_ = pall[jc, jx, PX : 2 * PX, :]
            tail = pall[jc, jx, 2 * PX : KVROWS, :].astype(F32)
            n = tail[0:1, :] * 16.0 + tail[1:2, :]
            n = jnp.concatenate([n] * 3, axis=1)
            pos = lax.broadcasted_iota(jnp.int32, (1, PX), 1).astype(F32)
            s = dot_t(q, k_) * SCALE + jnp.where(pos < n, 0.0, FLOOR)
            top = jnp.max(s, axis=1, keepdims=True)
            w = jnp.exp(s - top)
            total = jnp.sum(w, axis=1, keepdims=True)
            o = dot(w.astype(BF16), v_) / total
            osel[slot, 0:1024] = unstack_heads(o).astype(BF16)
            stat = jnp.zeros((SAMPLES, 128), F32)
            for h in range(GROUP):
                rows_h = slice(SAMPLES * h, SAMPLES * (h + 1))
                stat = jnp.where(lane16 == h, top[rows_h], stat)
                stat = jnp.where(lane16 == GROUP + h, total[rows_h], stat)
            hi = stat.astype(BF16).astype(F32)
            mid = (stat - hi).astype(BF16).astype(F32)
            lo = (stat - hi - mid).astype(BF16).astype(F32)
            packed = hi + pltpu.roll(mid, 16, 1) + pltpu.roll(lo, 32, 1)
            osel[slot, 1024:MSG] = packed.astype(BF16)
            return 0

        lax.fori_loop(0, 8, one_prompt, 0)
        back = dot(to_slot.astype(BF16), osel[...]).astype(BF16)
        rsend[...] = back.reshape(4, 2, SAMPLES, MSG)

    def merge():
        got = (
            rsend[y, zh].astype(F32)
            + rrecv[0, zh].astype(F32)
            + rrecv[1, zh].astype(F32)
            + rrecv[2, zh].astype(F32)
            + zrecv[...].astype(F32)
        )
        tag = got[:, 1024:MSG]
        stat = tag + pltpu.roll(tag, 128 - 16, 1) + pltpu.roll(tag, 128 - 32, 1)
        pre_m = jnp.concatenate([stat[:, h : h + 1] for h in range(GROUP)], axis=0)
        pre_l = jnp.concatenate([stat[:, GROUP + h : GROUP + h + 1] for h in range(GROUP)], axis=0)
        pre_o = stack_heads(got[:, 0:1024])
        m = suf_m[...]
        top = jnp.maximum(m, pre_m)
        pre_f = jnp.exp(pre_m - top) * pre_l
        suf_f = jnp.exp(m - top)
        out = (pre_o * pre_f + suf_o[...] * suf_f) / (pre_f + suf_l[...] * suf_f)
        dattn[...] = unstack_heads(out).astype(BF16)

    def sum_for_partner():
        zsend[...] = (
            rsend[y, 1 - zh].astype(F32)
            + rrecv[0, 1 - zh].astype(F32)
            + rrecv[1, 1 - zh].astype(F32)
            + rrecv[2, 1 - zh].astype(F32)
        ).astype(BF16)

    items(0, 1)
    z1.wait()
    for copy in y1:
        copy.start()
    suffix()
    items(1, 3)
    for copy in px:
        copy.wait()
    core.start()
    for copy in y1:
        copy.wait()
    core.wait()
    prefix()
    for copy in y2:
        copy.start()
    items(3, 6)
    for copy in y2:
        copy.wait()
    sum_for_partner()
    z2.start()
    items(6, 9)
    z2.wait()
    merge()
    decode_items(0)
    items(9, 11)
    decode_items(1)
    items(11, 13)
    decode_items(2)
    items(13, 15)
    lax.fori_loop(0, NCH - 1, lambda j, _: (final_item(j), 0)[1], 0)
    decode_final()
    final_item(NCH - 1)
    for n in (13, 14):
        send_wait(n // NCH, n % NCH)
    for p in range(3):

        @pl.when(p < 3 - k)
        def _():
            dright_copy(p).wait_send()

        @pl.when(p < k)
        def _():
            dleft_copy(p).wait_send()


def local(
    decode_query, new_kv, sample_order, suffix_len, suffix_kv, prefix_kv, prefix_len,
    prefill_query, prefill_kv, prefill_segment, out_weight,
):
    vmem = pl.BlockSpec(memory_space=pltpu.VMEM)
    smem = pl.BlockSpec(memory_space=pltpu.SMEM)
    hbm = pl.BlockSpec(memory_space=pl.ANY)
    dma = pltpu.SemaphoreType.DMA
    ring = pltpu.VMEM((3, NCH, 256, CH), BF16)
    dring = pltpu.VMEM((3, SAMPLES, SHARD), BF16)
    return pl.pallas_call(
        kernel,
        out_shape=(
            jax.ShapeDtypeStruct((SAMPLES, SHARD), BF16),
            jax.ShapeDtypeStruct((256, SHARD), BF16),
        ),
        in_specs=[smem] * 3 + [vmem] * 4 + [hbm] * 4,
        out_specs=(vmem, vmem),
        scratch_shapes=[
            pltpu.VMEM((1024, 4 * SHARD), BF16),
            pltpu.VMEM((256, 1024), BF16),
            pltpu.VMEM((SAMPLES, 2, 128, 128), BF16),
            pltpu.VMEM((2, 4, KVROWS, HD), BF16),
            pltpu.VMEM((4, 2, SAMPLES, MSG), BF16),
            pltpu.VMEM((4, 2, SAMPLES, MSG), BF16),
            pltpu.VMEM((3, 2, SAMPLES, MSG), BF16),
            pltpu.VMEM((SAMPLES, MSG), BF16),
            pltpu.VMEM((SAMPLES, MSG), BF16),
            pltpu.VMEM((256, 1024), BF16),
            pltpu.VMEM((SAMPLES, 1024), BF16),
            pltpu.VMEM((256, CH), F32),
            pltpu.VMEM((SAMPLES, SHARD), F32),
            pltpu.VMEM((256, 256), F32),
            pltpu.VMEM((128, 1024), BF16),
            pltpu.VMEM((128, MSG), BF16),
            pltpu.VMEM((128, 128), F32),
            pltpu.VMEM((128, 128), F32),
            pltpu.VMEM((128, 128), F32),
            ring, ring, ring, ring,
            dring, dring, dring, dring,
            dma((5,)), dma((3,)), dma((3,)), dma((3,)), dma((3,)), dma((3,)), dma((3,)), dma((3,)), dma((3,)),
            dma((3, NCH)), dma((3, NCH)), dma((3, NCH)), dma((3, NCH)),
            dma((3,)), dma((3,)), dma((3,)), dma((3,)),
        ],
        compiler_params=pltpu.CompilerParams(
            collective_id=0, has_side_effects=True, vmem_limit_bytes=60 << 20
        ),
    )(
        sample_order, suffix_len, prefix_len, decode_query, new_kv, prefill_kv, prefill_segment,
        prefill_query, suffix_kv, prefix_kv, out_weight,
    )


def solution(mesh):
    return jax.shard_map(
        local,
        mesh=mesh,
        in_specs=(
            P("dp", "head"),
            P("dp", None, "head"),
            P("dp"),
            P("dp"),
            P("dp", None, None, "head"),
            P("dp", None, None, "head"),
            P("dp"),
            P("dp", "head"),
            P("dp", None, "head"),
            P("dp", None),
            P("head", None),
        ),
        out_specs=(P("dp", "head"), P("dp", "head")),
        check_vma=False,
    )
```

```python
import math

import jax
import jax.numpy as jnp
from jax import lax
from jax.experimental import pallas as pl
from jax.experimental.pallas import tpu as pltpu
from jax.sharding import PartitionSpec as P

MESH = pl.DeviceIdType.MESH
HD = 128
SAMPLES = 16
GROUP = 8
FLOOR = -1e30
SCALE = 1.0 / math.sqrt(HD)
PX = 384
MSG = 1024 + 128
KVROWS = 2 * PX + 16
CH = 256
NCH = 5
SHARD = CH * NCH
F32 = jnp.float32
BF16 = jnp.bfloat16


def dot(a, b):
    return jnp.dot(a, b, preferred_element_type=F32)


def dot_t(a, b):
    return lax.dot_general(a, b, (((1,), (1,)), ((), ())), preferred_element_type=F32)


def stack_heads(rows):
    return jnp.concatenate([rows[:, HD * h : HD * (h + 1)] for h in range(GROUP)], axis=0)


def unstack_heads(rows):
    return jnp.concatenate([rows[SAMPLES * h : SAMPLES * (h + 1)] for h in range(GROUP)], axis=1)


def kernel(
    so_ref, sl_ref, pfl_ref, dq_ref, nkv_ref, pkv_ref, seg_ref, pq_hbm, skv_hbm, pre_hbm, w_hbm,
    dout_ref, pout_ref,
    wv, pq, skv, pall, qall, rsend, rrecv, zsend, zrecv,
    attn, dattn, tmp, dtmp, bias, qsel, osel, suf_o, suf_m, suf_l,
    outP, inP, outS, inS, doutP, dinP, doutS, dinS,
    lsem, xs, xr, ys, yr, y2s, y2r, ms, mr,
    outPs, inPr, outSs, inSr, doutPs, dinPr, doutSs, dinSr,
):
    d = lax.axis_index("dp")
    k = lax.axis_index("head")
    c = lax.rem(d, 2)
    x = lax.rem(d // 2, 4)
    zh = lax.rem(d // 8, 2)
    y = d // 16
    a = d // 8

    def dev(y_, zh_, x_, c_):
        return (((y_ * 2 + zh_) * 4 + x_) * 2 + c_, k)

    sibling = dev(y, zh, x, 1 - c)
    partner = dev(y, 1 - zh, x, c)
    xpeer = [dev(y, zh, lax.rem(x + i, 4), c) for i in (1, 2, 3)]
    ypeer = [dev(lax.rem(y + i, 4), zh, x, c) for i in (1, 2, 3)]
    right = (d, jnp.minimum(k + 1, 3))
    left = (d, jnp.maximum(k - 1, 0))

    bar = pltpu.get_barrier_semaphore()
    for peer in [sibling, partner] + xpeer + ypeer:
        pl.semaphore_signal(bar, inc=1, device_id=peer, device_id_type=MESH)

    @pl.when(k < 3)
    def _():
        pl.semaphore_signal(bar, inc=1, device_id=right, device_id_type=MESH)

    @pl.when(k > 0)
    def _():
        pl.semaphore_signal(bar, inc=1, device_id=left, device_id_type=MESH)

    loads = [
        pltpu.make_async_copy(pq_hbm, pq, lsem.at[0]),
        pltpu.make_async_copy(pre_hbm.at[0, 0], pall.at[c, x, pl.ds(0, PX)], lsem.at[1]),
        pltpu.make_async_copy(pre_hbm.at[0, 1], pall.at[c, x, pl.ds(PX, PX)], lsem.at[2]),
        pltpu.make_async_copy(w_hbm, wv, lsem.at[3]),
        pltpu.make_async_copy(skv_hbm, skv, lsem.at[4]),
    ]
    for load in loads:
        load.start()

    lane = lax.broadcasted_iota(jnp.int32, (SAMPLES, 128), 1)
    row = lax.broadcasted_iota(jnp.int32, (SAMPLES, 128), 0)
    extra = jnp.zeros((SAMPLES, 128), jnp.int32)
    for r in range(SAMPLES):
        number = so_ref[r]
        part = jnp.where(lane == 0, number >> 4, jnp.where(lane == 1, number & 15, 0))
        extra = jnp.where(row == r, part, extra)
    qall[y, zh, :, 0:1024] = dq_ref[...]
    qall[y, zh, :, 1024:MSG] = extra.astype(F32).astype(BF16)
    length = pfl_ref[0]
    pall[c, x, 2 * PX : KVROWS, :] = (
        jnp.where(row == 0, length >> 4, jnp.where(row == 1, length & 15, 0)).astype(F32).astype(BF16)
    )

    pl.semaphore_wait(bar, 8 + jnp.where(k < 3, 1, 0) + jnp.where(k > 0, 1, 0))

    def remote(src, dst, ss, rs, target):
        return pltpu.make_async_remote_copy(
            src_ref=src, dst_ref=dst, send_sem=ss, recv_sem=rs, device_id=target, device_id_type=MESH
        )

    z1 = remote(qall.at[y, zh], qall.at[y, zh], ms.at[0], mr.at[0], partner)
    z1.start()
    loads[1].wait()
    loads[2].wait()
    px = [
        remote(pall.at[c, x], pall.at[c, x], xs.at[i], xr.at[i], xpeer[i]) for i in range(3)
    ]
    for copy in px:
        copy.start()

    qpos = lax.broadcasted_iota(jnp.int32, (256, 256), 0)
    kpos = lax.broadcasted_iota(jnp.int32, (256, 256), 1)
    seg_row = jnp.broadcast_to(seg_ref[...].astype(F32), (256, 256))
    seg_col = jnp.sum(jnp.where(qpos == kpos, seg_row, 0.0), axis=1, keepdims=True)
    bias[...] = jnp.where((kpos <= qpos) & (seg_row == seg_col), 0.0, FLOOR)
    keys = pkv_ref[:, 0, :]
    values = pkv_ref[:, 1, :]
    loads[0].wait()

    def one_head(h, _):
        cols = pl.ds(pl.multiple_of(h * HD, HD), HD)
        s = dot_t(pq[:, cols], keys) * SCALE + bias[...]
        top = jnp.max(s, axis=1, keepdims=True)
        w = jnp.exp(s - top)
        total = jnp.sum(w, axis=1, keepdims=True)
        attn[:, cols] = (dot(w.astype(BF16), values) / total).astype(BF16)
        return 0

    lax.fori_loop(0, GROUP, one_head, 0)
    loads[3].wait()

    edge = (k == 0) | (k == 3)
    mid = (k == 1) | (k == 2)
    side = k // 2
    mid_same = (d, 1 + side)
    mid_other = (d, 2 - side)
    edge_same = (d, 3 * side)

    def first_dest(p):
        return jnp.where(side == 0, 3 - p, p)

    def edge_copy(p, j):
        return remote(outP.at[p, j], inP.at[p, j], outPs.at[p, j], inPr.at[p, j], mid_same)

    def mid_copy(p, j):
        return remote(outP.at[p, j], inS.at[p, j], outPs.at[p, j], inSr.at[p, j], mid_other)

    def back_copy(j):
        return remote(outS.at[j], inS.at[0, j], outSs.at[j], inSr.at[0, j], edge_same)

    def cols_of(dest, j):
        return pl.ds(pl.multiple_of(dest * SHARD + j * CH, CH), CH)

    def first(p, j):
        tmp[...] = dot(attn[...], wv[:, cols_of(first_dest(p), j)])

        @pl.when(mid)
        def _():
            edge_copy(p, j).wait_recv()
            tmp[...] += inP[p, j].astype(F32)

        outP[p, j] = tmp[...].astype(BF16)

        @pl.when(edge)
        def _():
            edge_copy(p, j).start()

        @pl.when(mid)
        def _():
            mid_copy(p, j).start()

    def second(j):
        tmp[...] = dot(attn[...], wv[:, cols_of(3 * side, j)])
        mid_copy(0, j).wait_recv()
        outS[j] = (tmp[...] + inS[0, j].astype(F32)).astype(BF16)
        back_copy(j).start()

    def final(j):
        tmp[...] = dot(attn[...], wv[:, cols_of(k, j)])

        @pl.when(mid)
        def _():
            edge_copy(2, j).wait_recv()
            mid_copy(1, j).wait_recv()
            tmp[...] += inP[2, j].astype(F32) + inS[1, j].astype(F32)

        @pl.when(edge)
        def _():
            back_copy(j).wait_recv()
            tmp[...] += inS[0, j].astype(F32)

        pout_ref[:, pl.ds(pl.multiple_of(j * CH, CH), CH)] = tmp[...].astype(BF16)

    def items(lo, hi):
        def body(n, _):
            p, j = n // NCH, lax.rem(n, NCH)

            @pl.when(edge & (n >= 2))
            def _():
                edge_copy((n - 2) // NCH, lax.rem(n - 2, NCH)).wait_send()

            @pl.when(edge | (n < 2 * NCH))
            def _():
                first(p, j)

            @pl.when(mid & (n >= 1) & (n <= NCH))
            def _():
                second(n - 1)

            @pl.when(n >= 2 * NCH)
            def _():
                final(n - 2 * NCH)

            return 0

        lax.fori_loop(lo, hi, body, 0)

    def dedge_copy(p):
        return remote(doutP.at[p], dinP.at[p], doutPs.at[p], dinPr.at[p], mid_same)

    def dmid_copy(p):
        return remote(doutP.at[p], dinS.at[p], doutPs.at[p], dinSr.at[p], mid_other)

    def dback_copy():
        return remote(doutS, dinS.at[0], doutSs.at[0], dinSr.at[0], edge_same)

    def ddot(dest):
        def tile(j, _):
            out = pl.ds(pl.multiple_of(j * CH, CH), CH)
            dtmp[:, out] = dot(dattn[...], wv[:, cols_of(dest, j)])
            return 0

        lax.fori_loop(0, NCH, tile, 0)

    def dfirst(p):
        ddot(first_dest(p))

        @pl.when(mid)
        def _():
            dedge_copy(p).wait_recv()
            dtmp[...] += dinP[p].astype(F32)

        doutP[p] = dtmp[...].astype(BF16)

        @pl.when(edge)
        def _():
            dedge_copy(p).start()

        @pl.when(mid)
        def _():
            dmid_copy(p).start()

    def dsecond():
        ddot(3 * side)
        dmid_copy(0).wait_recv()
        doutS[...] = (dtmp[...] + dinS[0].astype(F32)).astype(BF16)
        dback_copy().start()

    def dfinal():
        ddot(k)

        @pl.when(mid)
        def _():
            dedge_copy(2).wait_recv()
            dmid_copy(1).wait_recv()
            dtmp[...] += dinP[2].astype(F32) + dinS[1].astype(F32)

        @pl.when(edge)
        def _():
            dback_copy().wait_recv()
            dtmp[...] += dinS[0].astype(F32)

        dout_ref[...] = dtmp[...].astype(BF16)

    rmod = lax.rem(lax.broadcasted_iota(jnp.int32, (128, 128), 0), SAMPLES)
    lane128 = lax.broadcasted_iota(jnp.int32, (128, 128), 1)

    def suffix():
        loads[4].wait()
        qs = stack_heads(dq_ref[...])
        scores = jnp.zeros((128, 128), F32)
        lens = jnp.zeros((128, 128), jnp.int32)
        for r in range(SAMPLES):
            scores = jnp.where(rmod == r, dot_t(qs, skv[r, 0]), scores)
            lens = jnp.where(rmod == r, sl_ref[r], lens)
        live = lane128 < lens
        scores = jnp.where(live, scores * SCALE, FLOOR)
        new_k = jnp.concatenate([nkv_ref[:, 0, :].astype(F32)] * GROUP, axis=0)
        new_v = jnp.concatenate([nkv_ref[:, 1, :].astype(F32)] * GROUP, axis=0)
        new_score = jnp.sum(qs.astype(F32) * new_k, axis=1, keepdims=True) * SCALE
        top = jnp.maximum(jnp.max(scores, axis=1, keepdims=True), new_score)
        w = jnp.where(live, jnp.exp(scores - top), 0.0)
        new_w = jnp.exp(new_score - top)
        acc = new_w.astype(BF16).astype(F32) * new_v
        for r in range(SAMPLES):
            acc = acc + dot(jnp.where(rmod == r, w, 0.0).astype(BF16), skv[r, 1])
        suf_o[...] = acc
        suf_m[...] = jnp.broadcast_to(top, (128, 128))
        suf_l[...] = jnp.broadcast_to(jnp.sum(w, axis=1, keepdims=True) + new_w, (128, 128))

    y1 = [remote(qall.at[y], qall.at[y], ys.at[i], yr.at[i], ypeer[i]) for i in range(3)]
    core = remote(pall.at[c], pall.at[c], ms.at[1], mr.at[1], sibling)
    y2 = [
        remote(rsend.at[lax.rem(y + i + 1, 4)], rrecv.at[i], y2s.at[i], y2r.at[i], ypeer[i])
        for i in range(3)
    ]
    z2 = remote(zsend, zrecv, ms.at[2], mr.at[2], partner)

    def prefix():
        rows = qall[...].reshape(128, MSG)
        tags = rows[:, 1024:MSG].astype(F32)
        number = tags[:, 0:1] * 16.0 + tags[:, 1:2] - (a * 128).astype(F32)
        to_slot = jnp.where(number == lane128.astype(F32), 1.0, 0.0)
        qsel[...] = dot(to_slot.T.astype(BF16), rows[:, 0:1024]).astype(BF16)
        lane16 = lax.broadcasted_iota(jnp.int32, (SAMPLES, 128), 1)

        def one_prompt(j, _):
            slot = pl.ds(pl.multiple_of(j * SAMPLES, SAMPLES), SAMPLES)
            jc, jx = lax.rem(j, 2), j // 2
            q = stack_heads(qsel[slot, :])
            k_ = pall[jc, jx, 0:PX, :]
            v_ = pall[jc, jx, PX : 2 * PX, :]
            tail = pall[jc, jx, 2 * PX : KVROWS, :].astype(F32)
            n = tail[0:1, :] * 16.0 + tail[1:2, :]
            n = jnp.concatenate([n] * 3, axis=1)
            pos = lax.broadcasted_iota(jnp.int32, (1, PX), 1).astype(F32)
            s = dot_t(q, k_) * SCALE + jnp.where(pos < n, 0.0, FLOOR)
            top = jnp.max(s, axis=1, keepdims=True)
            w = jnp.exp(s - top)
            total = jnp.sum(w, axis=1, keepdims=True)
            o = dot(w.astype(BF16), v_) / total
            osel[slot, 0:1024] = unstack_heads(o).astype(BF16)
            stat = jnp.zeros((SAMPLES, 128), F32)
            for h in range(GROUP):
                rows_h = slice(SAMPLES * h, SAMPLES * (h + 1))
                stat = jnp.where(lane16 == h, top[rows_h], stat)
                stat = jnp.where(lane16 == GROUP + h, total[rows_h], stat)
            hi = stat.astype(BF16).astype(F32)
            mid = (stat - hi).astype(BF16).astype(F32)
            lo = (stat - hi - mid).astype(BF16).astype(F32)
            packed = hi + pltpu.roll(mid, 16, 1) + pltpu.roll(lo, 32, 1)
            osel[slot, 1024:MSG] = packed.astype(BF16)
            return 0

        lax.fori_loop(0, 8, one_prompt, 0)
        back = dot(to_slot.astype(BF16), osel[...]).astype(BF16)
        rsend[...] = back.reshape(4, 2, SAMPLES, MSG)

    def merge():
        got = (
            rsend[y, zh].astype(F32)
            + rrecv[0, zh].astype(F32)
            + rrecv[1, zh].astype(F32)
            + rrecv[2, zh].astype(F32)
            + zrecv[...].astype(F32)
        )
        tag = got[:, 1024:MSG]
        stat = tag + pltpu.roll(tag, 128 - 16, 1) + pltpu.roll(tag, 128 - 32, 1)
        pre_m = jnp.concatenate([stat[:, h : h + 1] for h in range(GROUP)], axis=0)
        pre_l = jnp.concatenate([stat[:, GROUP + h : GROUP + h + 1] for h in range(GROUP)], axis=0)
        pre_o = stack_heads(got[:, 0:1024])
        m = suf_m[...]
        top = jnp.maximum(m, pre_m)
        pre_f = jnp.exp(pre_m - top) * pre_l
        suf_f = jnp.exp(m - top)
        out = (pre_o * pre_f + suf_o[...] * suf_f) / (pre_f + suf_l[...] * suf_f)
        dattn[...] = unstack_heads(out).astype(BF16)

    def sum_for_partner():
        zsend[...] = (
            rsend[y, 1 - zh].astype(F32)
            + rrecv[0, 1 - zh].astype(F32)
            + rrecv[1, 1 - zh].astype(F32)
            + rrecv[2, 1 - zh].astype(F32)
        ).astype(BF16)

    items(0, 1)
    z1.wait()
    for copy in y1:
        copy.start()
    suffix()
    items(1, 4)
    for copy in px:
        copy.wait()
    core.start()
    for copy in y1:
        copy.wait()
    items(4, 5)
    core.wait()
    prefix()
    for copy in y2:
        copy.start()
    items(5, 7)
    for copy in y2:
        copy.wait()
    sum_for_partner()
    z2.start()
    items(7, 9)
    z2.wait()
    merge()
    dfirst(0)
    items(9, 11)
    dfirst(1)

    @pl.when(mid)
    def _():
        dsecond()

    items(11, 13)

    @pl.when(edge)
    def _():
        dfirst(2)

    items(13, 14)
    dfinal()
    items(14, 15)

    @pl.when(edge)
    def _():
        edge_copy(2, NCH - 2).wait_send()
        edge_copy(2, NCH - 1).wait_send()
        for p in range(3):
            dedge_copy(p).wait_send()

    @pl.when(mid)
    def _():
        def done(j, _):
            mid_copy(0, j).wait_send()
            mid_copy(1, j).wait_send()
            back_copy(j).wait_send()
            return 0

        lax.fori_loop(0, NCH, done, 0)
        dmid_copy(0).wait_send()
        dmid_copy(1).wait_send()
        dback_copy().wait_send()


def local(
    decode_query, new_kv, sample_order, suffix_len, suffix_kv, prefix_kv, prefix_len,
    prefill_query, prefill_kv, prefill_segment, out_weight,
):
    vmem = pl.BlockSpec(memory_space=pltpu.VMEM)
    smem = pl.BlockSpec(memory_space=pltpu.SMEM)
    hbm = pl.BlockSpec(memory_space=pl.ANY)
    dma = pltpu.SemaphoreType.DMA

    def ring(*lead):
        return pltpu.VMEM(lead + (256, CH), BF16)

    def dring(*lead):
        return pltpu.VMEM(lead + (SAMPLES, SHARD), BF16)

    return pl.pallas_call(
        kernel,
        out_shape=(
            jax.ShapeDtypeStruct((SAMPLES, SHARD), BF16),
            jax.ShapeDtypeStruct((256, SHARD), BF16),
        ),
        in_specs=[smem] * 3 + [vmem] * 4 + [hbm] * 4,
        out_specs=(vmem, vmem),
        scratch_shapes=[
            pltpu.VMEM((1024, 4 * SHARD), BF16),
            pltpu.VMEM((256, 1024), BF16),
            pltpu.VMEM((SAMPLES, 2, 128, 128), BF16),
            pltpu.VMEM((2, 4, KVROWS, HD), BF16),
            pltpu.VMEM((4, 2, SAMPLES, MSG), BF16),
            pltpu.VMEM((4, 2, SAMPLES, MSG), BF16),
            pltpu.VMEM((3, 2, SAMPLES, MSG), BF16),
            pltpu.VMEM((SAMPLES, MSG), BF16),
            pltpu.VMEM((SAMPLES, MSG), BF16),
            pltpu.VMEM((256, 1024), BF16),
            pltpu.VMEM((SAMPLES, 1024), BF16),
            pltpu.VMEM((256, CH), F32),
            pltpu.VMEM((SAMPLES, SHARD), F32),
            pltpu.VMEM((256, 256), F32),
            pltpu.VMEM((128, 1024), BF16),
            pltpu.VMEM((128, MSG), BF16),
            pltpu.VMEM((128, 128), F32),
            pltpu.VMEM((128, 128), F32),
            pltpu.VMEM((128, 128), F32),
            ring(3, NCH), ring(3, NCH), ring(NCH), ring(2, NCH),
            dring(3), dring(3), dring(), dring(2),
            dma((5,)), dma((3,)), dma((3,)), dma((3,)), dma((3,)), dma((3,)), dma((3,)), dma((3,)), dma((3,)),
            dma((3, NCH)), dma((3, NCH)), dma((NCH,)), dma((2, NCH)),
            dma((3,)), dma((3,)), dma((1,)), dma((2,)),
        ],
        compiler_params=pltpu.CompilerParams(
            collective_id=0, has_side_effects=True, vmem_limit_bytes=60 << 20
        ),
    )(
        sample_order, suffix_len, prefix_len, decode_query, new_kv, prefill_kv, prefill_segment,
        prefill_query, suffix_kv, prefix_kv, out_weight,
    )


def solution(mesh):
    return jax.shard_map(
        local,
        mesh=mesh,
        in_specs=(
            P("dp", "head"),
            P("dp", None, "head"),
            P("dp"),
            P("dp"),
            P("dp", None, None, "head"),
            P("dp", None, None, "head"),
            P("dp"),
            P("dp", "head"),
            P("dp", None, "head"),
            P("dp", None),
            P("head", None),
        ),
        out_specs=(P("dp", "head"), P("dp", "head")),
        check_vma=False,
    )
```

```python
import math

import jax
import jax.numpy as jnp
from jax import lax
from jax.experimental import pallas as pl
from jax.experimental.pallas import tpu as pltpu
from jax.sharding import PartitionSpec as P

MESH = pl.DeviceIdType.MESH
HD = 128
SAMPLES = 16
GROUP = 8
FLOOR = -1e30
SCALE = 1.0 / math.sqrt(HD)
PX = 384
MSG = 1024 + 128
KVROWS = 2 * PX + 16
CH = 256
NCH = 5
SHARD = CH * NCH
QT = 64
WR = 32
F32 = jnp.float32
BF16 = jnp.bfloat16


def dot(a, b):
    return jnp.dot(a, b, preferred_element_type=F32)


def dot_t(a, b):
    return lax.dot_general(a, b, (((1,), (1,)), ((), ())), preferred_element_type=F32)


def stack_heads(rows):
    return jnp.concatenate([rows[:, HD * h : HD * (h + 1)] for h in range(GROUP)], axis=0)


def unstack_heads(rows):
    return jnp.concatenate([rows[SAMPLES * h : SAMPLES * (h + 1)] for h in range(GROUP)], axis=1)


def kernel(
    so_ref, sl_ref, pfl_ref, dq_ref, nkv_ref, pkv_ref, seg_ref, pq_hbm, skv_hbm, pre_hbm, w_hbm,
    dout_ref, pout_ref,
    wv, pq, skv, pall, qall, rsend, rrecv, zsend, zrecv,
    attn, dattn, own, down, bias, qsel, osel, suf_o, suf_m, suf_l,
    wx, far_attn, outP, inP, outS, inS, outQ, inQ, doutP, dinP, doutS, dinS,
    lsem, xs, xr, ys, yr, y2s, y2r, ms, mr,
    shs, shr, gfs, gfr, gss, gsr, gcs, gcr,
    outPs, inPr, outSs, inSr, outAs, inAr, outQs, inQr, doutPs, dinPr, doutSs, dinSr,
):
    d = lax.axis_index("dp")
    k = lax.axis_index("head")
    c = lax.rem(d, 2)
    x = lax.rem(d // 2, 4)
    zh = lax.rem(d // 8, 2)
    y = d // 16
    a = d // 8

    def dev(y_, zh_, x_, c_):
        return (((y_ * 2 + zh_) * 4 + x_) * 2 + c_, k)

    sibling = dev(y, zh, x, 1 - c)
    partner = dev(y, 1 - zh, x, c)
    xpeer = [dev(y, zh, lax.rem(x + i, 4), c) for i in (1, 2, 3)]
    ypeer = [dev(lax.rem(y + i, 4), zh, x, c) for i in (1, 2, 3)]
    right = (d, jnp.minimum(k + 1, 3))
    left = (d, jnp.maximum(k - 1, 0))

    bar = pltpu.get_barrier_semaphore()
    for peer in [sibling, partner] + xpeer + ypeer:
        pl.semaphore_signal(bar, inc=1, device_id=peer, device_id_type=MESH)

    @pl.when(k < 3)
    def _():
        pl.semaphore_signal(bar, inc=1, device_id=right, device_id_type=MESH)

    @pl.when(k > 0)
    def _():
        pl.semaphore_signal(bar, inc=1, device_id=left, device_id_type=MESH)

    loads = [
        pltpu.make_async_copy(pq_hbm, pq, lsem.at[0]),
        pltpu.make_async_copy(pre_hbm.at[0, 0], pall.at[c, x, pl.ds(0, PX)], lsem.at[1]),
        pltpu.make_async_copy(pre_hbm.at[0, 1], pall.at[c, x, pl.ds(PX, PX)], lsem.at[2]),
        pltpu.make_async_copy(skv_hbm, skv, lsem.at[3]),
    ]
    side = k // 2
    near = 1 + side
    far = 2 - side
    role_dest = [jnp.where(side == 0, 3, 0), 3 * side, far, near]

    def slab(dest):
        return pl.ds(pl.multiple_of(dest * SHARD, SHARD), SHARD)

    slabs = [
        pltpu.make_async_copy(w_hbm.at[:, slab(role_dest[i])], wv.at[i], lsem.at[4 + i]) for i in range(4)
    ]
    for load in [loads[0], loads[1], loads[2], slabs[0], loads[3]] + slabs[1:]:
        load.start()

    lane = lax.broadcasted_iota(jnp.int32, (SAMPLES, 128), 1)
    row = lax.broadcasted_iota(jnp.int32, (SAMPLES, 128), 0)
    extra = jnp.zeros((SAMPLES, 128), jnp.int32)
    for r in range(SAMPLES):
        number = so_ref[r]
        part = jnp.where(lane == 0, number >> 4, jnp.where(lane == 1, number & 15, 0))
        extra = jnp.where(row == r, part, extra)
    qall[y, zh, :, 0:1024] = dq_ref[...]
    qall[y, zh, :, 1024:MSG] = extra.astype(F32).astype(BF16)
    length = pfl_ref[0]
    pall[c, x, 2 * PX : KVROWS, :] = (
        jnp.where(row == 0, length >> 4, jnp.where(row == 1, length & 15, 0)).astype(F32).astype(BF16)
    )

    pl.semaphore_wait(bar, 8 + jnp.where(k < 3, 1, 0) + jnp.where(k > 0, 1, 0))

    def remote(src, dst, ss, rs, target):
        return pltpu.make_async_remote_copy(
            src_ref=src, dst_ref=dst, send_sem=ss, recv_sem=rs, device_id=target, device_id_type=MESH
        )

    edge = (k == 0) | (k == 3)
    mid = (k == 1) | (k == 2)
    mid_same = (d, 1 + side)
    mid_other = (d, 2 - side)
    edge_same = (d, 3 * side)

    def chunk(j):
        return pl.ds(pl.multiple_of(j * CH, CH), CH)

    def rows_of(q):
        return pl.ds(pl.multiple_of(q * QT, QT), QT)

    fast = jnp.where(c == 0, x, y)
    slow = jnp.where(c == 0, y, x)
    share = c * 16 + slow * 4 + fast

    def share_copy(w):
        dest = far if w == 0 else near
        rows = pl.ds(pl.multiple_of(share * WR, WR), WR)
        return remote(w_hbm.at[rows, slab(dest)], wx.at[w, c, slow, fast], shs.at[w], shr.at[w], mid_same)

    def line_peer(i, fast_axis):
        along_x = (c == 0) if fast_axis else (c == 1)
        return (jnp.where(along_x, xpeer[i][0], ypeer[i][0]), k)

    z1 = remote(qall.at[y, zh], qall.at[y, zh], ms.at[0], mr.at[0], partner)
    z1.start()

    @pl.when(edge)
    def _():
        share_copy(0).start()

    loads[1].wait()
    loads[2].wait()
    px = [
        remote(pall.at[c, x], pall.at[c, x], xs.at[i], xr.at[i], xpeer[i]) for i in range(3)
    ]
    for copy in px:
        copy.start()

    qpos = lax.broadcasted_iota(jnp.int32, (256, 256), 0)
    kpos = lax.broadcasted_iota(jnp.int32, (256, 256), 1)
    seg_row = jnp.broadcast_to(seg_ref[...].astype(F32), (256, 256))
    seg_col = jnp.sum(jnp.where(qpos == kpos, seg_row, 0.0), axis=1, keepdims=True)
    bias[...] = jnp.where((kpos <= qpos) & (seg_row == seg_col), 0.0, FLOOR)
    keys = pkv_ref[:, 0, :]
    values = pkv_ref[:, 1, :]
    loads[0].wait()

    def one_head(h, _):
        cols = pl.ds(pl.multiple_of(h * HD, HD), HD)
        s = dot_t(pq[:, cols], keys) * SCALE + bias[...]
        top = jnp.max(s, axis=1, keepdims=True)
        w = jnp.exp(s - top)
        total = jnp.sum(w, axis=1, keepdims=True)
        attn[:, cols] = (dot(w.astype(BF16), values) / total).astype(BF16)
        return 0

    lax.fori_loop(0, GROUP, one_head, 0, unroll=True)

    def gather_fast(w):
        return [
            remote(wx.at[w, c, slow, fast], wx.at[w, c, slow, fast], gfs.at[w, i], gfr.at[w, i], line_peer(i, True))
            for i in range(3)
        ]

    def gather_slow(w):
        return [
            remote(wx.at[w, c, slow], wx.at[w, c, slow], gss.at[w, i], gsr.at[w, i], line_peer(i, False))
            for i in range(3)
        ]

    def gather_core(w):
        return [remote(wx.at[w, c], wx.at[w, c], gcs.at[w], gcr.at[w], sibling)]

    def start(copies):
        for copy in copies:
            copy.start()

    def wait(copies):
        for copy in copies:
            copy.wait()

    def edge_copy(j):
        return remote(outP.at[j], inP.at[j], outPs.at[j], inPr.at[j], mid_same)

    def rows_copy(q):
        return remote(attn.at[rows_of(q)], far_attn.at[rows_of(q)], outAs.at[q], inAr.at[q], mid_same)

    def mid_copy(j):
        return remote(outP.at[j], inS.at[j], outPs.at[j], inSr.at[j], mid_other)

    def back_copy(j):
        return remote(outS.at[j], inS.at[j], outSs.at[j], inSr.at[j], edge_same)

    def cross_copy(q):
        return remote(outQ.at[q], inQ.at[q], outQs.at[q], inQr.at[q], mid_other)

    def own_part(i):
        slabs[i].wait()
        own[i] = dot(attn[...], wv[i])

    def first(j):
        @pl.when(mid)
        def _():
            edge_copy(j).wait_recv()
            outP[j] = (own[0, :, chunk(j)] + inP[j].astype(F32)).astype(BF16)
            mid_copy(j).start()

        @pl.when(edge)
        def _():
            outP[j] = own[0, :, chunk(j)].astype(BF16)
            edge_copy(j).start()

    def second(j):
        @pl.when(mid)
        def _():
            mid_copy(j).wait_recv()
            outS[j] = (own[1, :, chunk(j)] + inS[j].astype(F32)).astype(BF16)
            back_copy(j).start()

    def quarter(q):
        @pl.when(mid)
        def _():
            rows_copy(q).wait_recv()
            part = dot(far_attn[rows_of(q), :], wx[0].reshape(1024, SHARD))
            outQ[q] = (own[2, rows_of(q), :] + part).astype(BF16)
            cross_copy(q).start()

    def far_part():
        own[3] += dot(far_attn[...], wx[1].reshape(1024, SHARD))

    def mid_final(q):
        @pl.when(mid)
        def _():
            cross_copy(q).wait_recv()
            pout_ref[rows_of(q), :] = (own[3, rows_of(q), :] + inQ[q].astype(F32)).astype(BF16)

    def edge_final(j):
        @pl.when(edge)
        def _():
            back_copy(j).wait_recv()
            pout_ref[:, chunk(j)] = (own[1, :, chunk(j)] + inS[j].astype(F32)).astype(BF16)

    def dedge_copy(p):
        return remote(doutP.at[p], dinP.at[p], doutPs.at[p], dinPr.at[p], mid_same)

    def dmid_copy(p):
        return remote(doutP.at[p], dinS.at[p], doutPs.at[p], dinSr.at[p], mid_other)

    def dback_copy():
        return remote(doutS, dinS.at[0], doutSs.at[0], dinSr.at[0], edge_same)

    def dot_all():
        for i in range(4):
            down[i] = dot(dattn[...], wv[i])

    def dfirst(p):
        i = (0, 2, 3)[p]

        @pl.when(mid)
        def _():
            dedge_copy(p).wait_recv()
            doutP[p] = (down[i] + dinP[p].astype(F32)).astype(BF16)
            dmid_copy(p).start()

        @pl.when(edge)
        def _():
            doutP[p] = down[i].astype(BF16)
            dedge_copy(p).start()

    def dsecond():
        dmid_copy(0).wait_recv()
        doutS[...] = (down[1] + dinS[0].astype(F32)).astype(BF16)
        dback_copy().start()

    def dfinal():
        @pl.when(mid)
        def _():
            dedge_copy(2).wait_recv()
            dmid_copy(1).wait_recv()
            dout_ref[...] = (down[3] + dinP[2].astype(F32) + dinS[1].astype(F32)).astype(BF16)

        @pl.when(edge)
        def _():
            dback_copy().wait_recv()
            dout_ref[...] = (down[1] + dinS[0].astype(F32)).astype(BF16)

    rmod = lax.rem(lax.broadcasted_iota(jnp.int32, (128, 128), 0), SAMPLES)
    lane128 = lax.broadcasted_iota(jnp.int32, (128, 128), 1)

    def suffix():
        loads[3].wait()
        qs = stack_heads(dq_ref[...])
        scores = jnp.zeros((128, 128), F32)
        lens = jnp.zeros((128, 128), jnp.int32)
        for r in range(SAMPLES):
            scores = jnp.where(rmod == r, dot_t(qs, skv[r, 0]), scores)
            lens = jnp.where(rmod == r, sl_ref[r], lens)
        live = lane128 < lens
        scores = jnp.where(live, scores * SCALE, FLOOR)
        new_k = jnp.concatenate([nkv_ref[:, 0, :].astype(F32)] * GROUP, axis=0)
        new_v = jnp.concatenate([nkv_ref[:, 1, :].astype(F32)] * GROUP, axis=0)
        new_score = jnp.sum(qs.astype(F32) * new_k, axis=1, keepdims=True) * SCALE
        top = jnp.maximum(jnp.max(scores, axis=1, keepdims=True), new_score)
        w = jnp.where(live, jnp.exp(scores - top), 0.0)
        new_w = jnp.exp(new_score - top)
        acc = new_w.astype(BF16).astype(F32) * new_v
        for r in range(SAMPLES):
            acc = acc + dot(jnp.where(rmod == r, w, 0.0).astype(BF16), skv[r, 1])
        suf_o[...] = acc
        suf_m[...] = jnp.broadcast_to(top, (128, 128))
        suf_l[...] = jnp.broadcast_to(jnp.sum(w, axis=1, keepdims=True) + new_w, (128, 128))

    y1 = [remote(qall.at[y], qall.at[y], ys.at[i], yr.at[i], ypeer[i]) for i in range(3)]
    core = remote(pall.at[c], pall.at[c], ms.at[1], mr.at[1], sibling)
    y2 = [
        remote(rsend.at[lax.rem(y + i + 1, 4)], rrecv.at[i], y2s.at[i], y2r.at[i], ypeer[i])
        for i in range(3)
    ]
    z2 = remote(zsend, zrecv, ms.at[2], mr.at[2], partner)

    def prefix():
        rows = qall[...].reshape(128, MSG)
        tags = rows[:, 1024:MSG].astype(F32)
        number = tags[:, 0:1] * 16.0 + tags[:, 1:2] - (a * 128).astype(F32)
        to_slot = jnp.where(number == lane128.astype(F32), 1.0, 0.0)
        qsel[...] = dot(to_slot.T.astype(BF16), rows[:, 0:1024]).astype(BF16)
        head128 = lax.broadcasted_iota(jnp.int32, (128, 128), 0) // SAMPLES

        def one_prompt(j, _):
            slot = pl.ds(pl.multiple_of(j * SAMPLES, SAMPLES), SAMPLES)
            jc, jx = lax.rem(j, 2), j // 2
            q = stack_heads(qsel[slot, :])
            k_ = pall[jc, jx, 0:PX, :]
            v_ = pall[jc, jx, PX : 2 * PX, :]
            tail = pall[jc, jx, 2 * PX : KVROWS, :].astype(F32)
            n = tail[0:1, :] * 16.0 + tail[1:2, :]
            n = jnp.concatenate([n] * 3, axis=1)
            pos = lax.broadcasted_iota(jnp.int32, (1, PX), 1).astype(F32)
            s = dot_t(q, k_) * SCALE + jnp.where(pos < n, 0.0, FLOOR)
            top = jnp.max(s, axis=1, keepdims=True)
            w = jnp.exp(s - top)
            total = jnp.sum(w, axis=1, keepdims=True)
            o = dot(w.astype(BF16), v_) / total
            osel[slot, 0:1024] = unstack_heads(o).astype(BF16)
            stat = jnp.where(lane128 == head128, top, jnp.where(lane128 == head128 + GROUP, total, 0.0))
            stat = sum(stat[SAMPLES * h : SAMPLES * (h + 1)] for h in range(GROUP))
            hi = stat.astype(BF16).astype(F32)
            mid = (stat - hi).astype(BF16).astype(F32)
            lo = (stat - hi - mid).astype(BF16).astype(F32)
            packed = hi + pltpu.roll(mid, 16, 1) + pltpu.roll(lo, 32, 1)
            osel[slot, 1024:MSG] = packed.astype(BF16)
            return 0

        lax.fori_loop(0, 8, one_prompt, 0, unroll=4)
        back = dot(to_slot.astype(BF16), osel[...]).astype(BF16)
        rsend[...] = back.reshape(4, 2, SAMPLES, MSG)

    def merge():
        got = (
            rsend[y, zh].astype(F32)
            + rrecv[0, zh].astype(F32)
            + rrecv[1, zh].astype(F32)
            + rrecv[2, zh].astype(F32)
            + zrecv[...].astype(F32)
        )
        tag = got[:, 1024:MSG]
        stat = tag + pltpu.roll(tag, 128 - 16, 1) + pltpu.roll(tag, 128 - 32, 1)
        pre_m = jnp.concatenate([stat[:, h : h + 1] for h in range(GROUP)], axis=0)
        pre_l = jnp.concatenate([stat[:, GROUP + h : GROUP + h + 1] for h in range(GROUP)], axis=0)
        pre_o = stack_heads(got[:, 0:1024])
        m = suf_m[...]
        top = jnp.maximum(m, pre_m)
        pre_f = jnp.exp(pre_m - top) * pre_l
        suf_f = jnp.exp(m - top)
        out = (pre_o * pre_f + suf_o[...] * suf_f) / (pre_f + suf_l[...] * suf_f)
        dattn[...] = unstack_heads(out).astype(BF16)

    def sum_for_partner():
        zsend[...] = (
            rsend[y, 1 - zh].astype(F32)
            + rrecv[0, 1 - zh].astype(F32)
            + rrecv[1, 1 - zh].astype(F32)
            + rrecv[2, 1 - zh].astype(F32)
        ).astype(BF16)

    def on_mid(f, *args):
        @pl.when(mid)
        def _():
            f(*args)

    def own_mid():
        own[2] = dot(attn[...], wv[2])
        own[3] = dot(attn[...], wv[3])

    def on_edge(f, *args):
        @pl.when(edge)
        def _():
            f(*args)

    def share_arrived(w):
        share_copy(w).wait_recv()
        start(gather_fast(w))

    def fast_done(w):
        wait(gather_fast(w))
        start(gather_slow(w))

    def slow_done(w):
        wait(gather_slow(w))
        start(gather_core(w))

    own_part(0)
    on_mid(share_arrived, 0)
    first(0)
    own_part(1)
    z1.wait()
    start(y1)
    first(1)
    on_edge(lambda: share_copy(1).start())
    suffix()
    on_mid(fast_done, 0)
    slabs[2].wait()
    slabs[3].wait()
    on_edge(lambda: edge_copy(0).wait_send())
    first(2)
    second(0)
    on_mid(own_mid)
    on_mid(share_arrived, 1)
    on_edge(lambda: edge_copy(1).wait_send())
    first(3)
    second(1)
    wait(px)
    core.start()
    wait(y1)
    on_edge(lambda: edge_copy(2).wait_send())
    first(4)
    second(2)
    on_mid(slow_done, 0)
    core.wait()
    on_edge(lambda: edge_copy(3).wait_send())
    on_edge(lambda: rows_copy(0).start())
    prefix()
    start(y2)
    second(3)
    on_mid(fast_done, 1)
    on_edge(lambda: edge_copy(4).wait_send())
    on_edge(lambda: rows_copy(1).start())
    on_mid(lambda: wait(gather_core(0)))
    quarter(0)
    second(4)
    on_edge(lambda: rows_copy(0).wait_send())
    on_edge(lambda: rows_copy(2).start())
    wait(y2)
    sum_for_partner()
    z2.start()
    quarter(1)
    on_edge(lambda: rows_copy(1).wait_send())
    on_edge(lambda: rows_copy(3).start())
    for j in range(NCH):
        edge_final(j)
    quarter(2)
    on_mid(slow_done, 1)
    z2.wait()
    merge()
    dot_all()
    dfirst(0)
    dfirst(1)
    on_edge(lambda: dfirst(2))
    quarter(3)
    on_mid(dsecond)
    on_mid(lambda: wait(gather_core(1)))
    on_mid(far_part)
    mid_final(0)
    mid_final(1)
    mid_final(2)
    dfinal()
    mid_final(3)

    @pl.when(edge)
    def _():
        share_copy(0).wait_send()
        share_copy(1).wait_send()
        rows_copy(2).wait_send()
        rows_copy(3).wait_send()
        for p in range(3):
            dedge_copy(p).wait_send()

    @pl.when(mid)
    def _():
        for j in range(NCH):
            mid_copy(j).wait_send()
            back_copy(j).wait_send()
        for q in range(4):
            cross_copy(q).wait_send()
        dmid_copy(0).wait_send()
        dmid_copy(1).wait_send()
        dback_copy().wait_send()


def hand_over(a_ref, b_ref, a_out, b_out):
    a_out[...] = a_ref[...]
    b_out[...] = b_ref[...]


def local(
    decode_query, new_kv, sample_order, suffix_len, suffix_kv, prefix_kv, prefix_len,
    prefill_query, prefill_kv, prefill_segment, out_weight,
):
    vmem = pl.BlockSpec(memory_space=pltpu.VMEM)
    smem = pl.BlockSpec(memory_space=pltpu.SMEM)
    hbm = pl.BlockSpec(memory_space=pl.ANY)
    dma = pltpu.SemaphoreType.DMA

    def ring(*lead):
        return pltpu.VMEM(lead + (256, CH), BF16)

    def dring(*lead):
        return pltpu.VMEM(lead + (SAMPLES, SHARD), BF16)

    results = pl.pallas_call(
        kernel,
        out_shape=(
            jax.ShapeDtypeStruct((SAMPLES, SHARD), BF16),
            jax.ShapeDtypeStruct((256, SHARD), BF16),
        ),
        in_specs=[smem] * 3 + [vmem] * 4 + [hbm] * 4,
        out_specs=(vmem, vmem),
        scratch_shapes=[
            pltpu.VMEM((4, 1024, SHARD), BF16),
            pltpu.VMEM((256, 1024), BF16),
            pltpu.VMEM((SAMPLES, 2, 128, 128), BF16),
            pltpu.VMEM((2, 4, KVROWS, HD), BF16),
            pltpu.VMEM((4, 2, SAMPLES, MSG), BF16),
            pltpu.VMEM((4, 2, SAMPLES, MSG), BF16),
            pltpu.VMEM((3, 2, SAMPLES, MSG), BF16),
            pltpu.VMEM((SAMPLES, MSG), BF16),
            pltpu.VMEM((SAMPLES, MSG), BF16),
            pltpu.VMEM((256, 1024), BF16),
            pltpu.VMEM((SAMPLES, 1024), BF16),
            pltpu.VMEM((4, 256, SHARD), F32),
            pltpu.VMEM((4, SAMPLES, SHARD), F32),
            pltpu.VMEM((256, 256), F32),
            pltpu.VMEM((128, 1024), BF16),
            pltpu.VMEM((128, MSG), BF16),
            pltpu.VMEM((128, 128), F32),
            pltpu.VMEM((128, 128), F32),
            pltpu.VMEM((128, 128), F32),
            pltpu.VMEM((2, 2, 4, 4, WR, SHARD), BF16),
            pltpu.VMEM((256, 1024), BF16),
            ring(NCH), ring(NCH), ring(NCH), ring(NCH),
            pltpu.VMEM((4, QT, SHARD), BF16),
            pltpu.VMEM((4, QT, SHARD), BF16),
            dring(3), dring(3), dring(), dring(2),
            dma((8,)), dma((3,)), dma((3,)), dma((3,)), dma((3,)), dma((3,)), dma((3,)), dma((3,)), dma((3,)),
            dma((2,)), dma((2,)), dma((2, 3)), dma((2, 3)), dma((2, 3)), dma((2, 3)), dma((2,)), dma((2,)),
            dma((NCH,)), dma((NCH,)), dma((NCH,)), dma((NCH,)), dma((4,)), dma((4,)), dma((4,)), dma((4,)),
            dma((3,)), dma((3,)), dma((1,)), dma((2,)),
        ],
        compiler_params=pltpu.CompilerParams(
            collective_id=0, has_side_effects=True, vmem_limit_bytes=60 << 20
        ),
    )(
        sample_order, suffix_len, prefix_len, decode_query, new_kv, prefill_kv, prefill_segment,
        prefill_query, suffix_kv, prefix_kv, out_weight,
    )
    return pl.pallas_call(
        hand_over,
        out_shape=tuple(jax.ShapeDtypeStruct(r.shape, r.dtype) for r in results),
        in_specs=[vmem, vmem],
        out_specs=(vmem, vmem),
    )(*results)


def solution(mesh):
    return jax.shard_map(
        local,
        mesh=mesh,
        in_specs=(
            P("dp", "head"),
            P("dp", None, "head"),
            P("dp"),
            P("dp"),
            P("dp", None, None, "head"),
            P("dp", None, None, "head"),
            P("dp"),
            P("dp", "head"),
            P("dp", None, "head"),
            P("dp", None),
            P("head", None),
        ),
        out_specs=(P("dp", "head"), P("dp", "head")),
        check_vma=False,
    )
```

```python
import math

import jax
import jax.numpy as jnp
from jax import lax
from jax.experimental import pallas as pl
from jax.experimental.pallas import tpu as pltpu
from jax.sharding import PartitionSpec as P

MESH = pl.DeviceIdType.MESH
HD = 128
SAMPLES = 16
GROUP = 8
FLOOR = -1e30
SCALE = 1.0 / math.sqrt(HD)
PX = 384
MSG = 1024 + 128
KVROWS = 2 * PX + 16
CH = 128
NCH = 10
SHARD = CH * NCH
QT = 64
EX = 2
FAR = SHARD - EX * CH
WR = 32
F32 = jnp.float32
BF16 = jnp.bfloat16


def dot(a, b):
    return jnp.dot(a, b, preferred_element_type=F32)


def dot_t(a, b):
    return lax.dot_general(a, b, (((1,), (1,)), ((), ())), preferred_element_type=F32)


def stack_heads(rows):
    return jnp.concatenate([rows[:, HD * h : HD * (h + 1)] for h in range(GROUP)], axis=0)


def unstack_heads(rows):
    return jnp.concatenate([rows[SAMPLES * h : SAMPLES * (h + 1)] for h in range(GROUP)], axis=1)


def kernel(
    so_ref, sl_ref, pfl_ref, dq_hbm, nkv_hbm, pkv_hbm, seg_hbm, pq_hbm, skv_hbm, pre_hbm, w_hbm,
    dout_hbm, pout_hbm,
    dout_ref, pout_ref, osem,
    wv, dq_ref, nkv_ref, pkv_ref, seg_ref, pq, skv, pall, qall, rsend, rrecv, zsend, zrecv,
    attn, dattn, own, down, bias, qsel, osel, suf_o, suf_m, suf_l,
    wx_far, wx_near, far_attn, outP, inP, outS, inS, outQ, inQ, down_out, down_in,
    lsem, xs, xr, ys, yr, y2s, y2r, ms, mr,
    shs, shr, gfs, gfr, gss, gsr, gcs, gcr,
    outPs, inPr, outSs, inSr, outAs, inAr, outQs, inQr, downs, downr,
):
    wx = (wx_far, wx_near)
    d = lax.axis_index("dp")
    k = lax.axis_index("head")
    c = lax.rem(d, 2)
    x = lax.rem(d // 2, 4)
    zh = lax.rem(d // 8, 2)
    y = d // 16
    a = d // 8

    def dev(y_, zh_, x_, c_):
        return (((y_ * 2 + zh_) * 4 + x_) * 2 + c_, k)

    sibling = dev(y, zh, x, 1 - c)
    partner = dev(y, 1 - zh, x, c)
    xpeer = [dev(y, zh, lax.rem(x + i, 4), c) for i in (1, 2, 3)]
    ypeer = [dev(lax.rem(y + i, 4), zh, x, c) for i in (1, 2, 3)]

    bar = pltpu.get_barrier_semaphore()
    for peer in [sibling, partner] + xpeer + ypeer:
        pl.semaphore_signal(bar, inc=1, device_id=peer, device_id_type=MESH)

    for i in (1, 2, 3):
        pl.semaphore_signal(bar, inc=1, device_id=(d, lax.rem(k + i, 4)), device_id_type=MESH)

    loads = [
        pltpu.make_async_copy(pq_hbm, pq, lsem.at[0]),
        pltpu.make_async_copy(pre_hbm.at[0, 0], pall.at[c, x, pl.ds(0, PX)], lsem.at[1]),
        pltpu.make_async_copy(pre_hbm.at[0, 1], pall.at[c, x, pl.ds(PX, PX)], lsem.at[2]),
        pltpu.make_async_copy(skv_hbm, skv, lsem.at[3]),
    ]
    side = k // 2
    near = 1 + side
    far = 2 - side
    role_dest = [jnp.where(side == 0, 3, 0), 3 * side, far, near]

    def slab(dest):
        return pl.ds(pl.multiple_of(dest * SHARD, SHARD), SHARD)

    slabs = [
        pltpu.make_async_copy(w_hbm.at[:, slab(role_dest[i])], wv.at[i], lsem.at[4 + i]) for i in range(4)
    ]
    small = [
        pltpu.make_async_copy(dq_hbm, dq_ref, lsem.at[8]),
        pltpu.make_async_copy(pkv_hbm, pkv_ref, lsem.at[9]),
        pltpu.make_async_copy(seg_hbm, seg_ref, lsem.at[10]),
        pltpu.make_async_copy(nkv_hbm, nkv_ref, lsem.at[11]),
    ]
    for load in small + [loads[0], loads[1], loads[2], slabs[0], loads[3]] + slabs[1:]:
        load.start()

    lane = lax.broadcasted_iota(jnp.int32, (SAMPLES, 128), 1)
    row = lax.broadcasted_iota(jnp.int32, (SAMPLES, 128), 0)
    extra = jnp.zeros((SAMPLES, 128), jnp.int32)
    for r in range(SAMPLES):
        number = so_ref[r]
        part = jnp.where(lane == 0, number >> 4, jnp.where(lane == 1, number & 15, 0))
        extra = jnp.where(row == r, part, extra)
    small[0].wait()
    qall[y, zh, :, 0:1024] = dq_ref[...]
    qall[y, zh, :, 1024:MSG] = extra.astype(F32).astype(BF16)
    length = pfl_ref[0]
    pall[c, x, 2 * PX : KVROWS, :] = (
        jnp.where(row == 0, length >> 4, jnp.where(row == 1, length & 15, 0)).astype(F32).astype(BF16)
    )

    pl.semaphore_wait(bar, 11)

    def remote(src, dst, ss, rs, target):
        return pltpu.make_async_remote_copy(
            src_ref=src, dst_ref=dst, send_sem=ss, recv_sem=rs, device_id=target, device_id_type=MESH
        )

    edge = (k == 0) | (k == 3)
    mid = (k == 1) | (k == 2)
    mid_same = (d, 1 + side)
    mid_other = (d, 2 - side)
    edge_same = (d, 3 * side)

    def chunk(j):
        return pl.ds(pl.multiple_of(j * CH, CH), CH)

    def rows_of(q):
        return pl.ds(pl.multiple_of(q * QT, QT), QT)

    fast = jnp.where(c == 0, x, y)
    slow = jnp.where(c == 0, y, x)
    share = c * 16 + slow * 4 + fast

    def share_copy(w):
        rows = pl.ds(pl.multiple_of(share * WR, WR), WR)
        if w == 0:
            cols = pl.ds(pl.multiple_of(far * SHARD + EX * CH, CH), FAR)
        else:
            cols = slab(near)
        return remote(w_hbm.at[rows, cols], wx[w].at[c, slow, fast], shs.at[w], shr.at[w], mid_same)

    def line_peer(i, fast_axis):
        along_x = (c == 0) if fast_axis else (c == 1)
        return (jnp.where(along_x, xpeer[i][0], ypeer[i][0]), k)

    z1 = remote(qall.at[y, zh], qall.at[y, zh], ms.at[0], mr.at[0], partner)
    z1.start()

    @pl.when(edge)
    def _():
        share_copy(0).start()

    loads[1].wait()
    loads[2].wait()
    px = [
        remote(pall.at[c, x], pall.at[c, x], xs.at[i], xr.at[i], xpeer[i]) for i in range(3)
    ]

    @pl.when(edge | (c == 1))
    def _():
        for copy in px:
            copy.start()


    small[1].wait()
    small[2].wait()
    small[3].wait()
    qpos = lax.broadcasted_iota(jnp.int32, (256, 256), 0)
    kpos = lax.broadcasted_iota(jnp.int32, (256, 256), 1)
    seg_row = jnp.broadcast_to(seg_ref[...].astype(F32), (256, 256))
    seg_col = jnp.sum(jnp.where(qpos == kpos, seg_row, 0.0), axis=1, keepdims=True)
    bias[...] = jnp.where((kpos <= qpos) & (seg_row == seg_col), 0.0, FLOOR)
    keys = pkv_ref[:, 0, :]
    values = pkv_ref[:, 1, :]
    loads[0].wait()

    def one_head(h, _):
        cols = pl.ds(pl.multiple_of(h * HD, HD), HD)
        s = dot_t(pq[:, cols], keys) * SCALE + bias[...]
        top = jnp.max(s, axis=1, keepdims=True)
        w = jnp.exp(s - top)
        total = jnp.sum(w, axis=1, keepdims=True)
        attn[:, cols] = (dot(w.astype(BF16), values) / total).astype(BF16)
        return 0

    lax.fori_loop(0, GROUP, one_head, 0, unroll=True)

    def gather_fast(w):
        return [
            remote(wx[w].at[c, slow, fast], wx[w].at[c, slow, fast], gfs.at[w, i], gfr.at[w, i], line_peer(i, True))
            for i in range(3)
        ]

    def gather_slow(w):
        return [
            remote(wx[w].at[c, slow], wx[w].at[c, slow], gss.at[w, i], gsr.at[w, i], line_peer(i, False))
            for i in range(3)
        ]

    def gather_core(w):
        return [remote(wx[w].at[c], wx[w].at[c], gcs.at[w], gcr.at[w], sibling)]

    def start(copies):
        for copy in copies:
            copy.start()

    def wait(copies):
        for copy in copies:
            copy.wait()

    def edge_copy(j):
        return remote(outP.at[j], inP.at[j], outPs.at[j], inPr.at[j], mid_same)

    def rows_copy(q):
        return remote(attn.at[rows_of(q)], far_attn.at[rows_of(q)], outAs.at[q], inAr.at[q], mid_same)

    def mid_copy(j):
        return remote(outP.at[j], inS.at[j], outPs.at[j], inSr.at[j], mid_other)

    def back_copy(j):
        return remote(outS.at[j], inS.at[j], outSs.at[j], inSr.at[j], edge_same)

    def cross_copy(q):
        return remote(outQ.at[q], inQ.at[q], outQs.at[q], inQr.at[q], mid_other)

    def own_part(i):
        slabs[i].wait()
        own[i] = dot(attn[...], wv[i])

    def own_first(j):
        return own[0, :, chunk(j)] if j < NCH else own[2, :, chunk(j - NCH)]

    def first(j):
        @pl.when(mid)
        def _():
            edge_copy(j).wait_recv()
            outP[j] = (own_first(j) + inP[j].astype(F32)).astype(BF16)
            mid_copy(j).start()

        @pl.when(edge)
        def _():
            outP[j] = own_first(j).astype(BF16)
            edge_copy(j).start()

    def second(j):
        @pl.when(mid)
        def _():
            mid_copy(j).wait_recv()
            outS[j] = (own[1, :, chunk(j)] + inS[j].astype(F32)).astype(BF16)
            back_copy(j).start()

    def quarter(q):
        @pl.when(mid)
        def _():
            rows_copy(q).wait_recv()
            part = dot(far_attn[rows_of(q), :], wx_far[...].reshape(1024, FAR))
            outQ[q] = (own[2, rows_of(q), EX * CH : SHARD] + part).astype(BF16)
            cross_copy(q).start()

    def far_part():
        own[3] += dot(far_attn[...], wx_near[...].reshape(1024, SHARD))

    far_cols = pl.ds(EX * CH, FAR)

    def quarter_home(q):
        return pltpu.make_async_copy(
            pout_ref.at[rows_of(q), far_cols], pout_hbm.at[rows_of(q), far_cols], osem.at[q]
        )

    def first_home():
        cols = pl.ds(0, EX * CH)
        return pltpu.make_async_copy(pout_ref.at[:, cols], pout_hbm.at[:, cols], osem.at[4])

    def all_home():
        return pltpu.make_async_copy(pout_ref, pout_hbm, osem.at[5])

    def decode_home():
        return pltpu.make_async_copy(dout_ref, dout_hbm, osem.at[6])

    def mid_final(q):
        @pl.when(mid)
        def _():
            cross_copy(q).wait_recv()
            cols = slice(EX * CH, SHARD)
            pout_ref[rows_of(q), cols] = (own[3, rows_of(q), cols] + inQ[q].astype(F32)).astype(BF16)
            quarter_home(q).start()

    def mid_final_first(j):
        @pl.when(mid)
        def _():
            mid_copy(j).wait_recv()
            cols = chunk(j - NCH)
            pout_ref[:, cols] = (own[3, :, cols] + inS[j].astype(F32)).astype(BF16)

    def edge_final(j):
        @pl.when(edge)
        def _():
            back_copy(j).wait_recv()
            pout_ref[:, chunk(j)] = (own[1, :, chunk(j)] + inS[j].astype(F32)).astype(BF16)

    def row_copy(i):
        return remote(down_out.at[i], down_in.at[k], downs.at[i], downr.at[k], (d, role_dest[i]))

    def row_from(j):
        return remote(down_out.at[0], down_in.at[j], downs.at[0], downr.at[j], (d, j))

    def decode_out(i):
        down[i] = dot(dattn[...], wv[i])

        @pl.when(role_dest[i] != k)
        def _():
            down_out[i] = down[i].astype(BF16)
            row_copy(i).start()

    def decode_final():
        on_edge(lambda: down_sum(down[1]))
        on_mid(lambda: down_sum(down[3]))
        for j in range(4):

            @pl.when(k != j)
            def _():
                row_from(j).wait_recv()
                down[4] += down_in[j].astype(F32)

        dout_ref[...] = down[4].astype(BF16)
        decode_home().start()

    def down_sum(value):
        down[4] = value

    def decode_sent():
        for i in range(4):

            @pl.when(role_dest[i] != k)
            def _():
                row_copy(i).wait_send()

    rmod = lax.rem(lax.broadcasted_iota(jnp.int32, (128, 128), 0), SAMPLES)
    lane128 = lax.broadcasted_iota(jnp.int32, (128, 128), 1)

    def suffix():
        loads[3].wait()
        qs = stack_heads(dq_ref[...])
        scores = jnp.zeros((128, 128), F32)
        lens = jnp.zeros((128, 128), jnp.int32)
        for r in range(SAMPLES):
            scores = jnp.where(rmod == r, dot_t(qs, skv[r, 0]), scores)
            lens = jnp.where(rmod == r, sl_ref[r], lens)
        live = lane128 < lens
        scores = jnp.where(live, scores * SCALE, FLOOR)
        new_k = jnp.concatenate([nkv_ref[:, 0, :].astype(F32)] * GROUP, axis=0)
        new_v = jnp.concatenate([nkv_ref[:, 1, :].astype(F32)] * GROUP, axis=0)
        new_score = jnp.sum(qs.astype(F32) * new_k, axis=1, keepdims=True) * SCALE
        top = jnp.maximum(jnp.max(scores, axis=1, keepdims=True), new_score)
        w = jnp.where(live, jnp.exp(scores - top), 0.0)
        new_w = jnp.exp(new_score - top)
        acc = new_w.astype(BF16).astype(F32) * new_v
        for r in range(SAMPLES):
            acc = acc + dot(jnp.where(rmod == r, w, 0.0).astype(BF16), skv[r, 1])
        suf_o[...] = acc
        suf_m[...] = jnp.broadcast_to(top, (128, 128))
        suf_l[...] = jnp.broadcast_to(jnp.sum(w, axis=1, keepdims=True) + new_w, (128, 128))

    y1 = [remote(qall.at[y], qall.at[y], ys.at[i], yr.at[i], ypeer[i]) for i in range(3)]
    core = remote(pall.at[c], pall.at[c], ms.at[1], mr.at[1], sibling)
    y2 = [
        remote(rsend.at[lax.rem(y + i + 1, 4)], rrecv.at[i], y2s.at[i], y2r.at[i], ypeer[i])
        for i in range(3)
    ]
    z2 = remote(zsend, zrecv, ms.at[2], mr.at[2], partner)

    def to_slots():
        tags = qall[:, :, :, 1024:MSG].reshape(128, 128).astype(F32)
        number = tags[:, 0:1] * 16.0 + tags[:, 1:2] - (a * 128).astype(F32)
        return jnp.where(number == lane128.astype(F32), 1.0, 0.0)

    def prefix_begin():
        rows = qall[:, :, :, 0:1024].reshape(128, 1024)
        qsel[...] = dot(to_slots().T.astype(BF16), rows).astype(BF16)

    def prefix_part(lo, hi):
        head128 = lax.broadcasted_iota(jnp.int32, (128, 128), 0) // SAMPLES

        def one_prompt(j, _):
            slot = pl.ds(pl.multiple_of(j * SAMPLES, SAMPLES), SAMPLES)
            jc, jx = lax.rem(j, 2), j // 2
            q = stack_heads(qsel[slot, :])
            k_ = pall[jc, jx, 0:PX, :]
            v_ = pall[jc, jx, PX : 2 * PX, :]
            tail = pall[jc, jx, 2 * PX : KVROWS, :].astype(F32)
            n = tail[0:1, :] * 16.0 + tail[1:2, :]
            n = jnp.concatenate([n] * 3, axis=1)
            pos = lax.broadcasted_iota(jnp.int32, (1, PX), 1).astype(F32)
            s = dot_t(q, k_) * SCALE + jnp.where(pos < n, 0.0, FLOOR)
            top = jnp.max(s, axis=1, keepdims=True)
            w = jnp.exp(s - top)
            total = jnp.sum(w, axis=1, keepdims=True)
            o = dot(w.astype(BF16), v_) / total
            osel[slot, 0:1024] = unstack_heads(o).astype(BF16)
            stat = jnp.where(lane128 == head128, top, jnp.where(lane128 == head128 + GROUP, total, 0.0))
            stat = sum(stat[SAMPLES * h : SAMPLES * (h + 1)] for h in range(GROUP))
            hi_ = stat.astype(BF16).astype(F32)
            mid_ = (stat - hi_).astype(BF16).astype(F32)
            lo_ = (stat - hi_ - mid_).astype(BF16).astype(F32)
            packed = hi_ + pltpu.roll(mid_, 16, 1) + pltpu.roll(lo_, 32, 1)
            osel[slot, 1024:MSG] = packed.astype(BF16)
            return 0

        lax.fori_loop(lo, hi, one_prompt, 0, unroll=True)

    def prefix_end():
        back = dot(to_slots().astype(BF16), osel[...]).astype(BF16)
        rsend[...] = back.reshape(4, 2, SAMPLES, MSG)

    def merge():
        got = (
            rsend[y, zh].astype(F32)
            + rrecv[0, zh].astype(F32)
            + rrecv[1, zh].astype(F32)
            + rrecv[2, zh].astype(F32)
            + zrecv[...].astype(F32)
        )
        tag = got[:, 1024:MSG]
        stat = tag + pltpu.roll(tag, 128 - 16, 1) + pltpu.roll(tag, 128 - 32, 1)
        pre_m = jnp.concatenate([stat[:, h : h + 1] for h in range(GROUP)], axis=0)
        pre_l = jnp.concatenate([stat[:, GROUP + h : GROUP + h + 1] for h in range(GROUP)], axis=0)
        pre_o = stack_heads(got[:, 0:1024])
        m = suf_m[...]
        top = jnp.maximum(m, pre_m)
        pre_f = jnp.exp(pre_m - top) * pre_l
        suf_f = jnp.exp(m - top)
        out = (pre_o * pre_f + suf_o[...] * suf_f) / (pre_f + suf_l[...] * suf_f)
        dattn[...] = unstack_heads(out).astype(BF16)

    def sum_for_partner():
        zsend[...] = (
            rsend[y, 1 - zh].astype(F32)
            + rrecv[0, 1 - zh].astype(F32)
            + rrecv[1, 1 - zh].astype(F32)
            + rrecv[2, 1 - zh].astype(F32)
        ).astype(BF16)

    def on_mid(f, *args):
        @pl.when(mid)
        def _():
            f(*args)

    def own_mid():
        own[2] = dot(attn[...], wv[2])
        own[3] = dot(attn[...], wv[3])

    def on_edge(f, *args):
        @pl.when(edge)
        def _():
            f(*args)

    def share_arrived(w):
        share_copy(w).wait_recv()
        start(gather_fast(w))

    def fast_done(w):
        wait(gather_fast(w))
        start(gather_slow(w))

    def slow_done(w):
        wait(gather_slow(w))
        start(gather_core(w))

    def firsts(j):
        first(2 * j)
        first(2 * j + 1)

    def seconds(j):
        second(2 * j)
        second(2 * j + 1)

    def on_mid_core(i, f, *args):
        @pl.when(mid & (c == i))
        def _():
            f(*args)

    def own_far():
        own[2] = dot(attn[...], wv[2])

    def own_near():
        own[3] = dot(attn[...], wv[3])

    own_part(0)
    on_edge(firsts, 0)
    on_edge(firsts, 1)
    on_mid(share_arrived, 0)
    on_mid_core(0, start, px)
    own_part(1)
    z1.wait()
    start(y1)
    suffix()
    on_edge(firsts, 2)
    on_edge(lambda: share_copy(1).start())
    slabs[2].wait()
    slabs[3].wait()
    on_mid(firsts, 0)
    own_far()
    on_mid(own_near)
    on_mid_core(0, fast_done, 0)
    on_edge(firsts, 3)
    on_mid(firsts, 1)
    wait(px)
    core.start()
    wait(y1)
    prefix_begin()
    on_mid(firsts, 2)
    seconds(0)
    core.wait()
    on_mid_core(1, fast_done, 0)
    on_mid(firsts, 3)
    on_edge(firsts, 4)
    prefix_part(0, 8)
    prefix_end()
    start(y2)
    on_edge(firsts, 5)
    on_edge(lambda: rows_copy(0).start())
    on_mid(share_arrived, 1)
    on_mid(firsts, 4)
    seconds(1)
    on_mid_core(0, slow_done, 0)
    seconds(2)
    on_mid(firsts, 5)
    on_mid_core(0, fast_done, 1)
    wait(y2)
    sum_for_partner()
    z2.start()
    on_edge(lambda: rows_copy(1).start())
    on_edge(lambda: rows_copy(2).start())
    on_edge(lambda: rows_copy(3).start())
    on_mid_core(1, slow_done, 0)
    on_mid_core(1, fast_done, 1)
    seconds(3)
    on_mid(lambda: wait(gather_core(0)))
    quarter(0)
    seconds(4)
    quarter(1)
    z2.wait()
    merge()
    decode_out(0)
    decode_out(2)
    decode_out(3)
    decode_out(1)
    on_mid_core(0, slow_done, 1)
    quarter(2)
    on_mid_core(1, slow_done, 1)
    quarter(3)
    for j in range(NCH):
        edge_final(j)
    on_edge(lambda: all_home().start())
    on_mid(lambda: wait(gather_core(1)))
    on_mid(far_part)
    for j in range(NCH, NCH + EX):
        mid_final_first(j)
    on_mid(lambda: first_home().start())
    mid_final(0)
    mid_final(1)
    mid_final(2)
    decode_final()
    mid_final(3)

    decode_home().wait()

    @pl.when(edge)
    def _():
        all_home().wait()
        share_copy(0).wait_send()
        share_copy(1).wait_send()
        for j in range(NCH + EX):
            edge_copy(j).wait_send()
        for q in range(4):
            rows_copy(q).wait_send()

    @pl.when(mid)
    def _():
        first_home().wait()
        for q in range(4):
            quarter_home(q).wait()
        for j in range(NCH + EX):
            mid_copy(j).wait_send()
        for j in range(NCH):
            back_copy(j).wait_send()
        for q in range(4):
            cross_copy(q).wait_send()

    decode_sent()


def hand_over(a_ref, b_ref, a_out, b_out):
    a_out[...] = a_ref[...]
    b_out[...] = b_ref[...]


def local(
    decode_query, new_kv, sample_order, suffix_len, suffix_kv, prefix_kv, prefix_len,
    prefill_query, prefill_kv, prefill_segment, out_weight,
):
    vmem = pl.BlockSpec(memory_space=pltpu.VMEM)
    smem = pl.BlockSpec(memory_space=pltpu.SMEM)
    hbm = pl.BlockSpec(memory_space=pl.ANY)
    dma = pltpu.SemaphoreType.DMA

    def ring(*lead):
        return pltpu.VMEM(lead + (256, CH), BF16)

    def dring(*lead):
        return pltpu.VMEM(lead + (SAMPLES, SHARD), BF16)

    results = pl.pallas_call(
        kernel,
        out_shape=(
            jax.ShapeDtypeStruct((SAMPLES, SHARD), BF16),
            jax.ShapeDtypeStruct((256, SHARD), BF16),
        ),
        in_specs=[smem] * 3 + [hbm] * 8,
        out_specs=(hbm, hbm),
        scratch_shapes=[
            pltpu.VMEM((SAMPLES, SHARD), BF16),
            pltpu.VMEM((256, SHARD), BF16),
            dma((9,)),
            pltpu.VMEM((4, 1024, SHARD), BF16),
            pltpu.VMEM(decode_query.shape, BF16),
            pltpu.VMEM(new_kv.shape, BF16),
            pltpu.VMEM(prefill_kv.shape, BF16),
            pltpu.VMEM(prefill_segment.shape, jnp.int32),
            pltpu.VMEM((256, 1024), BF16),
            pltpu.VMEM((SAMPLES, 2, 128, 128), BF16),
            pltpu.VMEM((2, 4, KVROWS, HD), BF16),
            pltpu.VMEM((4, 2, SAMPLES, MSG), BF16),
            pltpu.VMEM((4, 2, SAMPLES, MSG), BF16),
            pltpu.VMEM((3, 2, SAMPLES, MSG), BF16),
            pltpu.VMEM((SAMPLES, MSG), BF16),
            pltpu.VMEM((SAMPLES, MSG), BF16),
            pltpu.VMEM((256, 1024), BF16),
            pltpu.VMEM((SAMPLES, 1024), BF16),
            pltpu.VMEM((4, 256, SHARD), F32),
            pltpu.VMEM((5, SAMPLES, SHARD), F32),
            pltpu.VMEM((256, 256), F32),
            pltpu.VMEM((128, 1024), BF16),
            pltpu.VMEM((128, MSG), BF16),
            pltpu.VMEM((128, 128), F32),
            pltpu.VMEM((128, 128), F32),
            pltpu.VMEM((128, 128), F32),
            pltpu.VMEM((2, 4, 4, WR, FAR), BF16),
            pltpu.VMEM((2, 4, 4, WR, SHARD), BF16),
            pltpu.VMEM((256, 1024), BF16),
            ring(NCH + EX), ring(NCH + EX), ring(NCH), ring(NCH + EX),
            pltpu.VMEM((4, QT, FAR), BF16),
            pltpu.VMEM((4, QT, FAR), BF16),
            dring(4), dring(4),
            dma((12,)), dma((3,)), dma((3,)), dma((3,)), dma((3,)), dma((3,)), dma((3,)), dma((3,)), dma((3,)),
            dma((2,)), dma((2,)), dma((2, 3)), dma((2, 3)), dma((2, 3)), dma((2, 3)), dma((2,)), dma((2,)),
            dma((NCH + EX,)), dma((NCH + EX,)), dma((NCH,)), dma((NCH + EX,)), dma((4,)), dma((4,)), dma((4,)), dma((4,)),
            dma((4,)), dma((4,)),
        ],
        compiler_params=pltpu.CompilerParams(
            collective_id=0, has_side_effects=True, vmem_limit_bytes=60 << 20
        ),
    )(
        sample_order, suffix_len, prefix_len, decode_query, new_kv, prefill_kv, prefill_segment,
        prefill_query, suffix_kv, prefix_kv, out_weight,
    )
    return pl.pallas_call(
        hand_over,
        out_shape=tuple(jax.ShapeDtypeStruct(r.shape, r.dtype) for r in results),
        in_specs=[vmem, vmem],
        out_specs=(vmem, vmem),
    )(*results)


def solution(mesh):
    return jax.shard_map(
        local,
        mesh=mesh,
        in_specs=(
            P("dp", "head"),
            P("dp", None, "head"),
            P("dp"),
            P("dp"),
            P("dp", None, None, "head"),
            P("dp", None, None, "head"),
            P("dp"),
            P("dp", "head"),
            P("dp", None, "head"),
            P("dp", None),
            P("head", None),
        ),
        out_specs=(P("dp", "head"), P("dp", "head")),
        check_vma=False,
    )
```

```python
import math

import jax
import jax.numpy as jnp
from jax import lax
from jax.experimental import pallas as pl
from jax.experimental.pallas import tpu as pltpu
from jax.sharding import PartitionSpec as P

MESH = pl.DeviceIdType.MESH
HD = 128
SAMPLES = 16
GROUP = 8
FLOOR = -1e30
SCALE = 1.0 / math.sqrt(HD)
PX = 384
MSG = 1024 + 128
KVROWS = 2 * PX + 16
CH = 128
NCH = 10
SHARD = CH * NCH
QT = 32
NQ = 8
EX = 2
FAR = SHARD - EX * CH
WR = 32
F32 = jnp.float32
BF16 = jnp.bfloat16


def dot(a, b):
    return jnp.dot(a, b, preferred_element_type=F32)


def dot_t(a, b):
    return lax.dot_general(a, b, (((1,), (1,)), ((), ())), preferred_element_type=F32)


def stack_heads(rows):
    return jnp.concatenate([rows[:, HD * h : HD * (h + 1)] for h in range(GROUP)], axis=0)


def unstack_heads(rows):
    return jnp.concatenate([rows[SAMPLES * h : SAMPLES * (h + 1)] for h in range(GROUP)], axis=1)


def kernel(
    so_ref, sl_ref, pfl_ref, dq_hbm, nkv_hbm, pkv_hbm, seg_hbm, pq_hbm, skv_hbm, pre_hbm, w_hbm,
    dout_hbm, pout_hbm,
    dout_ref, pout_ref, osem,
    wv, dq_ref, nkv_ref, pkv_ref, seg_ref, pq, skv, pall, qall, rsend, rrecv, zsend, zrecv,
    attn, dattn, own, down, bias, qsel, osel, suf_o, suf_m, suf_l,
    wx_far, wx_near, far_attn, outP, inP, outS, inS, outQ, inQ, down_out, down_in,
    lsem, xs, xr, ys, yr, y2s, y2r, ms, mr,
    shs, shr, gfs, gfr, gss, gsr, gcs, gcr,
    outPs, inPr, outSs, inSr, outAs, inAr, outQs, inQr, downs, downr,
):
    wx = (wx_far, wx_near)
    d = lax.axis_index("dp")
    k = lax.axis_index("head")
    c = lax.rem(d, 2)
    x = lax.rem(d // 2, 4)
    zh = lax.rem(d // 8, 2)
    y = d // 16
    a = d // 8

    def dev(y_, zh_, x_, c_):
        return (((y_ * 2 + zh_) * 4 + x_) * 2 + c_, k)

    sibling = dev(y, zh, x, 1 - c)
    partner = dev(y, 1 - zh, x, c)
    xpeer = [dev(y, zh, lax.rem(x + i, 4), c) for i in (1, 2, 3)]
    ypeer = [dev(lax.rem(y + i, 4), zh, x, c) for i in (1, 2, 3)]

    bar = pltpu.get_barrier_semaphore()
    for peer in [sibling, partner] + xpeer + ypeer:
        pl.semaphore_signal(bar, inc=1, device_id=peer, device_id_type=MESH)

    for i in (1, 2, 3):
        pl.semaphore_signal(bar, inc=1, device_id=(d, lax.rem(k + i, 4)), device_id_type=MESH)

    loads = [
        pltpu.make_async_copy(pq_hbm, pq, lsem.at[0]),
        pltpu.make_async_copy(pre_hbm.at[0, 0], pall.at[c, x, pl.ds(0, PX)], lsem.at[1]),
        pltpu.make_async_copy(pre_hbm.at[0, 1], pall.at[c, x, pl.ds(PX, PX)], lsem.at[2]),
        pltpu.make_async_copy(skv_hbm, skv, lsem.at[3]),
    ]
    side = k // 2
    near = 1 + side
    far = 2 - side
    role_dest = [jnp.where(side == 0, 3, 0), 3 * side, far, near]

    def slab(dest):
        return pl.ds(pl.multiple_of(dest * SHARD, SHARD), SHARD)

    slabs = [
        pltpu.make_async_copy(w_hbm.at[:, slab(role_dest[i])], wv.at[i], lsem.at[4 + i]) for i in range(4)
    ]
    small = [
        pltpu.make_async_copy(dq_hbm, dq_ref, lsem.at[8]),
        pltpu.make_async_copy(pkv_hbm, pkv_ref, lsem.at[9]),
        pltpu.make_async_copy(seg_hbm, seg_ref, lsem.at[10]),
        pltpu.make_async_copy(nkv_hbm, nkv_ref, lsem.at[11]),
    ]
    for load in small + [loads[0], loads[1], loads[2], slabs[0], loads[3]] + slabs[1:]:
        load.start()

    pl.semaphore_wait(bar, 11)


    def remote(src, dst, ss, rs, target):
        return pltpu.make_async_remote_copy(
            src_ref=src, dst_ref=dst, send_sem=ss, recv_sem=rs, device_id=target, device_id_type=MESH
        )

    edge = (k == 0) | (k == 3)
    mid = (k == 1) | (k == 2)
    mid_same = (d, 1 + side)
    mid_other = (d, 2 - side)
    edge_same = (d, 3 * side)

    def chunk(j):
        return pl.ds(pl.multiple_of(j * CH, CH), CH)

    def rows_of(q):
        return pl.ds(pl.multiple_of(q * QT, QT), QT)

    fast = jnp.where(c == 0, x, y)
    slow = jnp.where(c == 0, y, x)
    share = c * 16 + slow * 4 + fast

    def share_copy(w):
        rows = pl.ds(pl.multiple_of(share * WR, WR), WR)
        if w == 0:
            cols = pl.ds(pl.multiple_of(far * SHARD + EX * CH, CH), FAR)
        else:
            cols = slab(near)
        return remote(w_hbm.at[rows, cols], wx[w].at[c, slow, fast], shs.at[w], shr.at[w], mid_same)

    def line_peer(i, fast_axis):
        along_x = (c == 0) if fast_axis else (c == 1)
        return (jnp.where(along_x, xpeer[i][0], ypeer[i][0]), k)

    z1 = remote(qall.at[y, zh], qall.at[y, zh], ms.at[0], mr.at[0], partner)

    @pl.when(edge)
    def _():
        share_copy(0).start()

    lane = lax.broadcasted_iota(jnp.int32, (SAMPLES, 128), 1)
    row = lax.broadcasted_iota(jnp.int32, (SAMPLES, 128), 0)
    extra = jnp.zeros((SAMPLES, 128), jnp.int32)
    for r in range(SAMPLES):
        number = so_ref[r]
        part = jnp.where(lane == 0, number >> 4, jnp.where(lane == 1, number & 15, 0))
        extra = jnp.where(row == r, part, extra)
    small[0].wait()
    qall[y, zh, :, 0:1024] = dq_ref[...]
    qall[y, zh, :, 1024:MSG] = extra.astype(F32).astype(BF16)
    length = pfl_ref[0]
    pall[c, x, 2 * PX : KVROWS, :] = (
        jnp.where(row == 0, length >> 4, jnp.where(row == 1, length & 15, 0)).astype(F32).astype(BF16)
    )

    z1.start()
    loads[1].wait()
    loads[2].wait()
    px = [
        remote(pall.at[c, x], pall.at[c, x], xs.at[i], xr.at[i], xpeer[i]) for i in range(3)
    ]

    @pl.when(edge | (c == 1))
    def _():
        for copy in px:
            copy.start()


    small[1].wait()
    small[2].wait()
    small[3].wait()
    qpos = lax.broadcasted_iota(jnp.int32, (256, 256), 0)
    kpos = lax.broadcasted_iota(jnp.int32, (256, 256), 1)
    seg_row = jnp.broadcast_to(seg_ref[...].astype(F32), (256, 256))
    seg_col = jnp.sum(jnp.where(qpos == kpos, seg_row, 0.0), axis=1, keepdims=True)
    bias[...] = jnp.where((kpos <= qpos) & (seg_row == seg_col), 0.0, FLOOR)
    keys = pkv_ref[:, 0, :]
    values = pkv_ref[:, 1, :]
    loads[0].wait()

    def one_head(h, _):
        cols = pl.ds(pl.multiple_of(h * HD, HD), HD)
        s = dot_t(pq[:, cols], keys) * SCALE + bias[...]
        top = jnp.max(s, axis=1, keepdims=True)
        w = jnp.exp(s - top)
        total = jnp.sum(w, axis=1, keepdims=True)
        attn[:, cols] = (dot(w.astype(BF16), values) / total).astype(BF16)
        return 0

    lax.fori_loop(0, GROUP, one_head, 0, unroll=True)

    def gather_fast(w):
        return [
            remote(wx[w].at[c, slow, fast], wx[w].at[c, slow, fast], gfs.at[w, i], gfr.at[w, i], line_peer(i, True))
            for i in range(3)
        ]

    def gather_slow(w):
        return [
            remote(wx[w].at[c, slow], wx[w].at[c, slow], gss.at[w, i], gsr.at[w, i], line_peer(i, False))
            for i in range(3)
        ]

    def gather_core(w):
        return [remote(wx[w].at[c], wx[w].at[c], gcs.at[w], gcr.at[w], sibling)]

    def start(copies):
        for copy in copies:
            copy.start()

    def wait(copies):
        for copy in copies:
            copy.wait()

    def edge_copy(j):
        return remote(outP.at[j], inP.at[j], outPs.at[j], inPr.at[j], mid_same)

    def rows_copy(q):
        return remote(attn.at[rows_of(q)], far_attn.at[rows_of(q)], outAs.at[q], inAr.at[q], mid_same)

    def mid_copy(j):
        return remote(outP.at[j], inS.at[j], outPs.at[j], inSr.at[j], mid_other)

    def back_copy(j):
        return remote(outS.at[j], inS.at[j], outSs.at[j], inSr.at[j], edge_same)

    def cross_copy(q):
        return remote(outQ.at[q], inQ.at[q], outQs.at[q], inQr.at[q], mid_other)

    def own_part(i):
        slabs[i].wait()
        own[i] = dot(attn[...], wv[i])

    def own_first(j):
        return own[0, :, chunk(j)] if j < NCH else own[2, :, chunk(j - NCH)]

    def first(j):
        @pl.when(mid)
        def _():
            edge_copy(j).wait_recv()
            outP[j] = (own_first(j) + inP[j].astype(F32)).astype(BF16)
            mid_copy(j).start()

        @pl.when(edge)
        def _():
            outP[j] = own_first(j).astype(BF16)
            edge_copy(j).start()

    def second(j):
        @pl.when(mid)
        def _():
            mid_copy(j).wait_recv()
            outS[j] = (own[1, :, chunk(j)] + inS[j].astype(F32)).astype(BF16)
            back_copy(j).start()

    def quarter(q):
        @pl.when(mid)
        def _():
            rows_copy(q).wait_recv()
            part = dot(far_attn[rows_of(q), :], wx_far[...].reshape(1024, FAR))
            outQ[q] = (own[2, rows_of(q), EX * CH : SHARD] + part).astype(BF16)
            cross_copy(q).start()

    def far_part():
        own[3] += dot(far_attn[...], wx_near[...].reshape(1024, SHARD))

    far_cols = pl.ds(EX * CH, FAR)

    def quarter_home(q):
        return pltpu.make_async_copy(
            pout_ref.at[rows_of(q), far_cols], pout_hbm.at[rows_of(q), far_cols], osem.at[q]
        )

    def first_home():
        cols = pl.ds(0, EX * CH)
        return pltpu.make_async_copy(pout_ref.at[:, cols], pout_hbm.at[:, cols], osem.at[NQ])

    def all_home():
        return pltpu.make_async_copy(pout_ref, pout_hbm, osem.at[NQ + 1])

    def decode_home():
        return pltpu.make_async_copy(dout_ref, dout_hbm, osem.at[NQ + 2])

    def mid_final(q):
        @pl.when(mid)
        def _():
            cross_copy(q).wait_recv()
            cols = slice(EX * CH, SHARD)
            pout_ref[rows_of(q), cols] = (own[3, rows_of(q), cols] + inQ[q].astype(F32)).astype(BF16)
            quarter_home(q).start()

    def mid_final_first(j):
        @pl.when(mid)
        def _():
            mid_copy(j).wait_recv()
            cols = chunk(j - NCH)
            pout_ref[:, cols] = (own[3, :, cols] + inS[j].astype(F32)).astype(BF16)

    def edge_final(j):
        @pl.when(edge)
        def _():
            back_copy(j).wait_recv()
            pout_ref[:, chunk(j)] = (own[1, :, chunk(j)] + inS[j].astype(F32)).astype(BF16)

    def row_copy(i, slot, target):
        return remote(down_out.at[i], down_in.at[slot], downs.at[i], downr.at[slot], target)

    def row_from_edge(i):
        return row_copy(i, (0, 0, 1, 2)[i], mid_same)

    def row_to_edge():
        return row_copy(1, 3, edge_same)

    def row_across(i):
        return row_copy(i, 4, (d, role_dest[i]))

    def decode_out(i):
        down[i] = dot(dattn[...], wv[i])

        @pl.when(edge & (i != 1))
        def _():
            down_out[i] = down[i].astype(BF16)
            row_from_edge(i).start()

        @pl.when(mid & (i == 1))
        def _():
            down_out[1] = down[1].astype(BF16)
            row_to_edge().start()

    def decode_across(i):
        row_from_edge(i).wait_recv()
        down_out[i] = (down[i] + down_in[(0, 0, 1, 2)[i]].astype(F32)).astype(BF16)
        row_across(i).start()

    def decode_final():
        @pl.when(mid)
        def _():
            row_from_edge(3).wait_recv()
            row_across(2).wait_recv()
            dout_ref[...] = (down[3] + down_in[2].astype(F32) + down_in[4].astype(F32)).astype(BF16)

        @pl.when(edge)
        def _():
            row_to_edge().wait_recv()
            row_across(0).wait_recv()
            dout_ref[...] = (down[1] + down_in[3].astype(F32) + down_in[4].astype(F32)).astype(BF16)

        decode_home().start()

    rmod = lax.rem(lax.broadcasted_iota(jnp.int32, (128, 128), 0), SAMPLES)
    lane128 = lax.broadcasted_iota(jnp.int32, (128, 128), 1)

    def suffix():
        loads[3].wait()
        qs = stack_heads(dq_ref[...])
        scores = jnp.zeros((128, 128), F32)
        lens = jnp.zeros((128, 128), jnp.int32)
        for r in range(SAMPLES):
            scores = jnp.where(rmod == r, dot_t(qs, skv[r, 0]), scores)
            lens = jnp.where(rmod == r, sl_ref[r], lens)
        live = lane128 < lens
        scores = jnp.where(live, scores * SCALE, FLOOR)
        new_k = jnp.concatenate([nkv_ref[:, 0, :].astype(F32)] * GROUP, axis=0)
        new_v = jnp.concatenate([nkv_ref[:, 1, :].astype(F32)] * GROUP, axis=0)
        new_score = jnp.sum(qs.astype(F32) * new_k, axis=1, keepdims=True) * SCALE
        top = jnp.maximum(jnp.max(scores, axis=1, keepdims=True), new_score)
        w = jnp.where(live, jnp.exp(scores - top), 0.0)
        new_w = jnp.exp(new_score - top)
        acc = new_w.astype(BF16).astype(F32) * new_v
        for r in range(SAMPLES):
            acc = acc + dot(jnp.where(rmod == r, w, 0.0).astype(BF16), skv[r, 1])
        suf_o[...] = acc
        suf_m[...] = jnp.broadcast_to(top, (128, 128))
        suf_l[...] = jnp.broadcast_to(jnp.sum(w, axis=1, keepdims=True) + new_w, (128, 128))

    y1 = [remote(qall.at[y], qall.at[y], ys.at[i], yr.at[i], ypeer[i]) for i in range(3)]
    core = remote(pall.at[c], pall.at[c], ms.at[1], mr.at[1], sibling)
    y2 = [
        remote(rsend.at[lax.rem(y + i + 1, 4)], rrecv.at[i], y2s.at[i], y2r.at[i], ypeer[i])
        for i in range(3)
    ]
    z2 = remote(zsend, zrecv, ms.at[2], mr.at[2], partner)

    def to_slots():
        tags = qall[:, :, :, 1024:MSG].reshape(128, 128).astype(F32)
        number = tags[:, 0:1] * 16.0 + tags[:, 1:2] - (a * 128).astype(F32)
        return jnp.where(number == lane128.astype(F32), 1.0, 0.0)

    def prefix_begin():
        rows = qall[:, :, :, 0:1024].reshape(128, 1024)
        qsel[...] = dot(to_slots().T.astype(BF16), rows).astype(BF16)

    def prefix_part(lo, hi):
        head128 = lax.broadcasted_iota(jnp.int32, (128, 128), 0) // SAMPLES

        def one_prompt(j, _):
            slot = pl.ds(pl.multiple_of(j * SAMPLES, SAMPLES), SAMPLES)
            jc, jx = lax.rem(j, 2), j // 2
            q = stack_heads(qsel[slot, :])
            k_ = pall[jc, jx, 0:PX, :]
            v_ = pall[jc, jx, PX : 2 * PX, :]
            tail = pall[jc, jx, 2 * PX : KVROWS, :].astype(F32)
            n = tail[0:1, :] * 16.0 + tail[1:2, :]
            n = jnp.concatenate([n] * 3, axis=1)
            pos = lax.broadcasted_iota(jnp.int32, (1, PX), 1).astype(F32)
            s = dot_t(q, k_) * SCALE + jnp.where(pos < n, 0.0, FLOOR)
            top = jnp.max(s, axis=1, keepdims=True)
            w = jnp.exp(s - top)
            total = jnp.sum(w, axis=1, keepdims=True)
            o = dot(w.astype(BF16), v_) / total
            osel[slot, 0:1024] = unstack_heads(o).astype(BF16)
            stat = jnp.where(lane128 == head128, top, jnp.where(lane128 == head128 + GROUP, total, 0.0))
            stat = sum(stat[SAMPLES * h : SAMPLES * (h + 1)] for h in range(GROUP))
            hi_ = stat.astype(BF16).astype(F32)
            mid_ = (stat - hi_).astype(BF16).astype(F32)
            lo_ = (stat - hi_ - mid_).astype(BF16).astype(F32)
            packed = hi_ + pltpu.roll(mid_, 16, 1) + pltpu.roll(lo_, 32, 1)
            osel[slot, 1024:MSG] = packed.astype(BF16)
            return 0

        lax.fori_loop(lo, hi, one_prompt, 0, unroll=True)

    def prefix_end():
        back = dot(to_slots().astype(BF16), osel[...]).astype(BF16)
        rsend[...] = back.reshape(4, 2, SAMPLES, MSG)

    def merge():
        got = (
            rsend[y, zh].astype(F32)
            + rrecv[0, zh].astype(F32)
            + rrecv[1, zh].astype(F32)
            + rrecv[2, zh].astype(F32)
            + zrecv[...].astype(F32)
        )
        tag = got[:, 1024:MSG]
        stat = tag + pltpu.roll(tag, 128 - 16, 1) + pltpu.roll(tag, 128 - 32, 1)
        pre_m = jnp.concatenate([stat[:, h : h + 1] for h in range(GROUP)], axis=0)
        pre_l = jnp.concatenate([stat[:, GROUP + h : GROUP + h + 1] for h in range(GROUP)], axis=0)
        pre_o = stack_heads(got[:, 0:1024])
        m = suf_m[...]
        top = jnp.maximum(m, pre_m)
        pre_f = jnp.exp(pre_m - top) * pre_l
        suf_f = jnp.exp(m - top)
        out = (pre_o * pre_f + suf_o[...] * suf_f) / (pre_f + suf_l[...] * suf_f)
        dattn[...] = unstack_heads(out).astype(BF16)

    def sum_for_partner():
        zsend[...] = (
            rsend[y, 1 - zh].astype(F32)
            + rrecv[0, 1 - zh].astype(F32)
            + rrecv[1, 1 - zh].astype(F32)
            + rrecv[2, 1 - zh].astype(F32)
        ).astype(BF16)

    def on_mid(f, *args):
        @pl.when(mid)
        def _():
            f(*args)

    def own_mid():
        own[2] = dot(attn[...], wv[2])
        own[3] = dot(attn[...], wv[3])

    def on_edge(f, *args):
        @pl.when(edge)
        def _():
            f(*args)

    def share_arrived(w):
        share_copy(w).wait_recv()
        start(gather_fast(w))

    def fast_done(w):
        wait(gather_fast(w))
        start(gather_slow(w))

    def slow_done(w):
        wait(gather_slow(w))
        start(gather_core(w))

    def firsts(j):
        for i in (2 * j, 2 * j + 1):
            if i < NCH + EX:
                first(i)

    def seconds(j):
        second(2 * j)
        second(2 * j + 1)

    def on_mid_core(i, f, *args):
        @pl.when(mid & (c == i))
        def _():
            f(*args)

    def own_far():
        own[2] = dot(attn[...], wv[2])

    def own_near():
        own[3] = dot(attn[...], wv[3])

    def rows_out(lo, hi):
        for q in range(lo, hi):
            rows_copy(q).start()

    def sent_early():
        for j in range(NCH + EX):
            mid_copy(j).wait_send()
        for j in range(NCH):
            back_copy(j).wait_send()

    own_part(0)
    on_edge(firsts, 0)
    on_edge(lambda: share_copy(1).start())
    on_edge(firsts, 1)
    on_mid(share_arrived, 0)
    on_mid_core(0, start, px)
    own_part(1)
    z1.wait()
    start(y1)
    on_edge(firsts, 2)
    suffix()
    slabs[2].wait()
    slabs[3].wait()
    on_mid(firsts, 0)
    own_far()
    on_mid(share_arrived, 1)
    on_mid_core(0, fast_done, 0)
    on_edge(firsts, 3)
    on_mid(own_near)
    on_mid(firsts, 1)
    wait(px)
    core.start()
    wait(y1)
    prefix_begin()
    on_mid(firsts, 2)
    seconds(0)
    on_mid_core(1, fast_done, 0)
    core.wait()
    on_edge(firsts, 4)
    prefix_part(0, 4)
    on_mid(firsts, 3)
    prefix_part(4, 8)
    prefix_end()
    start(y2)
    on_edge(firsts, 5)
    on_edge(firsts, 6)
    on_edge(rows_out, 0, 2)
    on_mid(firsts, 4)
    seconds(1)
    on_mid_core(0, slow_done, 0)
    on_mid_core(0, fast_done, 1)
    seconds(2)
    on_mid(firsts, 5)
    on_mid_core(1, slow_done, 0)
    on_mid_core(1, fast_done, 1)
    on_mid(firsts, 6)
    wait(y2)
    sum_for_partner()
    z2.start()
    on_edge(rows_out, 2, 6)
    seconds(3)
    on_mid(lambda: wait(gather_core(0)))
    quarter(0)
    quarter(1)
    seconds(4)
    quarter(2)
    quarter(3)
    z2.wait()
    merge()
    decode_out(0)
    decode_out(2)
    decode_out(3)
    on_edge(rows_out, 6, 8)
    quarter(4)
    on_mid_core(0, slow_done, 1)
    decode_out(1)
    quarter(5)
    on_mid_core(1, slow_done, 1)
    on_mid(decode_across, 0)
    on_mid(decode_across, 2)
    quarter(6)
    on_mid(sent_early)
    quarter(7)
    for j in range(NCH):
        edge_final(j)
    on_edge(lambda: all_home().start())
    on_mid(lambda: wait(gather_core(1)))
    on_mid(far_part)
    for j in range(NCH, NCH + EX):
        mid_final_first(j)
    on_mid(lambda: first_home().start())
    for q in range(NQ - 1):
        mid_final(q)
    decode_final()
    mid_final(NQ - 1)

    decode_home().wait()

    @pl.when(edge)
    def _():
        all_home().wait()
        share_copy(0).wait_send()
        share_copy(1).wait_send()
        for j in range(NCH + EX):
            edge_copy(j).wait_send()
        for q in range(NQ):
            rows_copy(q).wait_send()
        for i in (0, 2, 3):
            row_from_edge(i).wait_send()

    @pl.when(mid)
    def _():
        first_home().wait()
        for q in range(NQ):
            quarter_home(q).wait()
            cross_copy(q).wait_send()
        row_across(0).wait_send()
        row_across(2).wait_send()
        row_to_edge().wait_send()


def hand_over(a_hbm, b_hbm, a_out, b_out, a_vmem, b_vmem, in_sems, out_sems):
    rows = b_vmem.shape[0] // 4
    parts = [(a_hbm, a_vmem, a_out)]
    for i in range(4):
        part = pl.ds(i * rows, rows)
        parts.append((b_hbm.at[part], b_vmem.at[part], b_out.at[part]))
    inward = [pltpu.make_async_copy(p[0], p[1], in_sems.at[i]) for i, p in enumerate(parts)]
    outward = [pltpu.make_async_copy(p[1], p[2], out_sems.at[i]) for i, p in enumerate(parts)]
    for copy in inward:
        copy.start()
    for come, go in zip(inward, outward):
        come.wait()
        go.start()
    for copy in outward:
        copy.wait()


def local(
    decode_query, new_kv, sample_order, suffix_len, suffix_kv, prefix_kv, prefix_len,
    prefill_query, prefill_kv, prefill_segment, out_weight,
):
    vmem = pl.BlockSpec(memory_space=pltpu.VMEM)
    smem = pl.BlockSpec(memory_space=pltpu.SMEM)
    hbm = pl.BlockSpec(memory_space=pl.ANY)
    dma = pltpu.SemaphoreType.DMA

    def ring(*lead):
        return pltpu.VMEM(lead + (256, CH), BF16)

    def dring(*lead):
        return pltpu.VMEM(lead + (SAMPLES, SHARD), BF16)

    results = pl.pallas_call(
        kernel,
        out_shape=(
            jax.ShapeDtypeStruct((SAMPLES, SHARD), BF16),
            jax.ShapeDtypeStruct((256, SHARD), BF16),
        ),
        in_specs=[smem] * 3 + [hbm] * 8,
        out_specs=(hbm, hbm),
        scratch_shapes=[
            pltpu.VMEM((SAMPLES, SHARD), BF16),
            pltpu.VMEM((256, SHARD), BF16),
            dma((NQ + 3,)),
            pltpu.VMEM((4, 1024, SHARD), BF16),
            pltpu.VMEM(decode_query.shape, BF16),
            pltpu.VMEM(new_kv.shape, BF16),
            pltpu.VMEM(prefill_kv.shape, BF16),
            pltpu.VMEM(prefill_segment.shape, jnp.int32),
            pltpu.VMEM((256, 1024), BF16),
            pltpu.VMEM((SAMPLES, 2, 128, 128), BF16),
            pltpu.VMEM((2, 4, KVROWS, HD), BF16),
            pltpu.VMEM((4, 2, SAMPLES, MSG), BF16),
            pltpu.VMEM((4, 2, SAMPLES, MSG), BF16),
            pltpu.VMEM((3, 2, SAMPLES, MSG), BF16),
            pltpu.VMEM((SAMPLES, MSG), BF16),
            pltpu.VMEM((SAMPLES, MSG), BF16),
            pltpu.VMEM((256, 1024), BF16),
            pltpu.VMEM((SAMPLES, 1024), BF16),
            pltpu.VMEM((4, 256, SHARD), F32),
            pltpu.VMEM((4, SAMPLES, SHARD), F32),
            pltpu.VMEM((256, 256), F32),
            pltpu.VMEM((128, 1024), BF16),
            pltpu.VMEM((128, MSG), BF16),
            pltpu.VMEM((128, 128), F32),
            pltpu.VMEM((128, 128), F32),
            pltpu.VMEM((128, 128), F32),
            pltpu.VMEM((2, 4, 4, WR, FAR), BF16),
            pltpu.VMEM((2, 4, 4, WR, SHARD), BF16),
            pltpu.VMEM((256, 1024), BF16),
            ring(NCH + EX), ring(NCH + EX), ring(NCH), ring(NCH + EX),
            pltpu.VMEM((NQ, QT, FAR), BF16),
            pltpu.VMEM((NQ, QT, FAR), BF16),
            dring(4), dring(5),
            dma((12,)), dma((3,)), dma((3,)), dma((3,)), dma((3,)), dma((3,)), dma((3,)), dma((3,)), dma((3,)),
            dma((2,)), dma((2,)), dma((2, 3)), dma((2, 3)), dma((2, 3)), dma((2, 3)), dma((2,)), dma((2,)),
            dma((NCH + EX,)), dma((NCH + EX,)), dma((NCH,)), dma((NCH + EX,)), dma((NQ,)), dma((NQ,)), dma((NQ,)), dma((NQ,)),
            dma((4,)), dma((5,)),
        ],
        compiler_params=pltpu.CompilerParams(
            collective_id=0, has_side_effects=True, vmem_limit_bytes=60 << 20
        ),
    )(
        sample_order, suffix_len, prefix_len, decode_query, new_kv, prefill_kv, prefill_segment,
        prefill_query, suffix_kv, prefix_kv, out_weight,
    )
    return pl.pallas_call(
        hand_over,
        out_shape=tuple(jax.ShapeDtypeStruct(r.shape, r.dtype) for r in results),
        in_specs=[hbm, hbm],
        out_specs=(hbm, hbm),
        scratch_shapes=[pltpu.VMEM(r.shape, r.dtype) for r in results] + [dma((5,)), dma((5,))],
    )(*results)


def solution(mesh):
    return jax.shard_map(
        local,
        mesh=mesh,
        in_specs=(
            P("dp", "head"),
            P("dp", None, "head"),
            P("dp"),
            P("dp"),
            P("dp", None, None, "head"),
            P("dp", None, None, "head"),
            P("dp"),
            P("dp", "head"),
            P("dp", None, "head"),
            P("dp", None),
            P("head", None),
        ),
        out_specs=(P("dp", "head"), P("dp", "head")),
        check_vma=False,
    )
```

```python
import math

import jax
import jax.numpy as jnp
from jax import lax
from jax.experimental import pallas as pl
from jax.experimental.pallas import tpu as pltpu
from jax.sharding import PartitionSpec as P

MESH = pl.DeviceIdType.MESH
HD = 128
SAMPLES = 16
GROUP = 8
FLOOR = -1e30
SCALE = 1.0 / math.sqrt(HD)
PX = 384
MSG = 1024 + 128
KVROWS = 2 * PX + 16
CH = 128
NCH = 10
SHARD = CH * NCH
QT = 32
NQ = 8
EX = 2
FAR = SHARD - EX * CH
WR = 32
F32 = jnp.float32
BF16 = jnp.bfloat16


def dot(a, b):
    return jnp.dot(a, b, preferred_element_type=F32)


def dot_t(a, b):
    return lax.dot_general(a, b, (((1,), (1,)), ((), ())), preferred_element_type=F32)


def stack_heads(rows):
    return jnp.concatenate([rows[:, HD * h : HD * (h + 1)] for h in range(GROUP)], axis=0)


def unstack_heads(rows):
    return jnp.concatenate([rows[SAMPLES * h : SAMPLES * (h + 1)] for h in range(GROUP)], axis=1)


def kernel(
    so_ref, sl_ref, pfl_ref, dq_hbm, nkv_hbm, pkv_hbm, seg_hbm, pq_hbm, skv_hbm, pre_hbm, w_hbm,
    dout_ref, pout_ref,
    wv, dq_ref, nkv_ref, pkv_ref, seg_ref, pq, skv, pall, qall, rsend, rrecv, zsend, zrecv,
    attn, dattn, own, down, bias, qsel, osel, suf_o, suf_m, suf_l,
    wx_far, wx_near, far_attn, outP, inP, outS, inS, outQ, inQ, down_out, down_in,
    lsem, xs, xr, ys, yr, y2s, y2r, ms, mr,
    shs, shr, gfs, gfr, gss, gsr, gcs, gcr,
    outPs, inPr, outSs, inSr, outAs, inAr, outQs, inQr, downs, downr,
):
    wx = (wx_far, wx_near)
    d = lax.axis_index("dp")
    k = lax.axis_index("head")
    c = lax.rem(d, 2)
    x = lax.rem(d // 2, 4)
    zh = lax.rem(d // 8, 2)
    y = d // 16
    a = d // 8

    def dev(y_, zh_, x_, c_):
        return (((y_ * 2 + zh_) * 4 + x_) * 2 + c_, k)

    sibling = dev(y, zh, x, 1 - c)
    partner = dev(y, 1 - zh, x, c)
    xpeer = [dev(y, zh, lax.rem(x + i, 4), c) for i in (1, 2, 3)]
    ypeer = [dev(lax.rem(y + i, 4), zh, x, c) for i in (1, 2, 3)]

    bar = pltpu.get_barrier_semaphore()
    for peer in [sibling, partner] + xpeer + ypeer:
        pl.semaphore_signal(bar, inc=1, device_id=peer, device_id_type=MESH)

    for i in (1, 2, 3):
        pl.semaphore_signal(bar, inc=1, device_id=(d, lax.rem(k + i, 4)), device_id_type=MESH)

    loads = [
        pltpu.make_async_copy(pq_hbm, pq, lsem.at[0]),
        pltpu.make_async_copy(pre_hbm.at[0, 0], pall.at[c, x, pl.ds(0, PX)], lsem.at[1]),
        pltpu.make_async_copy(pre_hbm.at[0, 1], pall.at[c, x, pl.ds(PX, PX)], lsem.at[2]),
        pltpu.make_async_copy(skv_hbm, skv, lsem.at[3]),
    ]
    side = k // 2
    near = 1 + side
    far = 2 - side
    role_dest = [jnp.where(side == 0, 3, 0), 3 * side, far, near]

    def slab(dest):
        return pl.ds(pl.multiple_of(dest * SHARD, SHARD), SHARD)

    slabs = [
        pltpu.make_async_copy(w_hbm.at[:, slab(role_dest[i])], wv.at[i], lsem.at[4 + i]) for i in range(4)
    ]
    small = [
        pltpu.make_async_copy(dq_hbm, dq_ref, lsem.at[8]),
        pltpu.make_async_copy(pkv_hbm, pkv_ref, lsem.at[9]),
        pltpu.make_async_copy(seg_hbm, seg_ref, lsem.at[10]),
        pltpu.make_async_copy(nkv_hbm, nkv_ref, lsem.at[11]),
    ]
    for load in small + [loads[0], loads[1], loads[2], slabs[0], loads[3]] + slabs[1:]:
        load.start()

    pl.semaphore_wait(bar, 11)


    def remote(src, dst, ss, rs, target):
        return pltpu.make_async_remote_copy(
            src_ref=src, dst_ref=dst, send_sem=ss, recv_sem=rs, device_id=target, device_id_type=MESH
        )

    edge = (k == 0) | (k == 3)
    mid = (k == 1) | (k == 2)
    mid_same = (d, 1 + side)
    mid_other = (d, 2 - side)
    edge_same = (d, 3 * side)

    def chunk(j):
        return pl.ds(pl.multiple_of(j * CH, CH), CH)

    def rows_of(q):
        return pl.ds(pl.multiple_of(q * QT, QT), QT)

    fast = jnp.where(c == 0, x, y)
    slow = jnp.where(c == 0, y, x)
    share = c * 16 + slow * 4 + fast

    def share_copy(w):
        rows = pl.ds(pl.multiple_of(share * WR, WR), WR)
        if w == 0:
            cols = pl.ds(pl.multiple_of(far * SHARD + EX * CH, CH), FAR)
        else:
            cols = slab(near)
        return remote(w_hbm.at[rows, cols], wx[w].at[c, slow, fast], shs.at[w], shr.at[w], mid_same)

    def line_peer(i, fast_axis):
        along_x = (c == 0) if fast_axis else (c == 1)
        return (jnp.where(along_x, xpeer[i][0], ypeer[i][0]), k)

    z1 = remote(qall.at[y, zh], qall.at[y, zh], ms.at[0], mr.at[0], partner)

    @pl.when(edge)
    def _():
        share_copy(0).start()

    lane = lax.broadcasted_iota(jnp.int32, (SAMPLES, 128), 1)
    row = lax.broadcasted_iota(jnp.int32, (SAMPLES, 128), 0)
    extra = jnp.zeros((SAMPLES, 128), jnp.int32)
    for r in range(SAMPLES):
        number = so_ref[r]
        part = jnp.where(lane == 0, number >> 4, jnp.where(lane == 1, number & 15, 0))
        extra = jnp.where(row == r, part, extra)
    small[0].wait()
    qall[y, zh, :, 0:1024] = dq_ref[...]
    qall[y, zh, :, 1024:MSG] = extra.astype(F32).astype(BF16)
    length = pfl_ref[0]
    pall[c, x, 2 * PX : KVROWS, :] = (
        jnp.where(row == 0, length >> 4, jnp.where(row == 1, length & 15, 0)).astype(F32).astype(BF16)
    )

    z1.start()
    loads[1].wait()
    loads[2].wait()
    px = [
        remote(pall.at[c, x], pall.at[c, x], xs.at[0], xr.at[0], xpeer[i]) for i in range(3)
    ]

    @pl.when(edge | (c == 1))
    def _():
        for copy in px:
            copy.start()


    small[1].wait()
    small[2].wait()
    small[3].wait()
    qpos = lax.broadcasted_iota(jnp.int32, (256, 256), 0)
    kpos = lax.broadcasted_iota(jnp.int32, (256, 256), 1)
    seg_row = jnp.broadcast_to(seg_ref[...].astype(F32), (256, 256))
    seg_col = jnp.sum(jnp.where(qpos == kpos, seg_row, 0.0), axis=1, keepdims=True)
    bias[...] = jnp.where((kpos <= qpos) & (seg_row == seg_col), 0.0, FLOOR)
    keys = pkv_ref[:, 0, :]
    values = pkv_ref[:, 1, :]
    loads[0].wait()

    def one_head(h, _):
        cols = pl.ds(pl.multiple_of(h * HD, HD), HD)
        s = dot_t(pq[:, cols], keys) * SCALE + bias[...]
        top = jnp.max(s, axis=1, keepdims=True)
        w = jnp.exp(s - top)
        total = jnp.sum(w, axis=1, keepdims=True)
        attn[:, cols] = (dot(w.astype(BF16), values) / total).astype(BF16)
        return 0

    lax.fori_loop(0, GROUP, one_head, 0, unroll=True)

    def gather_fast(w):
        return [
            remote(wx[w].at[c, slow, fast], wx[w].at[c, slow, fast], gfs.at[w], gfr.at[w], line_peer(i, True))
            for i in range(3)
        ]

    def gather_slow(w):
        return [
            remote(wx[w].at[c, slow], wx[w].at[c, slow], gss.at[w], gsr.at[w], line_peer(i, False))
            for i in range(3)
        ]

    def gather_core(w):
        return [remote(wx[w].at[c], wx[w].at[c], gcs.at[w], gcr.at[w], sibling)]

    def fast_all(w):
        three = wx[w].at[c, slow, pl.ds(0, 3)]
        return remote(three, three, gfs.at[w], gfr.at[w], line_peer(0, True))

    def slow_all(w):
        three = wx[w].at[c, pl.ds(0, 3)]
        return remote(three, three, gss.at[w], gsr.at[w], line_peer(0, False))

    def px_all():
        three = pall.at[c, pl.ds(0, 3)]
        return remote(three, three, xs.at[0], xr.at[0], xpeer[0])

    def y1_all():
        three = qall.at[pl.ds(0, 3)]
        return remote(three, three, ys.at[0], yr.at[0], ypeer[0])

    def y2_all():
        return remote(rsend.at[pl.ds(0, 3)], rrecv, y2s.at[0], y2r.at[0], ypeer[0])

    def start(copies):
        for copy in copies:
            copy.start()

    def wait(copies):
        for copy in copies:
            copy.wait()

    def edge_copy(j):
        return remote(outP.at[j], inP.at[j], outPs.at[0], inPr.at[j], mid_same)

    def rows_copy(q):
        return remote(attn.at[rows_of(q)], far_attn.at[rows_of(q)], outAs.at[0], inAr.at[q], mid_same)

    def mid_copy(j):
        return remote(outP.at[j], inS.at[j], outPs.at[0], inSr.at[j // 2], mid_other)

    def back_copy(j):
        return remote(outS.at[j], inS.at[j], outSs.at[0], inSr.at[j // 2], edge_same)

    def cross_copy(q):
        return remote(outQ.at[q], inQ.at[q], outQs.at[0], inQr.at[q], mid_other)

    def own_part(i):
        slabs[i].wait()
        own[i] = dot(attn[...], wv[i])

    def own_head():
        slabs[0].wait()
        own[0, :, 0 : 2 * CH] = dot(attn[...], wv[0, :, 0 : 2 * CH])

    def own_rest():
        own[0, :, 2 * CH : SHARD] = dot(attn[...], wv[0, :, 2 * CH : SHARD])

    def own_first(j):
        return own[0, :, chunk(j)] if j < NCH else own[2, :, chunk(j - NCH)]

    def first(j):
        @pl.when(mid)
        def _():
            edge_copy(j).wait_recv()
            outP[j] = (own_first(j) + inP[j].astype(F32)).astype(BF16)
            mid_copy(j).start()

        @pl.when(edge)
        def _():
            outP[j] = own_first(j).astype(BF16)
            edge_copy(j).start()

    def pair_in(j):
        two = pl.ds(2 * j, 2)
        return remote(outP.at[two], inS.at[two], outPs.at[0], inSr.at[j], mid_other)

    def seconds(j):
        @pl.when(mid)
        def _():
            pair_in(j).wait_recv()
            for i in (2 * j, 2 * j + 1):
                outS[i] = (own[1, :, chunk(i)] + inS[i].astype(F32)).astype(BF16)
                back_copy(i).start()

    def quarter(q):
        @pl.when(mid)
        def _():
            rows_copy(q).wait_recv()
            part = dot(far_attn[rows_of(q), :], wx_far[...].reshape(1024, FAR))
            outQ[q] = (own[2, rows_of(q), EX * CH : SHARD] + part).astype(BF16)
            cross_copy(q).start()

    def far_part():
        own[3] += dot(far_attn[...], wx_near[...].reshape(1024, SHARD))

    far_cols = pl.ds(EX * CH, FAR)

    def quarter_home(q):
        return pltpu.make_async_copy(
            pout_ref.at[rows_of(q), far_cols], pout_hbm.at[rows_of(q), far_cols], osem.at[q]
        )

    def first_home():
        cols = pl.ds(0, EX * CH)
        return pltpu.make_async_copy(pout_ref.at[:, cols], pout_hbm.at[:, cols], osem.at[NQ])

    def all_home():
        return pltpu.make_async_copy(pout_ref, pout_hbm, osem.at[NQ + 1])

    def decode_home():
        return pltpu.make_async_copy(dout_ref, dout_hbm, osem.at[NQ + 2])

    def mid_final(q):
        @pl.when(mid)
        def _():
            cross_copy(q).wait_recv()
            cols = slice(EX * CH, SHARD)
            pout_ref[rows_of(q), cols] = (own[3, rows_of(q), cols] + inQ[q].astype(F32)).astype(BF16)

    def mid_final_first(j):
        pair_in(j).wait_recv()
        for i in (2 * j, 2 * j + 1):
            cols = chunk(i - NCH)
            pout_ref[:, cols] = (own[3, :, cols] + inS[i].astype(F32)).astype(BF16)

    def edge_final(j):
        pair_in(j).wait_recv()
        for i in (2 * j, 2 * j + 1):
            pout_ref[:, chunk(i)] = (own[1, :, chunk(i)] + inS[i].astype(F32)).astype(BF16)

    def row_copy(i, slot, target):
        return remote(down_out.at[i], down_in.at[slot], downs.at[0], downr.at[slot], target)

    def row_from_edge(i):
        return row_copy(i, (0, 0, 1, 2)[i], mid_same)

    def row_to_edge():
        return row_copy(1, 3, edge_same)

    def row_across(i):
        return row_copy(i, 4, (d, role_dest[i]))

    def decode_out(i):
        down[i] = dot(dattn[...], wv[i])

        @pl.when(edge & (i != 1))
        def _():
            down_out[i] = down[i].astype(BF16)
            row_from_edge(i).start()

        @pl.when(mid & (i == 1))
        def _():
            down_out[1] = down[1].astype(BF16)
            row_to_edge().start()

    def decode_across(i):
        row_from_edge(i).wait_recv()
        down_out[i] = (down[i] + down_in[(0, 0, 1, 2)[i]].astype(F32)).astype(BF16)
        row_across(i).start()

    def decode_final():
        @pl.when(mid)
        def _():
            row_from_edge(3).wait_recv()
            row_across(2).wait_recv()
            dout_ref[...] = (down[3] + down_in[2].astype(F32) + down_in[4].astype(F32)).astype(BF16)

        @pl.when(edge)
        def _():
            row_to_edge().wait_recv()
            row_across(0).wait_recv()
            dout_ref[...] = (down[1] + down_in[3].astype(F32) + down_in[4].astype(F32)).astype(BF16)

    rmod = lax.rem(lax.broadcasted_iota(jnp.int32, (128, 128), 0), SAMPLES)
    lane128 = lax.broadcasted_iota(jnp.int32, (128, 128), 1)

    def suffix():
        loads[3].wait()
        qs = stack_heads(dq_ref[...])
        scores = jnp.zeros((128, 128), F32)
        lens = jnp.zeros((128, 128), jnp.int32)
        for r in range(SAMPLES):
            scores = jnp.where(rmod == r, dot_t(qs, skv[r, 0]), scores)
            lens = jnp.where(rmod == r, sl_ref[r], lens)
        live = lane128 < lens
        scores = jnp.where(live, scores * SCALE, FLOOR)
        new_k = jnp.concatenate([nkv_ref[:, 0, :].astype(F32)] * GROUP, axis=0)
        new_v = jnp.concatenate([nkv_ref[:, 1, :].astype(F32)] * GROUP, axis=0)
        new_score = jnp.sum(qs.astype(F32) * new_k, axis=1, keepdims=True) * SCALE
        top = jnp.maximum(jnp.max(scores, axis=1, keepdims=True), new_score)
        w = jnp.where(live, jnp.exp(scores - top), 0.0)
        new_w = jnp.exp(new_score - top)
        acc = new_w.astype(BF16).astype(F32) * new_v
        for r in range(SAMPLES):
            acc = acc + dot(jnp.where(rmod == r, w, 0.0).astype(BF16), skv[r, 1])
        suf_o[...] = acc
        suf_m[...] = jnp.broadcast_to(top, (128, 128))
        suf_l[...] = jnp.broadcast_to(jnp.sum(w, axis=1, keepdims=True) + new_w, (128, 128))

    y1 = [remote(qall.at[y], qall.at[y], ys.at[0], yr.at[0], ypeer[i]) for i in range(3)]
    core = remote(pall.at[c], pall.at[c], ms.at[1], mr.at[1], sibling)
    y2 = [
        remote(rsend.at[lax.rem(y + i + 1, 4)], rrecv.at[i], y2s.at[0], y2r.at[0], ypeer[i])
        for i in range(3)
    ]
    z2 = remote(zsend, zrecv, ms.at[2], mr.at[2], partner)

    def to_slots():
        tags = qall[:, :, :, 1024:MSG].reshape(128, 128).astype(F32)
        number = tags[:, 0:1] * 16.0 + tags[:, 1:2] - (a * 128).astype(F32)
        return jnp.where(number == lane128.astype(F32), 1.0, 0.0)

    def prefix_begin():
        rows = qall[:, :, :, 0:1024].reshape(128, 1024)
        qsel[...] = dot(to_slots().T.astype(BF16), rows).astype(BF16)

    def prefix_part(lo, hi):
        head128 = lax.broadcasted_iota(jnp.int32, (128, 128), 0) // SAMPLES

        def one_prompt(j, _):
            slot = pl.ds(pl.multiple_of(j * SAMPLES, SAMPLES), SAMPLES)
            jc, jx = lax.rem(j, 2), j // 2
            q = stack_heads(qsel[slot, :])
            k_ = pall[jc, jx, 0:PX, :]
            v_ = pall[jc, jx, PX : 2 * PX, :]
            tail = pall[jc, jx, 2 * PX : KVROWS, :].astype(F32)
            n = tail[0:1, :] * 16.0 + tail[1:2, :]
            n = jnp.concatenate([n] * 3, axis=1)
            pos = lax.broadcasted_iota(jnp.int32, (1, PX), 1).astype(F32)
            s = dot_t(q, k_) * SCALE + jnp.where(pos < n, 0.0, FLOOR)
            top = jnp.max(s, axis=1, keepdims=True)
            w = jnp.exp(s - top)
            total = jnp.sum(w, axis=1, keepdims=True)
            o = dot(w.astype(BF16), v_) / total
            osel[slot, 0:1024] = unstack_heads(o).astype(BF16)
            stat = jnp.where(lane128 == head128, top, jnp.where(lane128 == head128 + GROUP, total, 0.0))
            stat = sum(stat[SAMPLES * h : SAMPLES * (h + 1)] for h in range(GROUP))
            hi_ = stat.astype(BF16).astype(F32)
            mid_ = (stat - hi_).astype(BF16).astype(F32)
            lo_ = (stat - hi_ - mid_).astype(BF16).astype(F32)
            packed = hi_ + pltpu.roll(mid_, 16, 1) + pltpu.roll(lo_, 32, 1)
            osel[slot, 1024:MSG] = packed.astype(BF16)
            return 0

        lax.fori_loop(lo, hi, one_prompt, 0, unroll=True)

    def prefix_end():
        back = dot(to_slots().astype(BF16), osel[...]).astype(BF16)
        rsend[...] = back.reshape(4, 2, SAMPLES, MSG)

    def merge():
        got = (
            rsend[y, zh].astype(F32)
            + rrecv[0, zh].astype(F32)
            + rrecv[1, zh].astype(F32)
            + rrecv[2, zh].astype(F32)
            + zrecv[...].astype(F32)
        )
        tag = got[:, 1024:MSG]
        stat = tag + pltpu.roll(tag, 128 - 16, 1) + pltpu.roll(tag, 128 - 32, 1)
        pre_m = jnp.concatenate([stat[:, h : h + 1] for h in range(GROUP)], axis=0)
        pre_l = jnp.concatenate([stat[:, GROUP + h : GROUP + h + 1] for h in range(GROUP)], axis=0)
        pre_o = stack_heads(got[:, 0:1024])
        m = suf_m[...]
        top = jnp.maximum(m, pre_m)
        pre_f = jnp.exp(pre_m - top) * pre_l
        suf_f = jnp.exp(m - top)
        out = (pre_o * pre_f + suf_o[...] * suf_f) / (pre_f + suf_l[...] * suf_f)
        dattn[...] = unstack_heads(out).astype(BF16)

    def sum_for_partner():
        zsend[...] = (
            rsend[y, 1 - zh].astype(F32)
            + rrecv[0, 1 - zh].astype(F32)
            + rrecv[1, 1 - zh].astype(F32)
            + rrecv[2, 1 - zh].astype(F32)
        ).astype(BF16)

    def on_mid(f, *args):
        @pl.when(mid)
        def _():
            f(*args)

    def own_mid():
        own[2] = dot(attn[...], wv[2])
        own[3] = dot(attn[...], wv[3])

    def on_edge(f, *args):
        @pl.when(edge)
        def _():
            f(*args)

    def share_arrived(w):
        share_copy(w).wait_recv()
        start(gather_fast(w))

    def fast_done(w):
        fast_all(w).wait()
        start(gather_slow(w))

    def slow_done(w):
        slow_all(w).wait()
        start(gather_core(w))

    def firsts(j):
        for i in (2 * j, 2 * j + 1):
            if i < NCH + EX:
                first(i)

    def on_mid_core(i, f, *args):
        @pl.when(mid & (c == i))
        def _():
            f(*args)

    def own_far():
        own[2] = dot(attn[...], wv[2])

    def own_near():
        own[3] = dot(attn[...], wv[3])

    def rows_out(lo, hi):
        for q in range(lo, hi):
            rows_copy(q).start()

    def sent_early():
        remote(outP, inP, outPs.at[0], inPr.at[0], mid_same).wait_send()
        remote(outS, outS, outSs.at[0], inPr.at[0], mid_same).wait_send()

    def edge_finals():
        for j in range(NCH // 2):
            edge_final(j)

    def mid_first_finals():
        for j in range(NCH // 2, (NCH + EX) // 2):
            mid_final_first(j)

    own_head()
    on_edge(firsts, 0)
    on_edge(lambda: share_copy(1).start())
    own_rest()
    on_edge(firsts, 1)
    on_mid(share_arrived, 0)
    on_mid_core(0, start, px)
    own_part(1)
    z1.wait()
    start(y1)
    on_edge(firsts, 2)
    suffix()
    slabs[2].wait()
    slabs[3].wait()
    on_mid(firsts, 0)
    own_far()
    on_mid(share_arrived, 1)
    on_mid_core(0, fast_done, 0)
    on_edge(firsts, 3)
    on_mid(own_near)
    on_mid(firsts, 1)
    px_all().wait()
    core.start()
    y1_all().wait()
    prefix_begin()
    on_mid(firsts, 2)
    seconds(0)
    on_mid_core(1, fast_done, 0)
    core.wait()
    on_edge(firsts, 4)
    prefix_part(0, 4)
    on_mid(firsts, 3)
    prefix_part(4, 8)
    prefix_end()
    start(y2)
    on_edge(firsts, 5)
    on_edge(firsts, 6)
    on_edge(rows_out, 0, 2)
    on_mid(firsts, 4)
    seconds(1)
    on_mid_core(0, slow_done, 0)
    on_mid_core(0, fast_done, 1)
    seconds(2)
    on_mid(firsts, 5)
    on_mid_core(1, slow_done, 0)
    on_mid_core(1, fast_done, 1)
    on_mid(firsts, 6)
    y2_all().wait()
    sum_for_partner()
    z2.start()
    on_edge(rows_out, 2, 6)
    seconds(3)
    on_mid(lambda: wait(gather_core(0)))
    quarter(0)
    quarter(1)
    seconds(4)
    quarter(2)
    quarter(3)
    z2.wait()
    merge()
    decode_out(0)
    decode_out(2)
    decode_out(3)
    on_edge(rows_out, 6, 8)
    quarter(4)
    on_mid_core(0, slow_done, 1)
    decode_out(1)
    quarter(5)
    on_mid_core(1, slow_done, 1)
    on_mid(decode_across, 0)
    on_mid(decode_across, 2)
    quarter(6)
    on_mid(sent_early)
    quarter(7)
    on_edge(edge_finals)
    on_mid(lambda: wait(gather_core(1)))
    on_mid(far_part)
    on_mid(mid_first_finals)
    for q in range(NQ - 1):
        mid_final(q)
    decode_final()
    mid_final(NQ - 1)

    @pl.when(edge)
    def _():
        share_copy(0).wait_send()
        share_copy(1).wait_send()
        remote(outP, inP, outPs.at[0], inPr.at[0], mid_same).wait_send()
        remote(attn, far_attn, outAs.at[0], inAr.at[0], mid_same).wait_send()

    @pl.when(mid)
    def _():
        remote(outQ, inQ, outQs.at[0], inQr.at[0], mid_other).wait_send()

    three = pl.ds(0, 3)
    remote(down_out.at[three], down_in.at[three], downs.at[0], downr.at[0], mid_same).wait_send()


def local(
    decode_query, new_kv, sample_order, suffix_len, suffix_kv, prefix_kv, prefix_len,
    prefill_query, prefill_kv, prefill_segment, out_weight,
):
    vmem = pl.BlockSpec(memory_space=pltpu.VMEM)
    smem = pl.BlockSpec(memory_space=pltpu.SMEM)
    hbm = pl.BlockSpec(memory_space=pl.ANY)
    dma = pltpu.SemaphoreType.DMA

    def ring(*lead):
        return pltpu.VMEM(lead + (256, CH), BF16)

    def dring(*lead):
        return pltpu.VMEM(lead + (SAMPLES, SHARD), BF16)

    return pl.pallas_call(
        kernel,
        out_shape=(pltpu.VMEM((SAMPLES, SHARD), BF16), pltpu.VMEM((256, SHARD), BF16)),
        in_specs=[smem] * 3 + [hbm] * 8,
        out_specs=(vmem, vmem),
        scratch_shapes=[
            pltpu.VMEM((4, 1024, SHARD), BF16),
            pltpu.VMEM(decode_query.shape, BF16),
            pltpu.VMEM(new_kv.shape, BF16),
            pltpu.VMEM(prefill_kv.shape, BF16),
            pltpu.VMEM(prefill_segment.shape, jnp.int32),
            pltpu.VMEM((256, 1024), BF16),
            pltpu.VMEM((SAMPLES, 2, 128, 128), BF16),
            pltpu.VMEM((2, 4, KVROWS, HD), BF16),
            pltpu.VMEM((4, 2, SAMPLES, MSG), BF16),
            pltpu.VMEM((4, 2, SAMPLES, MSG), BF16),
            pltpu.VMEM((3, 2, SAMPLES, MSG), BF16),
            pltpu.VMEM((SAMPLES, MSG), BF16),
            pltpu.VMEM((SAMPLES, MSG), BF16),
            pltpu.VMEM((256, 1024), BF16),
            pltpu.VMEM((SAMPLES, 1024), BF16),
            pltpu.VMEM((4, 256, SHARD), F32),
            pltpu.VMEM((4, SAMPLES, SHARD), F32),
            pltpu.VMEM((256, 256), F32),
            pltpu.VMEM((128, 1024), BF16),
            pltpu.VMEM((128, MSG), BF16),
            pltpu.VMEM((128, 128), F32),
            pltpu.VMEM((128, 128), F32),
            pltpu.VMEM((128, 128), F32),
            pltpu.VMEM((2, 4, 4, WR, FAR), BF16),
            pltpu.VMEM((2, 4, 4, WR, SHARD), BF16),
            pltpu.VMEM((256, 1024), BF16),
            ring(NCH + EX), ring(NCH + EX), ring(NCH), ring(NCH + EX),
            pltpu.VMEM((NQ, QT, FAR), BF16),
            pltpu.VMEM((NQ, QT, FAR), BF16),
            dring(4), dring(5),
            dma((12,)), dma((1,)), dma((1,)), dma((1,)), dma((1,)), dma((1,)), dma((1,)), dma((3,)), dma((3,)),
            dma((2,)), dma((2,)), dma((2,)), dma((2,)), dma((2,)), dma((2,)), dma((2,)), dma((2,)),
            dma((1,)), dma((NCH + EX,)), dma((1,)), dma(((NCH + EX) // 2,)), dma((1,)), dma((NQ,)), dma((1,)), dma((NQ,)),
            dma((1,)), dma((5,)),
        ],
        compiler_params=pltpu.CompilerParams(
            collective_id=0, has_side_effects=True, vmem_limit_bytes=60 << 20
        ),
    )(
        sample_order, suffix_len, prefix_len, decode_query, new_kv, prefill_kv, prefill_segment,
        prefill_query, suffix_kv, prefix_kv, out_weight,
    )


def solution(mesh):
    return jax.shard_map(
        local,
        mesh=mesh,
        in_specs=(
            P("dp", "head"),
            P("dp", None, "head"),
            P("dp"),
            P("dp"),
            P("dp", None, None, "head"),
            P("dp", None, None, "head"),
            P("dp"),
            P("dp", "head"),
            P("dp", None, "head"),
            P("dp", None),
            P("head", None),
        ),
        out_specs=(P("dp", "head"), P("dp", "head")),
        check_vma=False,
    )
```

```python
import math

import jax
import jax.numpy as jnp
from jax import lax
from jax.experimental import pallas as pl
from jax.experimental.pallas import tpu as pltpu
from jax.sharding import PartitionSpec as P

MESH = pl.DeviceIdType.MESH
HD = 128
SAMPLES = 16
GROUP = 8
FLOOR = -1e30
SCALE = 1.0 / math.sqrt(HD)
PX = 384
MSG = 1024 + 128
KVROWS = 2 * PX + 16
CH = 128
NCH = 10
SHARD = CH * NCH
QT = 32
NQ = 8
EX = 2
FAR = SHARD - EX * CH
WR = 32
F32 = jnp.float32
BF16 = jnp.bfloat16


def dot(a, b):
    return jnp.dot(a, b, preferred_element_type=F32)


def dot_t(a, b):
    return lax.dot_general(a, b, (((1,), (1,)), ((), ())), preferred_element_type=F32)


def stack_heads(rows):
    return jnp.concatenate([rows[:, HD * h : HD * (h + 1)] for h in range(GROUP)], axis=0)


def unstack_heads(rows):
    return jnp.concatenate([rows[SAMPLES * h : SAMPLES * (h + 1)] for h in range(GROUP)], axis=1)


def kernel(
    so_ref, sl_ref, pfl_ref, dq_hbm, nkv_hbm, pkv_hbm, seg_hbm, pq_hbm, skv_hbm, pre_hbm, w_hbm,
    dout_ref, pout_ref,
    wv, dq_ref, nkv_ref, pkv_ref, seg_ref, pq, skv, pall, qall, rsend, rrecv, zsend, zrecv,
    attn, dattn, own, down, bias, qsel, osel, suf_o, suf_m, suf_l,
    wx_far, wx_near, far_attn, outP, inP, outS, inS, outQ, inQ, down_out, down_in, far_dattn, head_out, head_in,
    half_sem, lsem, xs, xr, ys, yr, y2s, y2r, ms, mr,
    shs, shr, gfs, gfr, gss, gsr, gcs, gcr,
    outPs, inPr, outSs, inSr, outAs, inAr, outQs, inQr, downs, downr,
):
    wx = (wx_far, wx_near)
    d = lax.axis_index("dp")
    k = lax.axis_index("head")
    c = lax.rem(d, 2)
    x = lax.rem(d // 2, 4)
    zh = lax.rem(d // 8, 2)
    y = d // 16
    a = d // 8

    def dev(y_, zh_, x_, c_):
        return (((y_ * 2 + zh_) * 4 + x_) * 2 + c_, k)

    sibling = dev(y, zh, x, 1 - c)
    partner = dev(y, 1 - zh, x, c)
    xpeer = [dev(y, zh, lax.rem(x + i, 4), c) for i in (1, 2, 3)]
    ypeer = [dev(lax.rem(y + i, 4), zh, x, c) for i in (1, 2, 3)]

    bar = pltpu.get_barrier_semaphore()
    for peer in [sibling] + xpeer + ypeer:
        pl.semaphore_signal(bar, inc=1, device_id=peer, device_id_type=MESH)

    @pl.when(zh == 0)
    def _():
        pl.semaphore_signal(bar, inc=1, device_id=partner, device_id_type=MESH)


    for i in (1, 2, 3):
        pl.semaphore_signal(bar, inc=1, device_id=(d, lax.rem(k + i, 4)), device_id_type=MESH)

    loads = [
        pltpu.make_async_copy(pq_hbm, pq, lsem.at[0]),
        pltpu.make_async_copy(pre_hbm.at[0, 0], pall.at[c, x, pl.ds(0, PX)], lsem.at[1]),
        pltpu.make_async_copy(pre_hbm.at[0, 1], pall.at[c, x, pl.ds(PX, PX)], lsem.at[2]),
        pltpu.make_async_copy(skv_hbm, skv, lsem.at[3]),
    ]
    side = k // 2
    near = 1 + side
    far = 2 - side
    role_dest = [jnp.where(side == 0, 3, 0), 3 * side, far, near]

    def slab(dest):
        return pl.ds(pl.multiple_of(dest * SHARD, SHARD), SHARD)

    slabs = [
        pltpu.make_async_copy(w_hbm.at[:, slab(role_dest[i])], wv.at[i], lsem.at[4 + i]) for i in range(4)
    ]
    small = [
        pltpu.make_async_copy(dq_hbm, dq_ref, lsem.at[8]),
        pltpu.make_async_copy(pkv_hbm, pkv_ref, lsem.at[9]),
        pltpu.make_async_copy(seg_hbm, seg_ref, lsem.at[10]),
        pltpu.make_async_copy(nkv_hbm, nkv_ref, lsem.at[11]),
    ]
    for load in small + [loads[0], loads[1], loads[2], slabs[0], loads[3]] + slabs[1:]:
        load.start()

    pl.semaphore_wait(bar, 10 + zh)

    @pl.when(zh == 1)
    def _():
        pl.semaphore_signal(half_sem, inc=1, device_id=partner, device_id_type=MESH)


    def remote(src, dst, ss, rs, target):
        return pltpu.make_async_remote_copy(
            src_ref=src, dst_ref=dst, send_sem=ss, recv_sem=rs, device_id=target, device_id_type=MESH
        )

    edge = (k == 0) | (k == 3)
    mid = (k == 1) | (k == 2)
    mid_same = (d, 1 + side)
    mid_other = (d, 2 - side)
    edge_same = (d, 3 * side)

    def chunk(j):
        return pl.ds(pl.multiple_of(j * CH, CH), CH)

    def rows_of(q):
        return pl.ds(pl.multiple_of(q * QT, QT), QT)

    fast = jnp.where(c == 0, x, y)
    slow = jnp.where(c == 0, y, x)
    share = c * 16 + slow * 4 + fast

    def share_copy(w):
        rows = pl.ds(pl.multiple_of(share * WR, WR), WR)
        if w == 0:
            cols = pl.ds(pl.multiple_of(far * SHARD + EX * CH, CH), FAR)
        else:
            cols = slab(near)
        return remote(w_hbm.at[rows, cols], wx[w].at[c, slow, fast], shs.at[w], shr.at[w], mid_same)

    def line_peer(i, fast_axis):
        along_x = (c == 0) if fast_axis else (c == 1)
        return (jnp.where(along_x, xpeer[i][0], ypeer[i][0]), k)

    z1 = remote(qall.at[y, zh], qall.at[y, zh], ms.at[0], mr.at[0], partner)

    @pl.when(edge)
    def _():
        share_copy(0).start()

    lane = lax.broadcasted_iota(jnp.int32, (SAMPLES, 128), 1)
    row = lax.broadcasted_iota(jnp.int32, (SAMPLES, 128), 0)
    extra = jnp.zeros((SAMPLES, 128), jnp.int32)
    for r in range(SAMPLES):
        number = so_ref[r]
        part = jnp.where(lane == 0, number >> 4, jnp.where(lane == 1, number & 15, 0))
        extra = jnp.where(row == r, part, extra)
    small[0].wait()
    qall[y, zh, :, 0:1024] = dq_ref[...]
    qall[y, zh, :, 1024:MSG] = extra.astype(F32).astype(BF16)
    length = pfl_ref[0]
    pall[c, x, 2 * PX : KVROWS, :] = (
        jnp.where(row == 0, length >> 4, jnp.where(row == 1, length & 15, 0)).astype(F32).astype(BF16)
    )


    @pl.when(zh == 1)
    def _():
        z1.start()

    loads[1].wait()
    loads[2].wait()
    px = [
        remote(pall.at[c, x], pall.at[c, x], xs.at[0], xr.at[0], xpeer[i]) for i in range(3)
    ]

    @pl.when(edge | (c == 1))
    def _():
        for copy in px:
            copy.start()


    small[1].wait()
    small[2].wait()
    small[3].wait()
    qpos = lax.broadcasted_iota(jnp.int32, (256, 256), 0)
    kpos = lax.broadcasted_iota(jnp.int32, (256, 256), 1)
    seg_row = jnp.broadcast_to(seg_ref[...].astype(F32), (256, 256))
    seg_col = jnp.sum(jnp.where(qpos == kpos, seg_row, 0.0), axis=1, keepdims=True)
    bias[...] = jnp.where((kpos <= qpos) & (seg_row == seg_col), 0.0, FLOOR)
    keys = pkv_ref[:, 0, :]
    values = pkv_ref[:, 1, :]
    loads[0].wait()

    def one_head(h, _):
        cols = pl.ds(pl.multiple_of(h * HD, HD), HD)
        s = dot_t(pq[:, cols], keys) * SCALE + bias[...]
        top = jnp.max(s, axis=1, keepdims=True)
        w = jnp.exp(s - top)
        total = jnp.sum(w, axis=1, keepdims=True)
        attn[:, cols] = (dot(w.astype(BF16), values) / total).astype(BF16)
        return 0

    lax.fori_loop(0, GROUP, one_head, 0, unroll=True)

    def gather_fast(w):
        return [
            remote(wx[w].at[c, slow, fast], wx[w].at[c, slow, fast], gfs.at[w], gfr.at[w], line_peer(i, True))
            for i in range(3)
        ]

    def gather_slow(w):
        return [
            remote(wx[w].at[c, slow], wx[w].at[c, slow], gss.at[w], gsr.at[w], line_peer(i, False))
            for i in range(3)
        ]

    def gather_core(w):
        return [remote(wx[w].at[c], wx[w].at[c], gcs.at[w], gcr.at[w], sibling)]

    def fast_all(w):
        three = wx[w].at[c, slow, pl.ds(0, 3)]
        return remote(three, three, gfs.at[w], gfr.at[w], line_peer(0, True))

    def slow_all(w):
        three = wx[w].at[c, pl.ds(0, 3)]
        return remote(three, three, gss.at[w], gsr.at[w], line_peer(0, False))

    def px_all():
        three = pall.at[c, pl.ds(0, 3)]
        return remote(three, three, xs.at[0], xr.at[0], xpeer[0])

    def y1_all():
        three = qall.at[pl.ds(0, 3)]
        return remote(three, three, ys.at[0], yr.at[0], ypeer[0])

    def y2_all():
        return remote(rsend.at[pl.ds(0, 3)], rrecv, y2s.at[0], y2r.at[0], ypeer[0])

    def start(copies):
        for copy in copies:
            copy.start()

    def wait(copies):
        for copy in copies:
            copy.wait()

    def edge_copy(j):
        return remote(outP.at[j], inP.at[j], outPs.at[0], inPr.at[j], mid_same)

    def rows_copy(q):
        return remote(attn.at[rows_of(q)], far_attn.at[rows_of(q)], outAs.at[0], inAr.at[q], mid_same)

    def mid_copy(j):
        return remote(outP.at[j], inS.at[j], outPs.at[0], inSr.at[j // 2], mid_other)

    def back_copy(j):
        return remote(outS.at[j], inS.at[j], outSs.at[0], inSr.at[j // 2], edge_same)

    def cross_copy(q):
        return remote(outQ.at[q], inQ.at[q], outQs.at[0], inQr.at[q], mid_other)

    def own_part(i):
        slabs[i].wait()
        own[i] = dot(attn[...], wv[i])

    def own_head():
        slabs[0].wait()
        own[0, :, 0 : 2 * CH] = dot(attn[...], wv[0, :, 0 : 2 * CH])

    def own_rest():
        own[0, :, 2 * CH : SHARD] = dot(attn[...], wv[0, :, 2 * CH : SHARD])

    def own_first(j):
        return own[0, :, chunk(j)] if j < NCH else own[2, :, chunk(j - NCH)]

    def first(j):
        @pl.when(mid)
        def _():
            edge_copy(j).wait_recv()
            outP[j] = (own_first(j) + inP[j].astype(F32)).astype(BF16)
            mid_copy(j).start()

        @pl.when(edge)
        def _():
            outP[j] = own_first(j).astype(BF16)
            edge_copy(j).start()

    def pair_in(j):
        two = pl.ds(2 * j, min(2, NCH + EX - 2 * j))
        return remote(outP.at[two], inS.at[two], outPs.at[0], inSr.at[j], mid_other)

    def seconds(j):
        @pl.when(mid)
        def _():
            pair_in(j).wait_recv()
            for i in (2 * j, 2 * j + 1):
                outS[i] = (own[1, :, chunk(i)] + inS[i].astype(F32)).astype(BF16)
                back_copy(i).start()

    def quarter(q):
        @pl.when(mid)
        def _():
            rows_copy(q).wait_recv()
            part = dot(far_attn[rows_of(q), :], wx_far[...].reshape(1024, FAR))
            outQ[q] = (own[2, rows_of(q), EX * CH : SHARD] + part).astype(BF16)
            cross_copy(q).start()

    def far_part():
        own[3] += dot(far_attn[...], wx_near[...].reshape(1024, SHARD))

    far_cols = pl.ds(EX * CH, FAR)

    def quarter_home(q):
        return pltpu.make_async_copy(
            pout_ref.at[rows_of(q), far_cols], pout_hbm.at[rows_of(q), far_cols], osem.at[q]
        )

    def first_home():
        cols = pl.ds(0, EX * CH)
        return pltpu.make_async_copy(pout_ref.at[:, cols], pout_hbm.at[:, cols], osem.at[NQ])

    def all_home():
        return pltpu.make_async_copy(pout_ref, pout_hbm, osem.at[NQ + 1])

    def decode_home():
        return pltpu.make_async_copy(dout_ref, dout_hbm, osem.at[NQ + 2])

    def mid_final(q):
        @pl.when(mid)
        def _():
            cross_copy(q).wait_recv()
            cols = slice(EX * CH, SHARD)
            pout_ref[rows_of(q), cols] = (own[3, rows_of(q), cols] + inQ[q].astype(F32)).astype(BF16)

    def mid_final_first(j):
        pair_in(j).wait_recv()
        for i in range(2 * j, min(2 * j + 2, NCH + EX)):
            cols = chunk(i - NCH)
            pout_ref[:, cols] = (own[3, :, cols] + inS[i].astype(F32)).astype(BF16)

    def edge_final(j):
        pair_in(j).wait_recv()
        for i in (2 * j, 2 * j + 1):
            pout_ref[:, chunk(i)] = (own[1, :, chunk(i)] + inS[i].astype(F32)).astype(BF16)

    def row_copy(i, slot, target):
        return remote(down_out.at[i], down_in.at[slot], downs.at[i], downr.at[slot], target)

    def row_from_edge():
        return row_copy(0, 0, mid_same)

    def row_to_edge():
        return row_copy(1, 3, edge_same)

    def row_across(i):
        return row_copy(i, 4, (d, role_dest[i]))

    def dattn_copy():
        return remote(dattn, far_dattn, downs.at[3], downr.at[1], mid_same)

    def head_copy():
        return remote(head_out, head_in, downs.at[4], downr.at[2], mid_same)

    def decode_out_edge():
        down_out[0] = dot(dattn[...], wv[0]).astype(BF16)
        row_from_edge().start()
        dattn_copy().start()
        head_out[...] = dot(dattn[...], wv[2, :, 0 : EX * CH]).astype(BF16)
        head_copy().start()
        down[1] = dot(dattn[...], wv[1])

    def decode_own(i):
        @pl.when(mid)
        def _():
            down[i] = dot(dattn[...], wv[i])

    def decode_to_edge():
        down_out[1] = dot(dattn[...], wv[1]).astype(BF16)
        row_to_edge().start()

    def decode_across():
        row_from_edge().wait_recv()
        down_out[0] = (down[0] + down_in[0].astype(F32)).astype(BF16)
        row_across(0).start()
        dattn_copy().wait_recv()
        down[2, :, EX * CH : SHARD] += dot(far_dattn[...], wx_far[...].reshape(1024, FAR))
        head_copy().wait_recv()
        down[2, :, 0 : EX * CH] += head_in[...].astype(F32)
        down_out[2] = down[2].astype(BF16)
        row_across(2).start()

    def decode_near():
        down[3] += dot(far_dattn[...], wx_near[...].reshape(1024, SHARD))

    def decode_final():
        @pl.when(mid)
        def _():
            row_across(2).wait_recv()
            dout_ref[...] = (down[3] + down_in[4].astype(F32)).astype(BF16)

        @pl.when(edge)
        def _():
            row_to_edge().wait_recv()
            row_across(0).wait_recv()
            dout_ref[...] = (down[1] + down_in[3].astype(F32) + down_in[4].astype(F32)).astype(BF16)

    rmod = lax.rem(lax.broadcasted_iota(jnp.int32, (128, 128), 0), SAMPLES)
    lane128 = lax.broadcasted_iota(jnp.int32, (128, 128), 1)

    def suffix():
        loads[3].wait()
        qs = stack_heads(dq_ref[...])
        scores = jnp.zeros((128, 128), F32)
        lens = jnp.zeros((128, 128), jnp.int32)
        for r in range(SAMPLES):
            scores = jnp.where(rmod == r, dot_t(qs, skv[r, 0]), scores)
            lens = jnp.where(rmod == r, sl_ref[r], lens)
        live = lane128 < lens
        scores = jnp.where(live, scores * SCALE, FLOOR)
        new_k = jnp.concatenate([nkv_ref[:, 0, :].astype(F32)] * GROUP, axis=0)
        new_v = jnp.concatenate([nkv_ref[:, 1, :].astype(F32)] * GROUP, axis=0)
        new_score = jnp.sum(qs.astype(F32) * new_k, axis=1, keepdims=True) * SCALE
        top = jnp.maximum(jnp.max(scores, axis=1, keepdims=True), new_score)
        w = jnp.where(live, jnp.exp(scores - top), 0.0)
        new_w = jnp.exp(new_score - top)
        acc = new_w.astype(BF16).astype(F32) * new_v
        for r in range(SAMPLES):
            acc = acc + dot(jnp.where(rmod == r, w, 0.0).astype(BF16), skv[r, 1])
        suf_o[...] = acc
        suf_m[...] = jnp.broadcast_to(top, (128, 128))
        suf_l[...] = jnp.broadcast_to(jnp.sum(w, axis=1, keepdims=True) + new_w, (128, 128))

    y1 = [remote(qall.at[y], qall.at[y], ys.at[0], yr.at[0], ypeer[i]) for i in range(3)]
    core = remote(pall.at[c], pall.at[c], ms.at[1], mr.at[1], sibling)
    y2 = [
        remote(rsend.at[lax.rem(y + i + 1, 4)], rrecv.at[i], y2s.at[0], y2r.at[0], ypeer[i])
        for i in range(3)
    ]
    z2 = remote(zsend, zrecv, ms.at[2], mr.at[2], partner)

    def to_slots():
        tags = qall[:, :, :, 1024:MSG].reshape(128, 128).astype(F32)
        number = tags[:, 0:1] * 16.0 + tags[:, 1:2] - (a * 128).astype(F32)
        return jnp.where(number == lane128.astype(F32), 1.0, 0.0)

    def prefix_begin():
        rows = qall[:, :, :, 0:1024].reshape(128, 1024)
        qsel[...] = dot(to_slots().T.astype(BF16), rows).astype(BF16)

    def prefix_part(lo, hi):
        head128 = lax.broadcasted_iota(jnp.int32, (128, 128), 0) // SAMPLES

        def one_prompt(j, _):
            slot = pl.ds(pl.multiple_of(j * SAMPLES, SAMPLES), SAMPLES)
            jc, jx = lax.rem(j, 2), j // 2
            q = stack_heads(qsel[slot, :])
            k_ = pall[jc, jx, 0:PX, :]
            v_ = pall[jc, jx, PX : 2 * PX, :]
            tail = pall[jc, jx, 2 * PX : KVROWS, :].astype(F32)
            n = tail[0:1, :] * 16.0 + tail[1:2, :]
            n = jnp.concatenate([n] * 3, axis=1)
            pos = lax.broadcasted_iota(jnp.int32, (1, PX), 1).astype(F32)
            s = dot_t(q, k_) * SCALE + jnp.where(pos < n, 0.0, FLOOR)
            top = jnp.max(s, axis=1, keepdims=True)
            w = jnp.exp(s - top)
            total = jnp.sum(w, axis=1, keepdims=True)
            o = dot(w.astype(BF16), v_) / total
            osel[slot, 0:1024] = unstack_heads(o).astype(BF16)
            stat = jnp.where(lane128 == head128, top, jnp.where(lane128 == head128 + GROUP, total, 0.0))
            stat = sum(stat[SAMPLES * h : SAMPLES * (h + 1)] for h in range(GROUP))
            hi_ = stat.astype(BF16).astype(F32)
            mid_ = (stat - hi_).astype(BF16).astype(F32)
            lo_ = (stat - hi_ - mid_).astype(BF16).astype(F32)
            packed = hi_ + pltpu.roll(mid_, 16, 1) + pltpu.roll(lo_, 32, 1)
            osel[slot, 1024:MSG] = packed.astype(BF16)
            return 0

        lax.fori_loop(lo, hi, one_prompt, 0, unroll=True)

    def prefix_end():
        back = dot(to_slots().astype(BF16), osel[...]).astype(BF16)
        rsend[...] = back.reshape(4, 2, SAMPLES, MSG)

    def merge():
        got = (
            rsend[y, zh].astype(F32)
            + rrecv[0, zh].astype(F32)
            + rrecv[1, zh].astype(F32)
            + rrecv[2, zh].astype(F32)
            + zrecv[...].astype(F32)
        )
        tag = got[:, 1024:MSG]
        stat = tag + pltpu.roll(tag, 128 - 16, 1) + pltpu.roll(tag, 128 - 32, 1)
        pre_m = jnp.concatenate([stat[:, h : h + 1] for h in range(GROUP)], axis=0)
        pre_l = jnp.concatenate([stat[:, GROUP + h : GROUP + h + 1] for h in range(GROUP)], axis=0)
        pre_o = stack_heads(got[:, 0:1024])
        m = suf_m[...]
        top = jnp.maximum(m, pre_m)
        pre_f = jnp.exp(pre_m - top) * pre_l
        suf_f = jnp.exp(m - top)
        out = (pre_o * pre_f + suf_o[...] * suf_f) / (pre_f + suf_l[...] * suf_f)
        dattn[...] = unstack_heads(out).astype(BF16)

    def sum_for_partner():
        zsend[...] = (
            rsend[y, 1 - zh].astype(F32)
            + rrecv[0, 1 - zh].astype(F32)
            + rrecv[1, 1 - zh].astype(F32)
            + rrecv[2, 1 - zh].astype(F32)
        ).astype(BF16)

    def on_mid(f, *args):
        @pl.when(mid)
        def _():
            f(*args)

    def own_mid():
        own[2] = dot(attn[...], wv[2])
        own[3] = dot(attn[...], wv[3])

    def on_edge(f, *args):
        @pl.when(edge)
        def _():
            f(*args)

    def share_arrived(w):
        share_copy(w).wait_recv()
        start(gather_fast(w))

    def fast_done(w):
        fast_all(w).wait()
        start(gather_slow(w))

    def slow_done(w):
        slow_all(w).wait()
        start(gather_core(w))

    def firsts(j):
        for i in (2 * j, 2 * j + 1):
            if i < NCH + EX:
                first(i)

    def on_mid_core(i, f, *args):
        @pl.when(mid & (c == i))
        def _():
            f(*args)

    def own_far():
        own[2] = dot(attn[...], wv[2])

    def own_near():
        own[3] = dot(attn[...], wv[3])

    def rows_out(lo, hi):
        for q in range(lo, hi):
            rows_copy(q).start()

    def sent_early():
        remote(outP, inP, outPs.at[0], inPr.at[0], mid_same).wait_send()
        remote(outS, outS, outSs.at[0], inPr.at[0], mid_same).wait_send()

    def edge_finals():
        for j in range(NCH // 2):
            edge_final(j)

    def mid_first_finals():
        for j in range(NCH // 2, (NCH + EX + 1) // 2):
            mid_final_first(j)

    def queries_out():
        @pl.when(zh == 0)
        def _():
            pl.semaphore_wait(half_sem, 1)
            z1.start()

    own_head()
    on_edge(firsts, 0)
    on_edge(lambda: share_copy(1).start())
    own_rest()
    on_mid(share_arrived, 0)
    on_mid_core(0, start, px)
    own_part(1)
    queries_out()
    on_edge(firsts, 1)
    on_edge(firsts, 2)
    on_edge(firsts, 3)
    suffix()
    slabs[2].wait()
    slabs[3].wait()
    on_mid(firsts, 0)
    own_far()
    z1.wait()
    start(y1)
    on_edge(firsts, 4)
    on_mid(share_arrived, 1)
    on_mid_core(0, fast_done, 0)
    on_edge(firsts, 5)
    on_mid(own_near)
    on_mid(firsts, 1)
    px_all().wait()
    core.start()
    on_mid_core(1, fast_done, 0)
    y1_all().wait()
    prefix_begin()
    on_mid(firsts, 2)
    seconds(0)
    core.wait()
    prefix_part(0, 4)
    on_mid(firsts, 3)
    prefix_part(4, 8)
    prefix_end()
    start(y2)
    on_edge(rows_out, 0, 2)
    on_mid(firsts, 4)
    seconds(1)
    on_mid_core(0, slow_done, 0)
    on_mid_core(0, fast_done, 1)
    seconds(2)
    on_mid_core(1, slow_done, 0)
    on_mid_core(1, fast_done, 1)
    on_mid(firsts, 5)
    y2_all().wait()
    sum_for_partner()
    z2.start()
    on_edge(rows_out, 2, 6)
    seconds(3)
    on_mid(lambda: wait(gather_core(0)))
    quarter(0)
    quarter(1)
    seconds(4)
    quarter(2)
    quarter(3)
    quarter(4)
    on_mid_core(0, slow_done, 1)
    on_mid_core(1, slow_done, 1)
    z2.wait()
    merge()
    on_edge(decode_out_edge)
    on_edge(rows_out, 6, 8)
    decode_own(0)
    quarter(5)
    decode_own(2)
    on_mid(decode_to_edge)
    decode_own(3)
    on_mid(decode_across)
    quarter(6)
    on_mid(sent_early)
    quarter(7)
    on_edge(edge_finals)
    on_mid(lambda: wait(gather_core(1)))
    on_mid(far_part)
    on_mid(decode_near)
    on_mid(mid_first_finals)
    for q in range(NQ - 1):
        mid_final(q)
    decode_final()
    mid_final(NQ - 1)

    @pl.when(edge)
    def _():
        share_copy(0).wait_send()
        share_copy(1).wait_send()
        remote(outP, inP, outPs.at[0], inPr.at[0], mid_same).wait_send()
        remote(attn, far_attn, outAs.at[0], inAr.at[0], mid_same).wait_send()
        row_from_edge().wait_send()
        dattn_copy().wait_send()
        head_copy().wait_send()

    @pl.when(mid)
    def _():
        remote(outQ, inQ, outQs.at[0], inQr.at[0], mid_other).wait_send()
        row_to_edge().wait_send()
        row_across(0).wait_send()
        row_across(2).wait_send()


def local(
    decode_query, new_kv, sample_order, suffix_len, suffix_kv, prefix_kv, prefix_len,
    prefill_query, prefill_kv, prefill_segment, out_weight,
):
    vmem = pl.BlockSpec(memory_space=pltpu.VMEM)
    smem = pl.BlockSpec(memory_space=pltpu.SMEM)
    hbm = pl.BlockSpec(memory_space=pl.ANY)
    dma = pltpu.SemaphoreType.DMA

    def ring(*lead):
        return pltpu.VMEM(lead + (256, CH), BF16)

    def dring(*lead):
        return pltpu.VMEM(lead + (SAMPLES, SHARD), BF16)

    return pl.pallas_call(
        kernel,
        out_shape=(pltpu.VMEM((SAMPLES, SHARD), BF16), pltpu.VMEM((256, SHARD), BF16)),
        in_specs=[smem] * 3 + [hbm] * 8,
        out_specs=(vmem, vmem),
        scratch_shapes=[
            pltpu.VMEM((4, 1024, SHARD), BF16),
            pltpu.VMEM(decode_query.shape, BF16),
            pltpu.VMEM(new_kv.shape, BF16),
            pltpu.VMEM(prefill_kv.shape, BF16),
            pltpu.VMEM(prefill_segment.shape, jnp.int32),
            pltpu.VMEM((256, 1024), BF16),
            pltpu.VMEM((SAMPLES, 2, 128, 128), BF16),
            pltpu.VMEM((2, 4, KVROWS, HD), BF16),
            pltpu.VMEM((4, 2, SAMPLES, MSG), BF16),
            pltpu.VMEM((4, 2, SAMPLES, MSG), BF16),
            pltpu.VMEM((3, 2, SAMPLES, MSG), BF16),
            pltpu.VMEM((SAMPLES, MSG), BF16),
            pltpu.VMEM((SAMPLES, MSG), BF16),
            pltpu.VMEM((256, 1024), BF16),
            pltpu.VMEM((SAMPLES, 1024), BF16),
            pltpu.VMEM((4, 256, SHARD), F32),
            pltpu.VMEM((4, SAMPLES, SHARD), F32),
            pltpu.VMEM((256, 256), F32),
            pltpu.VMEM((128, 1024), BF16),
            pltpu.VMEM((128, MSG), BF16),
            pltpu.VMEM((128, 128), F32),
            pltpu.VMEM((128, 128), F32),
            pltpu.VMEM((128, 128), F32),
            pltpu.VMEM((2, 4, 4, WR, FAR), BF16),
            pltpu.VMEM((2, 4, 4, WR, SHARD), BF16),
            pltpu.VMEM((256, 1024), BF16),
            ring(NCH + EX), ring(NCH + EX), ring(NCH), ring(NCH + EX),
            pltpu.VMEM((NQ, QT, FAR), BF16),
            pltpu.VMEM((NQ, QT, FAR), BF16),
            dring(3), dring(5),
            pltpu.VMEM((SAMPLES, 1024), BF16),
            pltpu.VMEM((SAMPLES, EX * CH), BF16),
            pltpu.VMEM((SAMPLES, EX * CH), BF16),
            pltpu.SemaphoreType.REGULAR,
            dma((12,)), dma((1,)), dma((1,)), dma((1,)), dma((1,)), dma((1,)), dma((1,)), dma((3,)), dma((3,)),
            dma((2,)), dma((2,)), dma((2,)), dma((2,)), dma((2,)), dma((2,)), dma((2,)), dma((2,)),
            dma((1,)), dma((NCH + EX,)), dma((1,)), dma(((NCH + EX + 1) // 2,)), dma((1,)), dma((NQ,)), dma((1,)), dma((NQ,)),
            dma((5,)), dma((5,)),
        ],
        compiler_params=pltpu.CompilerParams(
            collective_id=0, has_side_effects=True, vmem_limit_bytes=60 << 20
        ),
    )(
        sample_order, suffix_len, prefix_len, decode_query, new_kv, prefill_kv, prefill_segment,
        prefill_query, suffix_kv, prefix_kv, out_weight,
    )


def solution(mesh):
    return jax.shard_map(
        local,
        mesh=mesh,
        in_specs=(
            P("dp", "head"),
            P("dp", None, "head"),
            P("dp"),
            P("dp"),
            P("dp", None, None, "head"),
            P("dp", None, None, "head"),
            P("dp"),
            P("dp", "head"),
            P("dp", None, "head"),
            P("dp", None),
            P("head", None),
        ),
        out_specs=(P("dp", "head"), P("dp", "head")),
        check_vma=False,
    )
```

```python
import math

import jax
import jax.numpy as jnp
from jax import lax
from jax.experimental import pallas as pl
from jax.experimental.pallas import tpu as pltpu
from jax.sharding import PartitionSpec as P

MESH = pl.DeviceIdType.MESH
HD = 128
SAMPLES = 16
GROUP = 8
FLOOR = -1e30
SCALE = 1.0 / math.sqrt(HD)
PX = 384
MSG = 1024 + 128
KVROWS = 2 * PX + 16
CH = 128
NCH = 10
SHARD = CH * NCH
QT = 32
NQ = 8
EX = 2
FAR = SHARD - EX * CH
WR = 32
F32 = jnp.float32
BF16 = jnp.bfloat16


def dot(a, b):
    return jnp.dot(a, b, preferred_element_type=F32)


def dot_t(a, b):
    return lax.dot_general(a, b, (((1,), (1,)), ((), ())), preferred_element_type=F32)


def stack_heads(rows):
    return jnp.concatenate([rows[:, HD * h : HD * (h + 1)] for h in range(GROUP)], axis=0)


def unstack_heads(rows):
    return jnp.concatenate([rows[SAMPLES * h : SAMPLES * (h + 1)] for h in range(GROUP)], axis=1)


def kernel(
    so_hbm, sl_hbm, pfl_hbm, dq_hbm, nkv_hbm, pkv_hbm, seg_hbm, pq_hbm, skv_hbm, pre_hbm, w_hbm,
    dout_ref, pout_ref,
    so_ref, sl_ref, pfl_ref, wv, dq_ref, nkv_ref, pkv_ref, seg_ref, pq, skv, pall, qall, rsend, rrecv, zsend, zrecv,
    attn, dattn, own, down, bias, qsel, osel, suf_o, suf_m, suf_l,
    wx_far, wx_near, far_attn, outP, inP, outS, inS, outQ, inQ, down_out, down_in, far_dattn, head_out, head_in,
    half_sem, lsem, xs, xr, ys, yr, y2s, y2r, ms, mr,
    shs, shr, gfs, gfr, gss, gsr, gcs, gcr,
    outPs, inPr, outSs, inSr, outAs, inAr, outQs, inQr, downs, downr,
):
    wx = (wx_far, wx_near)
    d = lax.axis_index("dp")
    k = lax.axis_index("head")
    c = lax.rem(d, 2)
    x = lax.rem(d // 2, 4)
    zh = lax.rem(d // 8, 2)
    y = d // 16
    a = d // 8

    def dev(y_, zh_, x_, c_):
        return (((y_ * 2 + zh_) * 4 + x_) * 2 + c_, k)

    sibling = dev(y, zh, x, 1 - c)
    partner = dev(y, 1 - zh, x, c)
    xpeer = [dev(y, zh, lax.rem(x + i, 4), c) for i in (1, 2, 3)]
    ypeer = [dev(lax.rem(y + i, 4), zh, x, c) for i in (1, 2, 3)]

    bar = pltpu.get_barrier_semaphore()
    for peer in [sibling] + xpeer + ypeer:
        pl.semaphore_signal(bar, inc=1, device_id=peer, device_id_type=MESH)

    @pl.when(zh == 0)
    def _():
        pl.semaphore_signal(bar, inc=1, device_id=partner, device_id_type=MESH)


    for i in (1, 2, 3):
        pl.semaphore_signal(bar, inc=1, device_id=(d, lax.rem(k + i, 4)), device_id_type=MESH)

    loads = [
        pltpu.make_async_copy(pq_hbm, pq, lsem.at[0]),
        pltpu.make_async_copy(pre_hbm.at[0, 0], pall.at[c, x, pl.ds(0, PX)], lsem.at[1]),
        pltpu.make_async_copy(pre_hbm.at[0, 1], pall.at[c, x, pl.ds(PX, PX)], lsem.at[2]),
        pltpu.make_async_copy(skv_hbm, skv, lsem.at[3]),
    ]
    side = k // 2
    near = 1 + side
    far = 2 - side
    role_dest = [jnp.where(side == 0, 3, 0), 3 * side, far, near]

    def slab(dest):
        return pl.ds(pl.multiple_of(dest * SHARD, SHARD), SHARD)

    slabs = [
        pltpu.make_async_copy(w_hbm.at[:, slab(role_dest[i])], wv.at[i], lsem.at[4 + i]) for i in range(4)
    ]
    small = [
        pltpu.make_async_copy(dq_hbm, dq_ref, lsem.at[8]),
        pltpu.make_async_copy(pkv_hbm, pkv_ref, lsem.at[9]),
        pltpu.make_async_copy(seg_hbm, seg_ref, lsem.at[10]),
        pltpu.make_async_copy(nkv_hbm, nkv_ref, lsem.at[11]),
        pltpu.make_async_copy(so_hbm, so_ref, lsem.at[12]),
        pltpu.make_async_copy(pfl_hbm, pfl_ref, lsem.at[13]),
        pltpu.make_async_copy(sl_hbm, sl_ref, lsem.at[14]),
    ]
    for load in small + [loads[0], loads[1], loads[2], slabs[0], loads[3]] + slabs[1:]:
        load.start()

    pl.semaphore_wait(bar, 10 + zh)

    @pl.when(zh == 1)
    def _():
        pl.semaphore_signal(half_sem, inc=1, device_id=partner, device_id_type=MESH)


    def remote(src, dst, ss, rs, target):
        return pltpu.make_async_remote_copy(
            src_ref=src, dst_ref=dst, send_sem=ss, recv_sem=rs, device_id=target, device_id_type=MESH
        )

    edge = (k == 0) | (k == 3)
    mid = (k == 1) | (k == 2)
    mid_same = (d, 1 + side)
    mid_other = (d, 2 - side)
    edge_same = (d, 3 * side)

    def chunk(j):
        return pl.ds(pl.multiple_of(j * CH, CH), CH)

    def rows_of(q):
        return pl.ds(pl.multiple_of(q * QT, QT), QT)

    fast = jnp.where(c == 0, x, y)
    slow = jnp.where(c == 0, y, x)
    share = c * 16 + slow * 4 + fast

    def share_copy(w):
        rows = pl.ds(pl.multiple_of(share * WR, WR), WR)
        if w == 0:
            cols = pl.ds(pl.multiple_of(far * SHARD + EX * CH, CH), FAR)
        else:
            cols = slab(near)
        return remote(w_hbm.at[rows, cols], wx[w].at[c, slow, fast], shs.at[w], shr.at[w], mid_same)

    def line_peer(i, fast_axis):
        along_x = (c == 0) if fast_axis else (c == 1)
        return (jnp.where(along_x, xpeer[i][0], ypeer[i][0]), k)

    z1 = remote(qall.at[y, zh], qall.at[y, zh], ms.at[0], mr.at[0], partner)

    @pl.when(edge)
    def _():
        share_copy(0).start()

    small[4].wait()
    small[5].wait()
    small[6].wait()
    lane = lax.broadcasted_iota(jnp.int32, (SAMPLES, 128), 1)
    row = lax.broadcasted_iota(jnp.int32, (SAMPLES, 128), 0)
    extra = jnp.zeros((SAMPLES, 128), jnp.int32)
    for r in range(SAMPLES):
        number = so_ref[r]
        part = jnp.where(lane == 0, number >> 4, jnp.where(lane == 1, number & 15, 0))
        extra = jnp.where(row == r, part, extra)
    small[0].wait()
    qall[y, zh, :, 0:1024] = dq_ref[...]
    qall[y, zh, :, 1024:MSG] = extra.astype(F32).astype(BF16)
    length = pfl_ref[0]
    pall[c, x, 2 * PX : KVROWS, :] = (
        jnp.where(row == 0, length >> 4, jnp.where(row == 1, length & 15, 0)).astype(F32).astype(BF16)
    )


    @pl.when(zh == 1)
    def _():
        z1.start()

    loads[1].wait()
    loads[2].wait()
    px = [
        remote(pall.at[c, x], pall.at[c, x], xs.at[0], xr.at[0], xpeer[i]) for i in range(3)
    ]

    @pl.when(edge | (c == 1))
    def _():
        for copy in px:
            copy.start()


    small[1].wait()
    small[2].wait()
    small[3].wait()
    qpos = lax.broadcasted_iota(jnp.int32, (256, 256), 0)
    kpos = lax.broadcasted_iota(jnp.int32, (256, 256), 1)
    seg_row = jnp.broadcast_to(seg_ref[...].astype(F32), (256, 256))
    seg_col = jnp.sum(jnp.where(qpos == kpos, seg_row, 0.0), axis=1, keepdims=True)
    bias[...] = jnp.where((kpos <= qpos) & (seg_row == seg_col), 0.0, FLOOR)
    keys = pkv_ref[:, 0, :]
    values = pkv_ref[:, 1, :]
    loads[0].wait()

    def one_head(h, _):
        cols = pl.ds(pl.multiple_of(h * HD, HD), HD)
        s = dot_t(pq[:, cols], keys) * SCALE + bias[...]
        top = jnp.max(s, axis=1, keepdims=True)
        w = jnp.exp(s - top)
        total = jnp.sum(w, axis=1, keepdims=True)
        attn[:, cols] = (dot(w.astype(BF16), values) / total).astype(BF16)
        return 0

    lax.fori_loop(0, GROUP, one_head, 0, unroll=True)

    def gather_fast(w):
        return [
            remote(wx[w].at[c, slow, fast], wx[w].at[c, slow, fast], gfs.at[w], gfr.at[w], line_peer(i, True))
            for i in range(3)
        ]

    def gather_slow(w):
        return [
            remote(wx[w].at[c, slow], wx[w].at[c, slow], gss.at[w], gsr.at[w], line_peer(i, False))
            for i in range(3)
        ]

    def gather_core(w):
        return [remote(wx[w].at[c], wx[w].at[c], gcs.at[w], gcr.at[w], sibling)]

    def fast_all(w):
        three = wx[w].at[c, slow, pl.ds(0, 3)]
        return remote(three, three, gfs.at[w], gfr.at[w], line_peer(0, True))

    def slow_all(w):
        three = wx[w].at[c, pl.ds(0, 3)]
        return remote(three, three, gss.at[w], gsr.at[w], line_peer(0, False))

    def px_all():
        three = pall.at[c, pl.ds(0, 3)]
        return remote(three, three, xs.at[0], xr.at[0], xpeer[0])

    def y1_all():
        three = qall.at[pl.ds(0, 3)]
        return remote(three, three, ys.at[0], yr.at[0], ypeer[0])

    def y2_all():
        return remote(rsend.at[pl.ds(0, 3)], rrecv, y2s.at[0], y2r.at[0], ypeer[0])

    def start(copies):
        for copy in copies:
            copy.start()

    def wait(copies):
        for copy in copies:
            copy.wait()

    def edge_copy(j):
        return remote(outP.at[j], inP.at[j], outPs.at[0], inPr.at[j], mid_same)

    def rows_copy(q):
        return remote(attn.at[rows_of(q)], far_attn.at[rows_of(q)], outAs.at[0], inAr.at[q], mid_same)

    def mid_copy(j):
        return remote(outP.at[j], inS.at[j], outPs.at[0], inSr.at[j // 2], mid_other)

    def back_copy(j):
        return remote(outS.at[j], inS.at[j], outSs.at[0], inSr.at[j // 2], edge_same)

    def cross_copy(q):
        return remote(outQ.at[q], inQ.at[q], outQs.at[0], inQr.at[q], mid_other)

    def own_part(i):
        slabs[i].wait()
        own[i] = dot(attn[...], wv[i])

    def own_head():
        slabs[0].wait()
        own[0, :, 0 : 2 * CH] = dot(attn[...], wv[0, :, 0 : 2 * CH])

    def own_rest():
        own[0, :, 2 * CH : SHARD] = dot(attn[...], wv[0, :, 2 * CH : SHARD])

    def own_first(j):
        return own[0, :, chunk(j)] if j < NCH else own[2, :, chunk(j - NCH)]

    def first(j):
        @pl.when(mid)
        def _():
            edge_copy(j).wait_recv()
            outP[j] = (own_first(j) + inP[j].astype(F32)).astype(BF16)
            mid_copy(j).start()

        @pl.when(edge)
        def _():
            outP[j] = own_first(j).astype(BF16)
            edge_copy(j).start()

    def pair_in(j):
        two = pl.ds(2 * j, min(2, NCH + EX - 2 * j))
        return remote(outP.at[two], inS.at[two], outPs.at[0], inSr.at[j], mid_other)

    def seconds(j):
        @pl.when(mid)
        def _():
            pair_in(j).wait_recv()
            for i in (2 * j, 2 * j + 1):
                outS[i] = (own[1, :, chunk(i)] + inS[i].astype(F32)).astype(BF16)
                back_copy(i).start()

    def quarter(q):
        @pl.when(mid)
        def _():
            rows_copy(q).wait_recv()
            part = dot(far_attn[rows_of(q), :], wx_far[...].reshape(1024, FAR))
            outQ[q] = (own[2, rows_of(q), EX * CH : SHARD] + part).astype(BF16)
            cross_copy(q).start()

    def far_part():
        own[3] += dot(far_attn[...], wx_near[...].reshape(1024, SHARD))

    far_cols = pl.ds(EX * CH, FAR)

    def quarter_home(q):
        return pltpu.make_async_copy(
            pout_ref.at[rows_of(q), far_cols], pout_hbm.at[rows_of(q), far_cols], osem.at[q]
        )

    def first_home():
        cols = pl.ds(0, EX * CH)
        return pltpu.make_async_copy(pout_ref.at[:, cols], pout_hbm.at[:, cols], osem.at[NQ])

    def all_home():
        return pltpu.make_async_copy(pout_ref, pout_hbm, osem.at[NQ + 1])

    def decode_home():
        return pltpu.make_async_copy(dout_ref, dout_hbm, osem.at[NQ + 2])

    def mid_final(q):
        @pl.when(mid)
        def _():
            cross_copy(q).wait_recv()
            cols = slice(EX * CH, SHARD)
            pout_ref[rows_of(q), cols] = (own[3, rows_of(q), cols] + inQ[q].astype(F32)).astype(BF16)

    def mid_final_first(j):
        pair_in(j).wait_recv()
        for i in range(2 * j, min(2 * j + 2, NCH + EX)):
            cols = chunk(i - NCH)
            pout_ref[:, cols] = (own[3, :, cols] + inS[i].astype(F32)).astype(BF16)

    def edge_final(j):
        pair_in(j).wait_recv()
        for i in (2 * j, 2 * j + 1):
            pout_ref[:, chunk(i)] = (own[1, :, chunk(i)] + inS[i].astype(F32)).astype(BF16)

    def row_copy(i, slot, target):
        return remote(down_out.at[i], down_in.at[slot], downs.at[i], downr.at[slot], target)

    def row_from_edge():
        return row_copy(0, 0, mid_same)

    def row_to_edge():
        return row_copy(1, 3, edge_same)

    def row_across(i):
        return row_copy(i, 4, (d, role_dest[i]))

    def dattn_copy():
        return remote(dattn, far_dattn, downs.at[3], downr.at[1], mid_same)

    def head_copy():
        return remote(head_out, head_in, downs.at[4], downr.at[2], mid_same)

    def decode_out_edge():
        down_out[0] = dot(dattn[...], wv[0]).astype(BF16)
        row_from_edge().start()
        dattn_copy().start()
        head_out[...] = dot(dattn[...], wv[2, :, 0 : EX * CH]).astype(BF16)
        head_copy().start()
        down[1] = dot(dattn[...], wv[1])

    def decode_own(i):
        @pl.when(mid)
        def _():
            down[i] = dot(dattn[...], wv[i])

    def decode_to_edge():
        down_out[1] = dot(dattn[...], wv[1]).astype(BF16)
        row_to_edge().start()

    def decode_across():
        row_from_edge().wait_recv()
        down_out[0] = (down[0] + down_in[0].astype(F32)).astype(BF16)
        row_across(0).start()
        dattn_copy().wait_recv()
        down[2, :, EX * CH : SHARD] += dot(far_dattn[...], wx_far[...].reshape(1024, FAR))
        head_copy().wait_recv()
        down[2, :, 0 : EX * CH] += head_in[...].astype(F32)
        down_out[2] = down[2].astype(BF16)
        row_across(2).start()

    def decode_near():
        down[3] += dot(far_dattn[...], wx_near[...].reshape(1024, SHARD))

    def decode_final():
        @pl.when(mid)
        def _():
            row_across(2).wait_recv()
            dout_ref[...] = (down[3] + down_in[4].astype(F32)).astype(BF16)

        @pl.when(edge)
        def _():
            row_to_edge().wait_recv()
            row_across(0).wait_recv()
            dout_ref[...] = (down[1] + down_in[3].astype(F32) + down_in[4].astype(F32)).astype(BF16)

    rmod = lax.rem(lax.broadcasted_iota(jnp.int32, (128, 128), 0), SAMPLES)
    lane128 = lax.broadcasted_iota(jnp.int32, (128, 128), 1)

    def suffix():
        loads[3].wait()
        qs = stack_heads(dq_ref[...])
        scores = jnp.zeros((128, 128), F32)
        lens = jnp.zeros((128, 128), jnp.int32)
        for r in range(SAMPLES):
            scores = jnp.where(rmod == r, dot_t(qs, skv[r, 0]), scores)
            lens = jnp.where(rmod == r, sl_ref[r], lens)
        live = lane128 < lens
        scores = jnp.where(live, scores * SCALE, FLOOR)
        new_k = jnp.concatenate([nkv_ref[:, 0, :].astype(F32)] * GROUP, axis=0)
        new_v = jnp.concatenate([nkv_ref[:, 1, :].astype(F32)] * GROUP, axis=0)
        new_score = jnp.sum(qs.astype(F32) * new_k, axis=1, keepdims=True) * SCALE
        top = jnp.maximum(jnp.max(scores, axis=1, keepdims=True), new_score)
        w = jnp.where(live, jnp.exp(scores - top), 0.0)
        new_w = jnp.exp(new_score - top)
        acc = new_w.astype(BF16).astype(F32) * new_v
        for r in range(SAMPLES):
            acc = acc + dot(jnp.where(rmod == r, w, 0.0).astype(BF16), skv[r, 1])
        suf_o[...] = acc
        suf_m[...] = jnp.broadcast_to(top, (128, 128))
        suf_l[...] = jnp.broadcast_to(jnp.sum(w, axis=1, keepdims=True) + new_w, (128, 128))

    y1 = [remote(qall.at[y], qall.at[y], ys.at[0], yr.at[0], ypeer[i]) for i in range(3)]
    core = remote(pall.at[c], pall.at[c], ms.at[1], mr.at[1], sibling)
    y2 = [
        remote(rsend.at[lax.rem(y + i + 1, 4)], rrecv.at[i], y2s.at[0], y2r.at[0], ypeer[i])
        for i in range(3)
    ]
    z2 = remote(zsend, zrecv, ms.at[2], mr.at[2], partner)

    def to_slots():
        tags = qall[:, :, :, 1024:MSG].reshape(128, 128).astype(F32)
        number = tags[:, 0:1] * 16.0 + tags[:, 1:2] - (a * 128).astype(F32)
        return jnp.where(number == lane128.astype(F32), 1.0, 0.0)

    def prefix_begin():
        rows = qall[:, :, :, 0:1024].reshape(128, 1024)
        qsel[...] = dot(to_slots().T.astype(BF16), rows).astype(BF16)

    def prefix_part(lo, hi):
        head128 = lax.broadcasted_iota(jnp.int32, (128, 128), 0) // SAMPLES

        def one_prompt(j, _):
            slot = pl.ds(pl.multiple_of(j * SAMPLES, SAMPLES), SAMPLES)
            jc, jx = lax.rem(j, 2), j // 2
            q = stack_heads(qsel[slot, :])
            k_ = pall[jc, jx, 0:PX, :]
            v_ = pall[jc, jx, PX : 2 * PX, :]
            tail = pall[jc, jx, 2 * PX : KVROWS, :].astype(F32)
            n = tail[0:1, :] * 16.0 + tail[1:2, :]
            n = jnp.concatenate([n] * 3, axis=1)
            pos = lax.broadcasted_iota(jnp.int32, (1, PX), 1).astype(F32)
            s = dot_t(q, k_) * SCALE + jnp.where(pos < n, 0.0, FLOOR)
            top = jnp.max(s, axis=1, keepdims=True)
            w = jnp.exp(s - top)
            total = jnp.sum(w, axis=1, keepdims=True)
            o = dot(w.astype(BF16), v_) / total
            osel[slot, 0:1024] = unstack_heads(o).astype(BF16)
            stat = jnp.where(lane128 == head128, top, jnp.where(lane128 == head128 + GROUP, total, 0.0))
            stat = sum(stat[SAMPLES * h : SAMPLES * (h + 1)] for h in range(GROUP))
            hi_ = stat.astype(BF16).astype(F32)
            mid_ = (stat - hi_).astype(BF16).astype(F32)
            lo_ = (stat - hi_ - mid_).astype(BF16).astype(F32)
            packed = hi_ + pltpu.roll(mid_, 16, 1) + pltpu.roll(lo_, 32, 1)
            osel[slot, 1024:MSG] = packed.astype(BF16)
            return 0

        lax.fori_loop(lo, hi, one_prompt, 0, unroll=True)

    def prefix_end():
        back = dot(to_slots().astype(BF16), osel[...]).astype(BF16)
        rsend[...] = back.reshape(4, 2, SAMPLES, MSG)

    def merge():
        got = (
            rsend[y, zh].astype(F32)
            + rrecv[0, zh].astype(F32)
            + rrecv[1, zh].astype(F32)
            + rrecv[2, zh].astype(F32)
            + zrecv[...].astype(F32)
        )
        tag = got[:, 1024:MSG]
        stat = tag + pltpu.roll(tag, 128 - 16, 1) + pltpu.roll(tag, 128 - 32, 1)
        pre_m = jnp.concatenate([stat[:, h : h + 1] for h in range(GROUP)], axis=0)
        pre_l = jnp.concatenate([stat[:, GROUP + h : GROUP + h + 1] for h in range(GROUP)], axis=0)
        pre_o = stack_heads(got[:, 0:1024])
        m = suf_m[...]
        top = jnp.maximum(m, pre_m)
        pre_f = jnp.exp(pre_m - top) * pre_l
        suf_f = jnp.exp(m - top)
        out = (pre_o * pre_f + suf_o[...] * suf_f) / (pre_f + suf_l[...] * suf_f)
        dattn[...] = unstack_heads(out).astype(BF16)

    def sum_for_partner():
        zsend[...] = (
            rsend[y, 1 - zh].astype(F32)
            + rrecv[0, 1 - zh].astype(F32)
            + rrecv[1, 1 - zh].astype(F32)
            + rrecv[2, 1 - zh].astype(F32)
        ).astype(BF16)

    def on_mid(f, *args):
        @pl.when(mid)
        def _():
            f(*args)

    def own_mid():
        own[2] = dot(attn[...], wv[2])
        own[3] = dot(attn[...], wv[3])

    def on_edge(f, *args):
        @pl.when(edge)
        def _():
            f(*args)

    def share_arrived(w):
        share_copy(w).wait_recv()
        start(gather_fast(w))

    def fast_done(w):
        fast_all(w).wait()
        start(gather_slow(w))

    def slow_done(w):
        slow_all(w).wait()
        start(gather_core(w))

    def firsts(j):
        for i in (2 * j, 2 * j + 1):
            if i < NCH + EX:
                first(i)

    def on_mid_core(i, f, *args):
        @pl.when(mid & (c == i))
        def _():
            f(*args)

    def own_far():
        own[2] = dot(attn[...], wv[2])

    def own_near():
        own[3] = dot(attn[...], wv[3])

    def rows_out(lo, hi):
        for q in range(lo, hi):
            rows_copy(q).start()

    def sent_early():
        remote(outP, inP, outPs.at[0], inPr.at[0], mid_same).wait_send()
        remote(outS, outS, outSs.at[0], inPr.at[0], mid_same).wait_send()

    def edge_finals():
        for j in range(NCH // 2):
            edge_final(j)

    def mid_first_finals():
        for j in range(NCH // 2, (NCH + EX + 1) // 2):
            mid_final_first(j)

    def queries_out():
        @pl.when(zh == 0)
        def _():
            pl.semaphore_wait(half_sem, 1)
            z1.start()

    own_head()
    on_edge(firsts, 0)
    on_edge(lambda: share_copy(1).start())
    own_rest()
    on_mid(share_arrived, 0)
    on_mid_core(0, start, px)
    own_part(1)
    queries_out()
    on_edge(firsts, 1)
    on_edge(firsts, 2)
    on_edge(firsts, 3)
    suffix()
    slabs[2].wait()
    slabs[3].wait()
    on_mid(firsts, 0)
    own_far()
    z1.wait()
    start(y1)
    on_edge(firsts, 4)
    on_mid(share_arrived, 1)
    on_mid_core(0, fast_done, 0)
    on_edge(firsts, 5)
    on_mid(own_near)
    on_mid(firsts, 1)
    px_all().wait()
    core.start()
    on_mid_core(1, fast_done, 0)
    y1_all().wait()
    prefix_begin()
    on_mid(firsts, 2)
    seconds(0)
    core.wait()
    prefix_part(0, 4)
    on_mid(firsts, 3)
    prefix_part(4, 8)
    prefix_end()
    start(y2)
    on_edge(rows_out, 0, 2)
    on_mid(firsts, 4)
    seconds(1)
    on_mid_core(0, slow_done, 0)
    on_mid_core(0, fast_done, 1)
    seconds(2)
    on_mid_core(1, slow_done, 0)
    on_mid_core(1, fast_done, 1)
    on_mid(firsts, 5)
    y2_all().wait()
    sum_for_partner()
    z2.start()
    on_edge(rows_out, 2, 6)
    seconds(3)
    on_mid(lambda: wait(gather_core(0)))
    quarter(0)
    quarter(1)
    seconds(4)
    quarter(2)
    quarter(3)
    quarter(4)
    on_mid_core(0, slow_done, 1)
    on_mid_core(1, slow_done, 1)
    z2.wait()
    merge()
    on_edge(decode_out_edge)
    on_edge(rows_out, 6, 8)
    decode_own(0)
    quarter(5)
    decode_own(2)
    on_mid(decode_to_edge)
    decode_own(3)
    on_mid(decode_across)
    quarter(6)
    on_mid(sent_early)
    quarter(7)
    on_edge(edge_finals)
    on_mid(lambda: wait(gather_core(1)))
    on_mid(far_part)
    on_mid(decode_near)
    on_mid(mid_first_finals)
    for q in range(NQ - 1):
        mid_final(q)
    decode_final()
    mid_final(NQ - 1)

    @pl.when(edge)
    def _():
        share_copy(0).wait_send()
        share_copy(1).wait_send()
        remote(outP, inP, outPs.at[0], inPr.at[0], mid_same).wait_send()
        remote(attn, far_attn, outAs.at[0], inAr.at[0], mid_same).wait_send()
        row_from_edge().wait_send()
        dattn_copy().wait_send()
        head_copy().wait_send()

    @pl.when(mid)
    def _():
        remote(outQ, inQ, outQs.at[0], inQr.at[0], mid_other).wait_send()
        row_to_edge().wait_send()
        row_across(0).wait_send()
        row_across(2).wait_send()


def local(
    decode_query, new_kv, sample_order, suffix_len, suffix_kv, prefix_kv, prefix_len,
    prefill_query, prefill_kv, prefill_segment, out_weight,
):
    vmem = pl.BlockSpec(memory_space=pltpu.VMEM)
    hbm = pl.BlockSpec(memory_space=pl.ANY)
    dma = pltpu.SemaphoreType.DMA

    def ring(*lead):
        return pltpu.VMEM(lead + (256, CH), BF16)

    def dring(*lead):
        return pltpu.VMEM(lead + (SAMPLES, SHARD), BF16)

    return pl.pallas_call(
        kernel,
        out_shape=(pltpu.VMEM((SAMPLES, SHARD), BF16), pltpu.VMEM((256, SHARD), BF16)),
        in_specs=[hbm] * 11,
        out_specs=(vmem, vmem),
        scratch_shapes=[
            pltpu.SMEM(sample_order.shape, jnp.int32),
            pltpu.SMEM(suffix_len.shape, jnp.int32),
            pltpu.SMEM(prefix_len.shape, jnp.int32),
            pltpu.VMEM((4, 1024, SHARD), BF16),
            pltpu.VMEM(decode_query.shape, BF16),
            pltpu.VMEM(new_kv.shape, BF16),
            pltpu.VMEM(prefill_kv.shape, BF16),
            pltpu.VMEM(prefill_segment.shape, jnp.int32),
            pltpu.VMEM((256, 1024), BF16),
            pltpu.VMEM((SAMPLES, 2, 128, 128), BF16),
            pltpu.VMEM((2, 4, KVROWS, HD), BF16),
            pltpu.VMEM((4, 2, SAMPLES, MSG), BF16),
            pltpu.VMEM((4, 2, SAMPLES, MSG), BF16),
            pltpu.VMEM((3, 2, SAMPLES, MSG), BF16),
            pltpu.VMEM((SAMPLES, MSG), BF16),
            pltpu.VMEM((SAMPLES, MSG), BF16),
            pltpu.VMEM((256, 1024), BF16),
            pltpu.VMEM((SAMPLES, 1024), BF16),
            pltpu.VMEM((4, 256, SHARD), F32),
            pltpu.VMEM((4, SAMPLES, SHARD), F32),
            pltpu.VMEM((256, 256), F32),
            pltpu.VMEM((128, 1024), BF16),
            pltpu.VMEM((128, MSG), BF16),
            pltpu.VMEM((128, 128), F32),
            pltpu.VMEM((128, 128), F32),
            pltpu.VMEM((128, 128), F32),
            pltpu.VMEM((2, 4, 4, WR, FAR), BF16),
            pltpu.VMEM((2, 4, 4, WR, SHARD), BF16),
            pltpu.VMEM((256, 1024), BF16),
            ring(NCH + EX), ring(NCH + EX), ring(NCH), ring(NCH + EX),
            pltpu.VMEM((NQ, QT, FAR), BF16),
            pltpu.VMEM((NQ, QT, FAR), BF16),
            dring(3), dring(5),
            pltpu.VMEM((SAMPLES, 1024), BF16),
            pltpu.VMEM((SAMPLES, EX * CH), BF16),
            pltpu.VMEM((SAMPLES, EX * CH), BF16),
            pltpu.SemaphoreType.REGULAR,
            dma((15,)), dma((1,)), dma((1,)), dma((1,)), dma((1,)), dma((1,)), dma((1,)), dma((3,)), dma((3,)),
            dma((2,)), dma((2,)), dma((2,)), dma((2,)), dma((2,)), dma((2,)), dma((2,)), dma((2,)),
            dma((1,)), dma((NCH + EX,)), dma((1,)), dma(((NCH + EX + 1) // 2,)), dma((1,)), dma((NQ,)), dma((1,)), dma((NQ,)),
            dma((5,)), dma((5,)),
        ],
        compiler_params=pltpu.CompilerParams(
            collective_id=0, has_side_effects=True, vmem_limit_bytes=60 << 20
        ),
    )(
        sample_order, suffix_len, prefix_len, decode_query, new_kv, prefill_kv, prefill_segment,
        prefill_query, suffix_kv, prefix_kv, out_weight,
    )


def solution(mesh):
    return jax.shard_map(
        local,
        mesh=mesh,
        in_specs=(
            P("dp", "head"),
            P("dp", None, "head"),
            P("dp"),
            P("dp"),
            P("dp", None, None, "head"),
            P("dp", None, None, "head"),
            P("dp"),
            P("dp", "head"),
            P("dp", None, "head"),
            P("dp", None),
            P("head", None),
        ),
        out_specs=(P("dp", "head"), P("dp", "head")),
        check_vma=False,
    )
```

```python
import math

import jax
import jax.numpy as jnp
from jax import lax
from jax.experimental import pallas as pl
from jax.experimental.pallas import tpu as pltpu
from jax.sharding import PartitionSpec as P

MESH = pl.DeviceIdType.MESH
HD = 128
SAMPLES = 16
GROUP = 8
FLOOR = -1e30
SCALE = 1.0 / math.sqrt(HD)
PX = 384
MSG = 1024 + 128
KVROWS = 2 * PX + 16
CH = 128
NCH = 10
SHARD = CH * NCH
QT = 32
NQ = 8
EX = 2
FAR = SHARD - EX * CH
WR = 32
F32 = jnp.float32
BF16 = jnp.bfloat16


def dot(a, b):
    return jnp.dot(a, b, preferred_element_type=F32)


def dot_t(a, b):
    return lax.dot_general(a, b, (((1,), (1,)), ((), ())), preferred_element_type=F32)


def stack_heads(rows):
    return jnp.concatenate([rows[:, HD * h : HD * (h + 1)] for h in range(GROUP)], axis=0)


def unstack_heads(rows):
    return jnp.concatenate([rows[SAMPLES * h : SAMPLES * (h + 1)] for h in range(GROUP)], axis=1)


def kernel(
    so_hbm, sl_hbm, pfl_hbm, dq_hbm, nkv_hbm, pkv_hbm, seg_hbm, pq_hbm, skv_hbm, pre_hbm, w_hbm,
    dout_ref, pout_ref,
    so_ref, sl_ref, pfl_ref, wv, dq_ref, nkv_ref, pkv_ref, seg_ref, pq, skv, pall, qall, rsend, rrecv, zsend, zrecv,
    attn, dattn, own, down, bias, qsel, osel, suf_o, suf_m, suf_l,
    wx_far, wx_near, far_attn, outP, inP, outS, inS, outQ, inQ, down_out, down_in, far_dattn, head_out, head_in,
    half_sem, lsem, xs, xr, ys, yr, y2s, y2r, ms, mr,
    shs, shr, gfs, gfr, gss, gsr, gcs, gcr,
    outPs, inPr, outSs, inSr, outAs, inAr, outQs, inQr, downs, downr,
):
    wx = (wx_far, wx_near)
    d = lax.axis_index("dp")
    k = lax.axis_index("head")
    c = lax.rem(d, 2)
    x = lax.rem(d // 2, 4)
    zh = lax.rem(d // 8, 2)
    y = d // 16
    a = d // 8

    def dev(y_, zh_, x_, c_):
        return (((y_ * 2 + zh_) * 4 + x_) * 2 + c_, k)

    sibling = dev(y, zh, x, 1 - c)
    partner = dev(y, 1 - zh, x, c)
    xpeer = [dev(y, zh, lax.rem(x + i, 4), c) for i in (1, 2, 3)]
    ypeer = [dev(lax.rem(y + i, 4), zh, x, c) for i in (1, 2, 3)]

    bar = pltpu.get_barrier_semaphore()
    for peer in [sibling] + xpeer + ypeer:
        pl.semaphore_signal(bar, inc=1, device_id=peer, device_id_type=MESH)

    @pl.when(zh == 0)
    def _():
        pl.semaphore_signal(bar, inc=1, device_id=partner, device_id_type=MESH)


    for i in (1, 2, 3):
        pl.semaphore_signal(bar, inc=1, device_id=(d, lax.rem(k + i, 4)), device_id_type=MESH)

    loads = [
        pltpu.make_async_copy(pq_hbm, pq, lsem.at[0]),
        pltpu.make_async_copy(pre_hbm.at[0, 0], pall.at[c, x, pl.ds(0, PX)], lsem.at[1]),
        pltpu.make_async_copy(pre_hbm.at[0, 1], pall.at[c, x, pl.ds(PX, PX)], lsem.at[2]),
        pltpu.make_async_copy(skv_hbm, skv, lsem.at[3]),
    ]
    side = k // 2
    near = 1 + side
    far = 2 - side
    role_dest = [jnp.where(side == 0, 3, 0), 3 * side, far, near]

    def slab(dest):
        return pl.ds(pl.multiple_of(dest * SHARD, SHARD), SHARD)

    slabs = [
        pltpu.make_async_copy(w_hbm.at[:, slab(role_dest[i])], wv.at[i], lsem.at[4 + i]) for i in range(4)
    ]
    small = [
        pltpu.make_async_copy(dq_hbm, dq_ref, lsem.at[8]),
        pltpu.make_async_copy(pkv_hbm, pkv_ref, lsem.at[9]),
        pltpu.make_async_copy(seg_hbm, seg_ref, lsem.at[10]),
        pltpu.make_async_copy(nkv_hbm, nkv_ref, lsem.at[11]),
        pltpu.make_async_copy(so_hbm, so_ref, lsem.at[12]),
        pltpu.make_async_copy(pfl_hbm, pfl_ref, lsem.at[13]),
        pltpu.make_async_copy(sl_hbm, sl_ref, lsem.at[14]),
    ]
    for load in small + [loads[0], loads[1], loads[2], slabs[0], loads[3]] + slabs[1:]:
        load.start()

    pl.semaphore_wait(bar, 10 + zh)

    @pl.when(zh == 1)
    def _():
        pl.semaphore_signal(half_sem, inc=1, device_id=partner, device_id_type=MESH)


    def remote(src, dst, ss, rs, target):
        return pltpu.make_async_remote_copy(
            src_ref=src, dst_ref=dst, send_sem=ss, recv_sem=rs, device_id=target, device_id_type=MESH
        )

    edge = (k == 0) | (k == 3)
    mid = (k == 1) | (k == 2)
    mid_same = (d, 1 + side)
    mid_other = (d, 2 - side)
    edge_same = (d, 3 * side)

    def chunk(j):
        return pl.ds(pl.multiple_of(j * CH, CH), CH)

    def rows_of(q):
        return pl.ds(pl.multiple_of(q * QT, QT), QT)

    fast = jnp.where(c == 0, x, y)
    slow = jnp.where(c == 0, y, x)
    share = c * 16 + slow * 4 + fast

    def share_copy(w):
        rows = pl.ds(pl.multiple_of(share * WR, WR), WR)
        if w == 0:
            cols = pl.ds(pl.multiple_of(far * SHARD + EX * CH, CH), FAR)
        else:
            cols = slab(near)
        return remote(w_hbm.at[rows, cols], wx[w].at[c, slow, fast], shs.at[w], shr.at[w], mid_same)

    def line_peer(i, fast_axis):
        along_x = (c == 0) if fast_axis else (c == 1)
        return (jnp.where(along_x, xpeer[i][0], ypeer[i][0]), k)

    z1 = remote(qall.at[y, zh], qall.at[y, zh], ms.at[0], mr.at[0], partner)

    @pl.when(edge)
    def _():
        share_copy(0).start()

    small[4].wait()
    small[5].wait()
    small[6].wait()
    lane = lax.broadcasted_iota(jnp.int32, (SAMPLES, 128), 1)
    row = lax.broadcasted_iota(jnp.int32, (SAMPLES, 128), 0)
    extra = jnp.zeros((SAMPLES, 128), jnp.int32)
    for r in range(SAMPLES):
        number = so_ref[r]
        part = jnp.where(lane == 0, number >> 4, jnp.where(lane == 1, number & 15, 0))
        extra = jnp.where(row == r, part, extra)
    small[0].wait()
    qall[y, zh, :, 0:1024] = dq_ref[...]
    qall[y, zh, :, 1024:MSG] = extra.astype(F32).astype(BF16)
    length = pfl_ref[0]
    pall[c, x, 2 * PX : KVROWS, :] = (
        jnp.where(row == 0, length >> 4, jnp.where(row == 1, length & 15, 0)).astype(F32).astype(BF16)
    )


    @pl.when(zh == 1)
    def _():
        z1.start()

    loads[1].wait()
    loads[2].wait()
    px = [
        remote(pall.at[c, x], pall.at[c, x], xs.at[0], xr.at[0], xpeer[i]) for i in range(3)
    ]

    @pl.when(edge | (c == 1))
    def _():
        for copy in px:
            copy.start()


    small[1].wait()
    small[2].wait()
    small[3].wait()
    qpos = lax.broadcasted_iota(jnp.int32, (256, 256), 0)
    kpos = lax.broadcasted_iota(jnp.int32, (256, 256), 1)
    seg_row = jnp.broadcast_to(seg_ref[...].astype(F32), (256, 256))
    seg_col = jnp.sum(jnp.where(qpos == kpos, seg_row, 0.0), axis=1, keepdims=True)
    bias[...] = jnp.where((kpos <= qpos) & (seg_row == seg_col), 0.0, FLOOR)
    keys = pkv_ref[:, 0, :]
    values = pkv_ref[:, 1, :]
    loads[0].wait()

    def one_head(h, _):
        cols = pl.ds(pl.multiple_of(h * HD, HD), HD)
        s = dot_t(pq[:, cols], keys) * SCALE + bias[...]
        top = jnp.max(s, axis=1, keepdims=True)
        w = jnp.exp(s - top)
        total = jnp.sum(w, axis=1, keepdims=True)
        attn[:, cols] = (dot(w.astype(BF16), values) / total).astype(BF16)
        return 0

    lax.fori_loop(0, GROUP, one_head, 0, unroll=True)

    def gather_fast(w):
        return [
            remote(wx[w].at[c, slow, fast], wx[w].at[c, slow, fast], gfs.at[w], gfr.at[w], line_peer(i, True))
            for i in range(3)
        ]

    def gather_slow(w):
        return [
            remote(wx[w].at[c, slow], wx[w].at[c, slow], gss.at[w], gsr.at[w], line_peer(i, False))
            for i in range(3)
        ]

    def gather_core(w):
        return [remote(wx[w].at[c], wx[w].at[c], gcs.at[w], gcr.at[w], sibling)]

    def fast_all(w):
        three = wx[w].at[c, slow, pl.ds(0, 3)]
        return remote(three, three, gfs.at[w], gfr.at[w], line_peer(0, True))

    def slow_all(w):
        three = wx[w].at[c, pl.ds(0, 3)]
        return remote(three, three, gss.at[w], gsr.at[w], line_peer(0, False))

    def px_all():
        three = pall.at[c, pl.ds(0, 3)]
        return remote(three, three, xs.at[0], xr.at[0], xpeer[0])

    def y1_all():
        three = qall.at[pl.ds(0, 3)]
        return remote(three, three, ys.at[0], yr.at[0], ypeer[0])

    def y2_all():
        return remote(rsend.at[pl.ds(0, 3)], rrecv, y2s.at[0], y2r.at[0], ypeer[0])

    def start(copies):
        for copy in copies:
            copy.start()

    def wait(copies):
        for copy in copies:
            copy.wait()

    def edge_copy(j):
        return remote(outP.at[j], inP.at[j], outPs.at[0], inPr.at[j], mid_same)

    def rows_copy(q):
        return remote(attn.at[rows_of(q)], far_attn.at[rows_of(q)], outAs.at[0], inAr.at[q], mid_same)

    def mid_copy(j):
        return remote(outP.at[j], inS.at[j], outPs.at[0], inSr.at[j // 2], mid_other)

    def back_copy(j):
        return remote(outS.at[j], inS.at[j], outSs.at[0], inSr.at[j // 2], edge_same)

    def cross_copy(q):
        return remote(outQ.at[q], inQ.at[q], outQs.at[0], inQr.at[q], mid_other)

    def own_part(i):
        slabs[i].wait()
        own[i] = dot(attn[...], wv[i])

    def own_head():
        slabs[0].wait()
        own[0, :, 0 : 2 * CH] = dot(attn[...], wv[0, :, 0 : 2 * CH])

    def own_rest():
        own[0, :, 2 * CH : SHARD] = dot(attn[...], wv[0, :, 2 * CH : SHARD])

    def own_first(j):
        return own[0, :, chunk(j)] if j < NCH else own[2, :, chunk(j - NCH)]

    def first(j):
        @pl.when(mid)
        def _():
            edge_copy(j).wait_recv()
            outP[j] = (own_first(j) + inP[j].astype(F32)).astype(BF16)
            mid_copy(j).start()

        @pl.when(edge)
        def _():
            outP[j] = own_first(j).astype(BF16)
            edge_copy(j).start()

    def pair_in(j):
        two = pl.ds(2 * j, min(2, NCH + EX - 2 * j))
        return remote(outP.at[two], inS.at[two], outPs.at[0], inSr.at[j], mid_other)

    def seconds(j):
        @pl.when(mid)
        def _():
            pair_in(j).wait_recv()
            for i in (2 * j, 2 * j + 1):
                outS[i] = (own[1, :, chunk(i)] + inS[i].astype(F32)).astype(BF16)
                back_copy(i).start()

    def quarter(q):
        @pl.when(mid)
        def _():
            rows_copy(q).wait_recv()
            part = dot(far_attn[rows_of(q), :], wx_far[...].reshape(1024, FAR))
            outQ[q] = (own[2, rows_of(q), EX * CH : SHARD] + part).astype(BF16)
            cross_copy(q).start()

    def far_part():
        own[3] += dot(far_attn[...], wx_near[...].reshape(1024, SHARD))

    far_cols = pl.ds(EX * CH, FAR)

    def quarter_home(q):
        return pltpu.make_async_copy(
            pout_ref.at[rows_of(q), far_cols], pout_hbm.at[rows_of(q), far_cols], osem.at[q]
        )

    def first_home():
        cols = pl.ds(0, EX * CH)
        return pltpu.make_async_copy(pout_ref.at[:, cols], pout_hbm.at[:, cols], osem.at[NQ])

    def all_home():
        return pltpu.make_async_copy(pout_ref, pout_hbm, osem.at[NQ + 1])

    def decode_home():
        return pltpu.make_async_copy(dout_ref, dout_hbm, osem.at[NQ + 2])

    def mid_final(q):
        @pl.when(mid)
        def _():
            cross_copy(q).wait_recv()
            cols = slice(EX * CH, SHARD)
            pout_ref[rows_of(q), cols] = (own[3, rows_of(q), cols] + inQ[q].astype(F32)).astype(BF16)

    def mid_final_first(j):
        pair_in(j).wait_recv()
        for i in range(2 * j, min(2 * j + 2, NCH + EX)):
            cols = chunk(i - NCH)
            pout_ref[:, cols] = (own[3, :, cols] + inS[i].astype(F32)).astype(BF16)

    def edge_final(j):
        pair_in(j).wait_recv()
        for i in (2 * j, 2 * j + 1):
            pout_ref[:, chunk(i)] = (own[1, :, chunk(i)] + inS[i].astype(F32)).astype(BF16)

    def row_copy(i, slot, target):
        return remote(down_out.at[i], down_in.at[slot], downs.at[i], downr.at[slot], target)

    def row_from_edge():
        return row_copy(0, 0, mid_same)

    def row_to_edge():
        return row_copy(1, 3, edge_same)

    def row_across(i):
        return row_copy(i, 4, (d, role_dest[i]))

    def dattn_copy():
        return remote(dattn, far_dattn, downs.at[3], downr.at[1], mid_same)

    def head_copy():
        return remote(head_out, head_in, downs.at[4], downr.at[2], mid_same)

    def decode_out_edge():
        down_out[0] = dot(dattn[...], wv[0]).astype(BF16)
        row_from_edge().start()
        dattn_copy().start()
        head_out[...] = dot(dattn[...], wv[2, :, 0 : EX * CH]).astype(BF16)
        head_copy().start()
        down[1] = dot(dattn[...], wv[1])

    def decode_own(i):
        @pl.when(mid)
        def _():
            down[i] = dot(dattn[...], wv[i])

    def decode_to_edge():
        down_out[1] = dot(dattn[...], wv[1]).astype(BF16)
        row_to_edge().start()

    def decode_across():
        row_from_edge().wait_recv()
        down_out[0] = (down[0] + down_in[0].astype(F32)).astype(BF16)
        row_across(0).start()
        dattn_copy().wait_recv()
        down[2, :, EX * CH : SHARD] += dot(far_dattn[...], wx_far[...].reshape(1024, FAR))
        head_copy().wait_recv()
        down[2, :, 0 : EX * CH] += head_in[...].astype(F32)
        down_out[2] = down[2].astype(BF16)
        row_across(2).start()

    def decode_near():
        down[3] += dot(far_dattn[...], wx_near[...].reshape(1024, SHARD))

    def decode_final():
        @pl.when(mid)
        def _():
            row_across(2).wait_recv()
            dout_ref[...] = (down[3] + down_in[4].astype(F32)).astype(BF16)

        @pl.when(edge)
        def _():
            row_to_edge().wait_recv()
            row_across(0).wait_recv()
            dout_ref[...] = (down[1] + down_in[3].astype(F32) + down_in[4].astype(F32)).astype(BF16)

    rmod = lax.rem(lax.broadcasted_iota(jnp.int32, (128, 128), 0), SAMPLES)
    lane128 = lax.broadcasted_iota(jnp.int32, (128, 128), 1)

    def suffix():
        loads[3].wait()
        qs = stack_heads(dq_ref[...])
        scores = jnp.zeros((128, 128), F32)
        lens = jnp.zeros((128, 128), jnp.int32)
        for r in range(SAMPLES):
            scores = jnp.where(rmod == r, dot_t(qs, skv[r, 0]), scores)
            lens = jnp.where(rmod == r, sl_ref[r], lens)
        live = lane128 < lens
        scores = jnp.where(live, scores * SCALE, FLOOR)
        new_k = jnp.concatenate([nkv_ref[:, 0, :].astype(F32)] * GROUP, axis=0)
        new_v = jnp.concatenate([nkv_ref[:, 1, :].astype(F32)] * GROUP, axis=0)
        new_score = jnp.sum(qs.astype(F32) * new_k, axis=1, keepdims=True) * SCALE
        top = jnp.maximum(jnp.max(scores, axis=1, keepdims=True), new_score)
        w = jnp.where(live, jnp.exp(scores - top), 0.0)
        new_w = jnp.exp(new_score - top)
        acc = new_w.astype(BF16).astype(F32) * new_v
        for r in range(SAMPLES):
            acc = acc + dot(jnp.where(rmod == r, w, 0.0).astype(BF16), skv[r, 1])
        suf_o[...] = acc
        suf_m[...] = jnp.broadcast_to(top, (128, 128))
        suf_l[...] = jnp.broadcast_to(jnp.sum(w, axis=1, keepdims=True) + new_w, (128, 128))

    y1 = [remote(qall.at[y], qall.at[y], ys.at[0], yr.at[0], ypeer[i]) for i in range(3)]
    core = remote(pall.at[c], pall.at[c], ms.at[1], mr.at[1], sibling)
    y2 = [
        remote(rsend.at[lax.rem(y + i + 1, 4)], rrecv.at[i], y2s.at[0], y2r.at[0], ypeer[i])
        for i in range(3)
    ]
    z2 = remote(zsend, zrecv, ms.at[2], mr.at[2], partner)

    def to_slots():
        tags = qall[:, :, :, 1024:MSG].reshape(128, 128).astype(F32)
        number = tags[:, 0:1] * 16.0 + tags[:, 1:2] - (a * 128).astype(F32)
        return jnp.where(number == lane128.astype(F32), 1.0, 0.0)

    def prefix_begin():
        rows = qall[:, :, :, 0:1024].reshape(128, 1024)
        qsel[...] = dot(to_slots().T.astype(BF16), rows).astype(BF16)

    def prefix_part(lo, hi):
        head128 = lax.broadcasted_iota(jnp.int32, (128, 128), 0) // SAMPLES

        def one_prompt(j, _):
            slot = pl.ds(pl.multiple_of(j * SAMPLES, SAMPLES), SAMPLES)
            jc, jx = lax.rem(j, 2), j // 2
            q = stack_heads(qsel[slot, :])
            k_ = pall[jc, jx, 0:PX, :]
            v_ = pall[jc, jx, PX : 2 * PX, :]
            tail = pall[jc, jx, 2 * PX : KVROWS, :].astype(F32)
            n = tail[0:1, :] * 16.0 + tail[1:2, :]
            n = jnp.concatenate([n] * 3, axis=1)
            pos = lax.broadcasted_iota(jnp.int32, (1, PX), 1).astype(F32)
            s = dot_t(q, k_) * SCALE + jnp.where(pos < n, 0.0, FLOOR)
            top = jnp.max(s, axis=1, keepdims=True)
            w = jnp.exp(s - top)
            total = jnp.sum(w, axis=1, keepdims=True)
            o = dot(w.astype(BF16), v_) / total
            osel[slot, 0:1024] = unstack_heads(o).astype(BF16)
            stat = jnp.where(lane128 == head128, top, jnp.where(lane128 == head128 + GROUP, total, 0.0))
            stat = sum(stat[SAMPLES * h : SAMPLES * (h + 1)] for h in range(GROUP))
            hi_ = stat.astype(BF16).astype(F32)
            mid_ = (stat - hi_).astype(BF16).astype(F32)
            lo_ = (stat - hi_ - mid_).astype(BF16).astype(F32)
            packed = hi_ + pltpu.roll(mid_, 16, 1) + pltpu.roll(lo_, 32, 1)
            osel[slot, 1024:MSG] = packed.astype(BF16)
            return 0

        lax.fori_loop(lo, hi, one_prompt, 0, unroll=True)

    def prefix_end():
        back = dot(to_slots().astype(BF16), osel[...]).astype(BF16)
        rsend[...] = back.reshape(4, 2, SAMPLES, MSG)

    def merge():
        got = (
            rsend[y, zh].astype(F32)
            + rrecv[0, zh].astype(F32)
            + rrecv[1, zh].astype(F32)
            + rrecv[2, zh].astype(F32)
            + zrecv[...].astype(F32)
        )
        tag = got[:, 1024:MSG]
        stat = tag + pltpu.roll(tag, 128 - 16, 1) + pltpu.roll(tag, 128 - 32, 1)
        pre_m = jnp.concatenate([stat[:, h : h + 1] for h in range(GROUP)], axis=0)
        pre_l = jnp.concatenate([stat[:, GROUP + h : GROUP + h + 1] for h in range(GROUP)], axis=0)
        pre_o = stack_heads(got[:, 0:1024])
        m = suf_m[...]
        top = jnp.maximum(m, pre_m)
        pre_f = jnp.exp(pre_m - top) * pre_l
        suf_f = jnp.exp(m - top)
        out = (pre_o * pre_f + suf_o[...] * suf_f) / (pre_f + suf_l[...] * suf_f)
        dattn[...] = unstack_heads(out).astype(BF16)

    def sum_for_partner():
        zsend[...] = (
            rsend[y, 1 - zh].astype(F32)
            + rrecv[0, 1 - zh].astype(F32)
            + rrecv[1, 1 - zh].astype(F32)
            + rrecv[2, 1 - zh].astype(F32)
        ).astype(BF16)

    def on_mid(f, *args):
        @pl.when(mid)
        def _():
            f(*args)

    def own_mid():
        own[2] = dot(attn[...], wv[2])
        own[3] = dot(attn[...], wv[3])

    def on_edge(f, *args):
        @pl.when(edge)
        def _():
            f(*args)

    def share_arrived(w):
        share_copy(w).wait_recv()
        start(gather_fast(w))

    def fast_done(w):
        fast_all(w).wait()
        start(gather_slow(w))

    def slow_done(w):
        slow_all(w).wait()
        start(gather_core(w))

    def firsts(j):
        for i in (2 * j, 2 * j + 1):
            if i < NCH + EX:
                first(i)

    def on_mid_core(i, f, *args):
        @pl.when(mid & (c == i))
        def _():
            f(*args)

    def own_far():
        own[2] = dot(attn[...], wv[2])

    def own_near():
        own[3] = dot(attn[...], wv[3])

    def rows_out(lo, hi):
        for q in range(lo, hi):
            rows_copy(q).start()

    def sent_early():
        remote(outP, inP, outPs.at[0], inPr.at[0], mid_same).wait_send()
        remote(outS, outS, outSs.at[0], inPr.at[0], mid_same).wait_send()

    def edge_finals():
        for j in range(NCH // 2):
            edge_final(j)

    def mid_first_finals():
        for j in range(NCH // 2, (NCH + EX + 1) // 2):
            mid_final_first(j)

    def queries_out():
        @pl.when(zh == 0)
        def _():
            pl.semaphore_wait(half_sem, 1)
            z1.start()

    own_head()
    on_edge(firsts, 0)
    on_edge(lambda: share_copy(1).start())
    own_rest()
    on_mid(share_arrived, 0)
    on_mid_core(0, start, px)
    own_part(1)
    queries_out()
    on_edge(firsts, 1)
    on_edge(firsts, 2)
    on_edge(firsts, 3)
    suffix()
    slabs[2].wait()
    slabs[3].wait()
    on_mid(firsts, 0)
    own_far()
    z1.wait()
    start(y1)
    on_edge(firsts, 4)
    on_mid(share_arrived, 1)
    on_mid_core(0, fast_done, 0)
    on_edge(firsts, 5)
    on_mid(own_near)
    on_mid(firsts, 1)
    px_all().wait()
    core.start()
    on_mid_core(1, fast_done, 0)
    y1_all().wait()
    prefix_begin()
    on_mid(firsts, 2)
    seconds(0)
    core.wait()
    prefix_part(0, 4)
    on_mid(firsts, 3)
    prefix_part(4, 8)
    prefix_end()
    start(y2)
    on_edge(rows_out, 0, 2)
    on_mid(firsts, 4)
    seconds(1)
    on_mid_core(0, slow_done, 0)
    on_mid_core(0, fast_done, 1)
    seconds(2)
    on_mid_core(1, slow_done, 0)
    on_mid_core(1, fast_done, 1)
    on_mid(firsts, 5)
    y2_all().wait()
    sum_for_partner()
    z2.start()
    on_edge(rows_out, 2, 6)
    seconds(3)
    on_mid(lambda: wait(gather_core(0)))
    quarter(0)
    quarter(1)
    seconds(4)
    quarter(2)
    quarter(3)
    quarter(4)
    on_mid_core(0, slow_done, 1)
    on_mid_core(1, slow_done, 1)
    z2.wait()
    merge()
    on_edge(decode_out_edge)
    on_edge(rows_out, 6, 8)
    decode_own(0)
    quarter(5)
    decode_own(2)
    on_mid(decode_across)
    on_mid(decode_to_edge)
    quarter(6)
    decode_own(3)
    on_mid(sent_early)
    quarter(7)
    on_edge(edge_finals)
    on_mid(lambda: wait(gather_core(1)))
    on_mid(far_part)
    on_mid(decode_near)
    on_mid(mid_first_finals)
    for q in range(NQ - 1):
        mid_final(q)
    decode_final()
    mid_final(NQ - 1)

    @pl.when(edge)
    def _():
        share_copy(0).wait_send()
        share_copy(1).wait_send()
        remote(outP, inP, outPs.at[0], inPr.at[0], mid_same).wait_send()
        remote(attn, far_attn, outAs.at[0], inAr.at[0], mid_same).wait_send()
        row_from_edge().wait_send()
        dattn_copy().wait_send()
        head_copy().wait_send()

    @pl.when(mid)
    def _():
        remote(outQ, inQ, outQs.at[0], inQr.at[0], mid_other).wait_send()
        row_to_edge().wait_send()
        row_across(0).wait_send()
        row_across(2).wait_send()


def local(
    decode_query, new_kv, sample_order, suffix_len, suffix_kv, prefix_kv, prefix_len,
    prefill_query, prefill_kv, prefill_segment, out_weight,
):
    vmem = pl.BlockSpec(memory_space=pltpu.VMEM)
    hbm = pl.BlockSpec(memory_space=pl.ANY)
    dma = pltpu.SemaphoreType.DMA

    def ring(*lead):
        return pltpu.VMEM(lead + (256, CH), BF16)

    def dring(*lead):
        return pltpu.VMEM(lead + (SAMPLES, SHARD), BF16)

    return pl.pallas_call(
        kernel,
        out_shape=(pltpu.VMEM((SAMPLES, SHARD), BF16), pltpu.VMEM((256, SHARD), BF16)),
        in_specs=[hbm] * 11,
        out_specs=(vmem, vmem),
        scratch_shapes=[
            pltpu.SMEM(sample_order.shape, jnp.int32),
            pltpu.SMEM(suffix_len.shape, jnp.int32),
            pltpu.SMEM(prefix_len.shape, jnp.int32),
            pltpu.VMEM((4, 1024, SHARD), BF16),
            pltpu.VMEM(decode_query.shape, BF16),
            pltpu.VMEM(new_kv.shape, BF16),
            pltpu.VMEM(prefill_kv.shape, BF16),
            pltpu.VMEM(prefill_segment.shape, jnp.int32),
            pltpu.VMEM((256, 1024), BF16),
            pltpu.VMEM((SAMPLES, 2, 128, 128), BF16),
            pltpu.VMEM((2, 4, KVROWS, HD), BF16),
            pltpu.VMEM((4, 2, SAMPLES, MSG), BF16),
            pltpu.VMEM((4, 2, SAMPLES, MSG), BF16),
            pltpu.VMEM((3, 2, SAMPLES, MSG), BF16),
            pltpu.VMEM((SAMPLES, MSG), BF16),
            pltpu.VMEM((SAMPLES, MSG), BF16),
            pltpu.VMEM((256, 1024), BF16),
            pltpu.VMEM((SAMPLES, 1024), BF16),
            pltpu.VMEM((4, 256, SHARD), F32),
            pltpu.VMEM((4, SAMPLES, SHARD), F32),
            pltpu.VMEM((256, 256), F32),
            pltpu.VMEM((128, 1024), BF16),
            pltpu.VMEM((128, MSG), BF16),
            pltpu.VMEM((128, 128), F32),
            pltpu.VMEM((128, 128), F32),
            pltpu.VMEM((128, 128), F32),
            pltpu.VMEM((2, 4, 4, WR, FAR), BF16),
            pltpu.VMEM((2, 4, 4, WR, SHARD), BF16),
            pltpu.VMEM((256, 1024), BF16),
            ring(NCH + EX), ring(NCH + EX), ring(NCH), ring(NCH + EX),
            pltpu.VMEM((NQ, QT, FAR), BF16),
            pltpu.VMEM((NQ, QT, FAR), BF16),
            dring(3), dring(5),
            pltpu.VMEM((SAMPLES, 1024), BF16),
            pltpu.VMEM((SAMPLES, EX * CH), BF16),
            pltpu.VMEM((SAMPLES, EX * CH), BF16),
            pltpu.SemaphoreType.REGULAR,
            dma((15,)), dma((1,)), dma((1,)), dma((1,)), dma((1,)), dma((1,)), dma((1,)), dma((3,)), dma((3,)),
            dma((2,)), dma((2,)), dma((2,)), dma((2,)), dma((2,)), dma((2,)), dma((2,)), dma((2,)),
            dma((1,)), dma((NCH + EX,)), dma((1,)), dma(((NCH + EX + 1) // 2,)), dma((1,)), dma((NQ,)), dma((1,)), dma((NQ,)),
            dma((5,)), dma((5,)),
        ],
        compiler_params=pltpu.CompilerParams(
            collective_id=0, has_side_effects=True, vmem_limit_bytes=60 << 20
        ),
    )(
        sample_order, suffix_len, prefix_len, decode_query, new_kv, prefill_kv, prefill_segment,
        prefill_query, suffix_kv, prefix_kv, out_weight,
    )


def solution(mesh):
    return jax.shard_map(
        local,
        mesh=mesh,
        in_specs=(
            P("dp", "head"),
            P("dp", None, "head"),
            P("dp"),
            P("dp"),
            P("dp", None, None, "head"),
            P("dp", None, None, "head"),
            P("dp"),
            P("dp", "head"),
            P("dp", None, "head"),
            P("dp", None),
            P("head", None),
        ),
        out_specs=(P("dp", "head"), P("dp", "head")),
        check_vma=False,
    )
```
